32 devices in a mesh: dp: 4 (over x, core), fsdp: 8 (over z, y).
Axes of the slice: x: 2, y: 2, z: 4, core: 2. Of those that a mesh axis runs over, the one named last changes fastest.
Arguments:
- tokens: bfloat16 [32768, 512], P(('dp', 'fsdp')), may hold values from -6 to 6
- gating: bfloat16 [512, 3072], P(None, ('dp', 'fsdp')), may hold values from -0.25 to 0.25
- offsets: bfloat16 [3072], P(('dp', 'fsdp')), may hold values from -4 to 4
- prescale: bfloat16 [512], P(('dp', 'fsdp')), may hold values from 0.25 to 1.75
- readout: bfloat16 [1024, 512], P(('dp', 'fsdp')), may hold values from -0.1875 to 0.1875
- midscale: bfloat16 [512], P(('dp', 'fsdp')), may hold values from 0.25 to 1.75
- expand: bfloat16 [512, 2048], P(None, ('dp', 'fsdp')), may hold values from -0.25 to 0.25
- shifts: bfloat16 [2048], P(('dp', 'fsdp')), may hold values from -3 to 3
- contract: bfloat16 [2048, 512], P(('dp', 'fsdp')), may hold values from -0.125 to 0.125
- cotangent: bfloat16 [32768, 512], P(('dp', 'fsdp')), may hold values from -6 to 6
Outputs:
- block_output: bfloat16 [32768, 512], P(('dp', 'fsdp'))
- tokens_grad: float32 [32768, 512], P(('dp', 'fsdp'))
- gating_grad: float32 [512, 3072], P(None, ('dp', 'fsdp'))
- offsets_grad: float32 [3072], P(('dp', 'fsdp'))
- prescale_grad: float32 [512], P(('dp', 'fsdp'))
- readout_grad: float32 [1024, 512], P(('dp', 'fsdp'))
- midscale_grad: float32 [512], P(('dp', 'fsdp'))
- expand_grad: float32 [512, 2048], P(None, ('dp', 'fsdp'))
- shifts_grad: float32 [2048], P(('dp', 'fsdp'))
- contract_grad: float32 [2048, 512], P(('dp', 'fsdp'))
The draws below stay inside these ranges and needn't reach their ends.
All inputs are finite; a program needn't handle non-finite values.
Results may differ from the reference program's by a relative error of at most 0.0063.
Values may be sent and summed in bfloat16 or wider, within the bound.
No kernel may reach another device: no remote copies, remote signals or barrier semaphores. Data moves between devices by JAX's collectives and lax.ppermute only.
A program may use at most 192 MiB of HBM per device.

```python
import math
import jax
import jax.numpy as jnp
from jax import lax

D = 512
H = 1024
F = 2048
LEN = 1024
TOKENS = 32768


def shard_levels(stream_key, extent, cuts, low, top_value):
    factor_of, own = 1.0, jax.random.fold_in(stream_key, 6)
    for dim, blocks in cuts:
        heights = jnp.exp(jax.random.uniform(jax.random.fold_in(own, dim), (blocks,), jnp.float32, low / len(cuts), top_value / len(cuts)))
        factor_of = factor_of * jnp.repeat(heights, extent[dim] // blocks).reshape([-1 if axis == dim else 1 for axis in range(len(extent))])
    return factor_of


def bell_draw(own_key, extent, spread, bound, cuts=(), held_as=jnp.bfloat16):
    level = shard_levels(own_key, extent, cuts, -0.22, 0.18) if cuts else 1.0
    drawn = jax.random.normal(own_key, extent, jnp.float32) * spread * level
    return jnp.minimum(jnp.maximum(drawn, -bound), bound).astype(held_as)


def setup_inputs(seed: int = 0) -> dict:
    key_list = jax.random.split(jax.random.key(seed), 11)
    tokens = bell_draw(key_list[0], (TOKENS, D), 1.0, 6.0, ((0, 32),))
    gating = bell_draw(key_list[1], (D, 3 * H), D ** -0.5, 0.25, ((1, 32),))
    offsets = bell_draw(key_list[2], (3 * H,), 1.0, 4.0, ((0, 32),))
    prescale = jnp.clip(1.0 + 0.15 * jax.random.normal(key_list[3], (D,), jnp.float32), 0.25, 1.75).astype(jnp.bfloat16)
    readout = bell_draw(key_list[4], (H, D), H ** -0.5, 0.1875, ((0, 32),))
    midscale = jnp.clip(1.0 + 0.15 * jax.random.normal(key_list[5], (D,), jnp.float32), 0.25, 1.75).astype(jnp.bfloat16)
    expand = bell_draw(key_list[6], (D, F), D ** -0.5, 0.25, ((1, 32),))
    shifts = bell_draw(key_list[7], (F,), 0.5, 3.0, ((0, 32),))
    contract = bell_draw(key_list[8], (F, D), F ** -0.5, 0.125, ((0, 32),))
    cotangent = bell_draw(key_list[9], (TOKENS, D), 1.0, 6.0, ((0, 32),))
    return {"tokens": tokens, "gating": gating, "offsets": offsets, "prescale": prescale, "readout": readout, "midscale": midscale, "expand": expand, "shifts": shifts, "contract": contract, "cotangent": cotangent}


epsilon = 1e-06
highest = lax.Precision.HIGHEST

@jax.custom_vjp
def low(v):
    return lax.optimization_barrier(v.astype(jnp.bfloat16)).astype(jnp.float32)

@jax.custom_vjp
def low_back(v):
    return v

def low_keep(v):
    return (low(v), None)

def low_pass(kept, grad):
    return (grad,)

def back_keep(v):
    return (v, None)

def back_low(kept, grad):
    return (low(grad),)
low.defvjp(low_keep, low_pass)
low_back.defvjp(back_keep, back_low)

def rms_scale(values, gain):
    return values * lax.rsqrt(lax.optimization_barrier(jnp.mean(values * values, axis=-1, keepdims=True)) + epsilon) * gain

def combine(earlier, later):
    return (earlier[0] * later[0], later[0] * earlier[1] + later[1])

def product(left, right):
    return jnp.einsum('bld,dk->blk', left, right, precision=highest)

def forward(inputs, weights):
    gating, offsets, prescale, readout, midscale, expand, shifts, contract = weights
    normed = low(rms_scale(inputs, prescale))
    gate_pre = low_back(product(normed, gating) + offsets)
    forget_pre, input_pre, candidate = jnp.split(gate_pre, 3, axis=-1)
    forget_sig = jax.nn.sigmoid(forget_pre)
    input_sig = jax.nn.sigmoid(input_pre)
    retain = forget_sig / (forget_sig + input_sig)
    inflow = input_sig / (forget_sig + input_sig) * candidate
    _, states = lax.associative_scan(combine, (retain, inflow), axis=1)
    branch_one = low_back(product(low(states), readout))
    residual = inputs + branch_one
    normed_two = low(rms_scale(residual, midscale))
    expand_pre = low_back(product(normed_two, expand) + shifts)
    hidden = low(jax.nn.gelu(expand_pre, approximate=True))
    branch_two = low_back(product(hidden, contract))
    return residual + branch_two

def reference(tokens, gating, offsets, prescale, readout, midscale, expand, shifts, contract, cotangent):
    weights = tuple((weight.astype(jnp.float32) for weight in (gating, offsets, prescale, readout, midscale, expand, shifts, contract)))
    seq_count = tokens.shape[0] // LEN
    group_size = math.gcd(seq_count, max(1, 4096 // LEN))
    inputs = tokens.astype(jnp.float32).reshape(seq_count // group_size, group_size, LEN, D)
    upstream = cotangent.astype(jnp.float32).reshape(seq_count // group_size, group_size, LEN, D)
    starting = tuple((jnp.zeros_like(weight) for weight in weights))

    def accumulate(totals, sample):
        values, pull = jax.vjp(forward, sample[0], weights)
        inputs_grad, weight_grads = pull(sample[1])
        totals = tuple((total + part_grad for total, part_grad in zip(totals, weight_grads)))
        return (totals, (values.astype(jnp.bfloat16), inputs_grad))
    totals, (outputs, input_grads) = lax.scan(accumulate, starting, (inputs, upstream))
    return (outputs.reshape(-1, D), input_grads.reshape(-1, D), totals[0], totals[1], totals[2], totals[3], totals[4], totals[5], totals[6], totals[7])
```

```python
from functools import partial

import jax
import jax.numpy as jnp
import numpy as np
from jax import lax
from jax.experimental import pallas as pl
from jax.experimental.pallas import tpu as pltpu
from jax.sharding import PartitionSpec as P

LEN = 1024
LANES = 8
AXES = ("dp", "fsdp")
epsilon = 1e-06
bf16 = jnp.bfloat16
f32 = jnp.float32
VMEM_BYTES = 56 * 1024 * 1024


def matmul(left, right):
    return jnp.dot(left, right, preferred_element_type=f32)


def across(left, right):
    return lax.dot_general(left, right, (((0,), (0,)), ((), ())), preferred_element_type=f32)


def against(left, right):
    return lax.dot_general(left, right, (((1,), (1,)), ((), ())), preferred_element_type=f32)


def interleaved(values):
    runs = values.reshape(LANES, LEN // LANES, values.shape[-1])
    return runs.transpose(1, 0, 2).reshape(values.shape)


def sequential(values):
    steps = values.reshape(LEN // LANES, LANES, values.shape[-1])
    return steps.transpose(1, 0, 2).reshape(values.shape)


def fetch(pairs, sem):
    copies = [pltpu.make_async_copy(source, target, sem) for source, target in pairs]
    for copy in copies:
        copy.start()
    return copies


def down(values):
    return jnp.concatenate([jnp.zeros_like(values[:1]), values[:-1]], axis=0)


def up(values):
    return jnp.concatenate([values[1:], jnp.zeros_like(values[:1])], axis=0)


def gates_kernel(normed, offsets, w0, w1, w2, w3, retain, states, candidate, low, kept_f, kept_i, weights, pre, decay, drive, sem):
    group = pl.program_id(0)
    wide = retain.shape[1]
    nb = w0.shape[0]

    @pl.when(group == 0)
    def _():
        pairs = [
            (w.at[:, t], weights.at[t, pl.ds(k * nb, nb)]) for k, w in enumerate((w0, w1, w2, w3)) for t in range(3)
        ]
        for copy in fetch(pairs, sem):
            copy.wait()

    blocks = pl.ds(group * 2 * nb, 2 * nb)
    rows = 256
    for t in range(3):
        w = weights[t, blocks].reshape(wide, -1)
        for k in range(LEN // rows):
            part = slice(k * rows, (k + 1) * rows)
            pre[t, part] = against(normed[part], w) + offsets[t : t + 1]

    def step(k, carry):
        prod, held = carry
        rows = pl.ds(pl.multiple_of(k * 2 * LANES, 2 * LANES), 2 * LANES)
        forget = 1.0 / (1.0 + jnp.exp(-pre[0, rows]))
        entry = 1.0 / (1.0 + jnp.exp(-pre[1, rows]))
        cand = pre[2, rows]
        share = 1.0 / (forget + entry)
        keep = forget * share
        flow = entry * share * cand
        retain[rows] = keep
        candidate[rows] = cand
        kept_f[rows] = (1.0 - forget).astype(bf16)
        kept_i[rows] = (1.0 - entry).astype(bf16)
        held_0 = keep[:LANES] * held + flow[:LANES]
        prod_0 = keep[:LANES] * prod
        held = keep[LANES:] * held_0 + flow[LANES:]
        prod = keep[LANES:] * prod_0
        drive[rows] = jnp.concatenate([held_0, held], axis=0)
        decay[rows] = jnp.concatenate([prod_0, prod], axis=0)
        return prod, held

    start = (jnp.ones((LANES, wide), f32), jnp.zeros((LANES, wide), f32))
    prod, held = lax.fori_loop(0, LEN // (2 * LANES), step, start, unroll=4)
    ends = [jnp.zeros((1, wide), f32)]
    for k in range(LANES - 1):
        ends.append(prod[k : k + 1] * ends[-1] + held[k : k + 1])
    entering = jnp.concatenate(ends, axis=0)
    entering = jnp.concatenate([entering, entering], axis=0)

    def finish(k, _):
        rows = pl.ds(pl.multiple_of(k * 2 * LANES, 2 * LANES), 2 * LANES)
        value = drive[rows] + decay[rows] * entering
        states[rows] = value
        low[rows] = value.astype(bf16)
        return 0

    lax.fori_loop(0, LEN // (2 * LANES), finish, 0, unroll=4)


def gates(normed, offsets, arrays):
    nb, _, unit, width = arrays[0].shape
    total = 4 * nb * unit
    wide = total // 2
    tall = lambda g: (0, g)
    out = lambda dtype: jax.ShapeDtypeStruct((LEN, total), dtype)
    return pl.pallas_call(
        gates_kernel,
        grid=(2,),
        in_specs=[
            pl.BlockSpec((LEN, width), lambda g: (0, 0)),
            pl.BlockSpec((3, wide), tall),
        ]
        + [pl.BlockSpec(memory_space=pl.ANY)] * 4,
        out_specs=[pl.BlockSpec((LEN, wide), tall)] * 6,
        out_shape=[out(f32), out(f32), out(f32), out(bf16), out(bf16), out(bf16)],
        scratch_shapes=[
            pltpu.VMEM((3, 4 * nb, unit, width), bf16),
            pltpu.VMEM((3, LEN, wide), f32),
            pltpu.VMEM((LEN, wide), f32),
            pltpu.VMEM((LEN, wide), f32),
            pltpu.SemaphoreType.DMA,
        ],
        compiler_params=pltpu.CompilerParams(vmem_limit_bytes=VMEM_BYTES),
        cost_estimate=pl.CostEstimate(
            flops=6 * LEN * width * total, bytes_accessed=20 * LEN * total, transcendentals=2 * LEN * total
        ),
        name="gates",
    )(normed, offsets, *arrays)


def gelu_both(x):
    inner = np.float32(np.sqrt(2 / np.pi))
    square = x * x
    t = jnp.tanh(inner * (x + np.float32(0.044715) * (square * x)))
    cdf = 0.5 + 0.5 * t
    slope = cdf + (0.5 * x) * (1.0 - t * t) * (inner + np.float32(3 * 0.044715) * inner * square)
    return x * cdf, slope


def ffn_body(normed_two, cotangent, shifts, expand, contract, hidden, slope, finish, sent, kept, shift_grad):
    units, width = expand.shape
    rows = 256
    wide = 256
    total = [jnp.zeros((1, wide), f32) for _ in range(units // wide)]
    for k in range(LEN // rows):
        part = slice(k * rows, (k + 1) * rows)
        n2 = normed_two[part]
        ct = cotangent[part]
        for j in range(units // wide):
            cols = slice(j * wide, (j + 1) * wide)
            act, grad = gelu_both(against(n2, expand[cols]) + shifts[:, cols])
            hidden[part, cols] = act.astype(bf16)
            rounded = (against(ct, contract[cols]) * grad).astype(bf16)
            slope[part, cols] = rounded
            total[j] = total[j] + jnp.sum(rounded.astype(f32), axis=0, keepdims=True)
        finish(part, matmul(hidden[part], contract[...]), matmul(slope[part], expand[...]))
    shift_grad[...] = jnp.concatenate(total, axis=1)
    half = units // 2
    blocks, _, unit, _ = kept.shape
    for j, (target, dtype) in enumerate(((kept, f32), (sent, bf16))):
        cols = slice(j * half, (j + 1) * half)
        target[:, 0] = across(slope[:, cols], normed_two[...]).astype(dtype).reshape(blocks, unit, width)
        target[:, 1] = across(hidden[:, cols], cotangent[...]).astype(dtype).reshape(blocks, unit, width)


def first_kernel(inputs, cotangent, low0, low1, gain, shifts, *refs):
    own, readers = refs[:4], refs[4:12]
    (residual, scale, normed_two, branch, grad, sent, kept, shift_grad) = refs[12:20]
    expand, contract, readout, hidden, slope, sem, sem_two = refs[20:]
    nb = own[0].shape[0]
    unit, small = kept.shape[2], readout.shape[1]
    width = gain.shape[1]
    reads = fetch(
        [(r.at[:, pl.ds(2 * unit, small)], readout.at[pl.ds(k * nb, nb)]) for k, r in enumerate(readers)], sem
    )
    writes = fetch(
        [(w.at[:, pl.ds(0, unit)], expand.at[pl.ds(k * nb, nb)]) for k, w in enumerate(own)]
        + [(w.at[:, pl.ds(unit, unit)], contract.at[pl.ds(k * nb, nb)]) for k, w in enumerate(own)],
        sem_two,
    )
    for copy in reads:
        copy.wait()
    full = readout[...].reshape(-1, width)
    half = low0.shape[1]
    rows = 256
    for k in range(LEN // rows):
        part = slice(k * rows, (k + 1) * rows)
        value = inputs[part].astype(f32) + (matmul(low0[part], full[:half]) + matmul(low1[part], full[half:]))
        residual[part] = value
        inverse = lax.rsqrt(jnp.mean(value * value, axis=-1, keepdims=True) + epsilon)
        scale[part] = inverse
        normed_two[part] = (value * inverse * gain[...]).astype(bf16)
    for copy in writes:
        copy.wait()

    def finish(part, one, two):
        branch[part] = one
        grad[part] = two

    ffn_body(
        normed_two, cotangent, shifts, expand[...].reshape(-1, width), contract[...].reshape(-1, width), hidden, slope,
        finish, sent, kept, shift_grad,
    )


def second_kernel(residual, scale, normed_two, branch, grad, cotangent, gain, shifts, *refs):
    own = refs[:4]
    (output, residual_grad, rounded, gain_grad, sent, kept, shift_grad) = refs[4:11]
    expand, contract, hidden, slope, sem = refs[11:]
    nb = own[0].shape[0]
    unit = kept.shape[2]
    width = gain.shape[1]
    for copy in fetch(
        [(w.at[:, pl.ds(0, unit)], expand.at[pl.ds(k * nb, nb)]) for k, w in enumerate(own)]
        + [(w.at[:, pl.ds(unit, unit)], contract.at[pl.ds(k * nb, nb)]) for k, w in enumerate(own)],
        sem,
    ):
        copy.wait()
    gain_grad[...] = jnp.zeros_like(gain_grad)

    def finish(part, one, two):
        value = residual[part]
        output[part] = (value + (branch[part] + one)).astype(bf16)
        total = grad[part] + two
        inverse = scale[part]
        unscaled = value * inverse
        gain_grad[...] += jnp.sum(total * unscaled, axis=0, keepdims=True)
        pulled = total * gain[...]
        mean = jnp.mean(pulled * unscaled, axis=-1, keepdims=True)
        back = cotangent[part].astype(f32) + inverse * (pulled - unscaled * mean)
        residual_grad[part] = back
        rounded[part] = back.astype(bf16)

    ffn_body(
        normed_two, cotangent, shifts, expand[...].reshape(-1, width), contract[...].reshape(-1, width), hidden, slope,
        finish, sent, kept, shift_grad,
    )


def whole_specs(count):
    return [pl.BlockSpec(memory_space=pltpu.VMEM)] * count


def ffn_cost(units, width):
    return pl.CostEstimate(flops=12 * LEN * width * units, bytes_accessed=20 * 2**20, transcendentals=LEN * units)


def ffn_first(inputs, cotangent, lows, gain, shifts, own, readers, cut):
    nb, unit, small = own[0].shape[0], cut[0], cut[1]
    width = inputs.shape[1]
    units = 4 * nb * unit
    shape = jax.ShapeDtypeStruct
    return pl.pallas_call(
        first_kernel,
        in_specs=whole_specs(6) + [pl.BlockSpec(memory_space=pl.ANY)] * 12,
        out_specs=whole_specs(8),
        out_shape=[
            shape((LEN, width), f32),
            shape((LEN, 1), f32),
            shape((LEN, width), bf16),
            shape((LEN, width), f32),
            shape((LEN, width), f32),
            shape((2 * nb, 2, unit, width), bf16),
            shape((2 * nb, 2, unit, width), f32),
            shape((1, units), f32),
        ],
        scratch_shapes=[
            pltpu.VMEM((4 * nb, unit, width), bf16),
            pltpu.VMEM((4 * nb, unit, width), bf16),
            pltpu.VMEM((8 * nb, small, width), bf16),
            pltpu.VMEM((LEN, units), bf16),
            pltpu.VMEM((LEN, units), bf16),
            pltpu.SemaphoreType.DMA,
            pltpu.SemaphoreType.DMA,
        ],
        compiler_params=pltpu.CompilerParams(vmem_limit_bytes=VMEM_BYTES),
        cost_estimate=ffn_cost(units, width),
        name="ffn_first",
    )(inputs, cotangent, *lows, gain, shifts, *own, *readers)


def ffn_second(residual, scale, normed_two, branch, grad, cotangent, gain, shifts, own, cut):
    nb, unit = own[0].shape[0], cut[0]
    width = cotangent.shape[1]
    units = 4 * nb * unit
    shape = jax.ShapeDtypeStruct
    return pl.pallas_call(
        second_kernel,
        in_specs=whole_specs(8) + [pl.BlockSpec(memory_space=pl.ANY)] * 4,
        out_specs=whole_specs(7),
        out_shape=[
            shape((LEN, width), bf16),
            shape((LEN, width), f32),
            shape((LEN, width), bf16),
            shape((1, width), f32),
            shape((2 * nb, 2, unit, width), bf16),
            shape((2 * nb, 2, unit, width), f32),
            shape((1, units), f32),
        ],
        scratch_shapes=[
            pltpu.VMEM((4 * nb, unit, width), bf16),
            pltpu.VMEM((4 * nb, unit, width), bf16),
            pltpu.VMEM((LEN, units), bf16),
            pltpu.VMEM((LEN, units), bf16),
            pltpu.SemaphoreType.DMA,
        ],
        compiler_params=pltpu.CompilerParams(vmem_limit_bytes=VMEM_BYTES),
        cost_estimate=ffn_cost(units, width),
        name="ffn_second",
    )(residual, scale, normed_two, branch, grad, cotangent, gain, shifts, *own)


def back_kernel(skip, start, rounded, normed, retain, states, candidate, low, kept_f, kept_i, *refs):
    readers, weighers = refs[:4], refs[4:8]
    normed_grad, sent, kept, offset_grad = refs[8:12]
    readout, weights, pulled, decay, grads, sem = refs[12:]
    group = pl.program_id(0)
    wide = retain.shape[1]
    nb = weighers[0].shape[0]
    unit = weights.shape[2]
    width = normed.shape[1]
    steps = LEN // LANES

    @pl.when(group == 0)
    def _():
        pairs = [(r.at[:, pl.ds(skip, unit)], readout.at[pl.ds(k * nb, nb)]) for k, r in enumerate(readers)]
        pairs += [
            (w.at[:, t], weights.at[t, pl.ds(k * nb, nb)]) for k, w in enumerate(weighers) for t in range(3)
        ]
        for copy in fetch(pairs, sem):
            copy.wait()

    blocks = pl.ds((1 - group) * 2 * nb, 2 * nb)
    reader = readout[blocks].reshape(wide, width)
    rows = 256
    for k in range(LEN // rows):
        part = slice(k * rows, (k + 1) * rows)
        pulled[part] = against(rounded[part], reader)

    def step(k, carry):
        prod, held = carry
        at = steps - 2 - k
        rows = pl.ds(pl.multiple_of(at * LANES, LANES), LANES)
        after = retain[pl.ds(pl.multiple_of((at + 1) * LANES, LANES), LANES)]
        held = pulled[rows] + after * held
        prod = after * prod
        pulled[rows] = held
        decay[rows] = prod
        return prod, held

    last = pl.ds((steps - 1) * LANES, LANES)
    decay[last] = jnp.ones((LANES, wide), f32)
    prod, held = lax.fori_loop(0, steps - 1, step, (decay[last], pulled[last]), unroll=8)
    first_retain = retain[pl.ds(0, LANES)]
    ends = [jnp.zeros((1, wide), f32)]
    for k in range(LANES - 1, 0, -1):
        whole = held[k : k + 1] + prod[k : k + 1] * ends[-1]
        ends.append(first_retain[k : k + 1] * whole)
    entering = jnp.concatenate(ends[::-1], axis=0)

    def grads_of(rows, prior, entering):
        keep = retain[rows]
        carried = pulled[rows] + decay[rows] * entering
        rest = 1.0 - keep
        both = (carried * (prior - candidate[rows])) * (keep * rest)
        one = (both * kept_f[rows].astype(f32)).astype(bf16)
        two = (both * kept_i[rows].astype(f32) * -1.0).astype(bf16)
        three = (carried * rest).astype(bf16)
        for t, value in enumerate((one, two, three)):
            grads[rows, t * wide : (t + 1) * wide] = value
        return one.astype(f32), two.astype(f32), three.astype(f32)

    twice = jnp.concatenate([entering, entering], axis=0)
    before = jnp.concatenate([down(states[last]), states[pl.ds(0, LANES)]], axis=0)
    sums = grads_of(pl.ds(0, 2 * LANES), before, twice)

    def finish(k, sums):
        rows = pl.ds(pl.multiple_of(k * 2 * LANES, 2 * LANES), 2 * LANES)
        prior = states[pl.ds(pl.multiple_of(k * 2 * LANES - LANES, LANES), 2 * LANES)]
        return tuple(a + b for a, b in zip(sums, grads_of(rows, prior, twice)))

    sums = lax.fori_loop(1, steps // 2, finish, sums, unroll=3)
    for t in range(3):
        offset_grad[t : t + 1] = jnp.sum(sums[t], axis=0, keepdims=True)

    def produce(target, dtype):
        for t in range(3):
            value = across(grads[:, t * wide : (t + 1) * wide], normed[...])
            target[:, t] = value.astype(dtype).reshape(2 * nb, unit, width)
        target[:, 3] = across(low[...], rounded[...]).astype(dtype).reshape(2 * nb, unit, width)

    @pl.when(group == 0)
    def _():
        produce(sent, bf16)

    @pl.when(group == 1)
    def _():
        produce(kept, f32)

    w = weights[:, blocks].reshape(3 * wide, width)
    for k in range(LEN // rows):
        part = slice(k * rows, (k + 1) * rows)
        value = matmul(grads[part], w)

        @pl.when(group == 0)
        def _():
            normed_grad[part] = start[part] + value if start is not None else value

        @pl.when(group == 1)
        def _():
            normed_grad[part] = normed_grad[part] + value


def back_start(skip, *refs):
    back_kernel(skip, None, *refs)


def back_more(skip, start, *refs):
    back_kernel(skip, start, *refs)


def back(start, rounded, normed, kept, readers, weighers, skip):
    nb, _, unit, width = weighers[0].shape
    total = 4 * nb * unit
    wide = total // 2
    fixed = lambda g: (0, 0)
    tall = lambda g: (0, 1 - g)
    shape = jax.ShapeDtypeStruct
    firm = pl.BlockSpec((LEN, width), fixed)
    solid = pl.BlockSpec((2 * nb, 4, unit, width), lambda g: (0, 0, 0, 0))
    begun = [] if start is None else [start]
    return pl.pallas_call(
        partial(back_more if begun else back_start, skip),
        grid=(2,),
        in_specs=[firm] * (len(begun) + 2)
        + [pl.BlockSpec((LEN, wide), tall)] * 6
        + [pl.BlockSpec(memory_space=pl.ANY)] * 8,
        out_specs=[firm, solid, solid, pl.BlockSpec((3, wide), tall)],
        out_shape=[
            shape((LEN, width), f32),
            shape((2 * nb, 4, unit, width), bf16),
            shape((2 * nb, 4, unit, width), f32),
            shape((3, total), f32),
        ],
        scratch_shapes=[
            pltpu.VMEM((4 * nb, unit, width), bf16),
            pltpu.VMEM((3, 4 * nb, unit, width), bf16),
            pltpu.VMEM((LEN, wide), f32),
            pltpu.VMEM((LEN, wide), f32),
            pltpu.VMEM((LEN, 3 * wide), bf16),
            pltpu.SemaphoreType.DMA,
        ],
        compiler_params=pltpu.CompilerParams(vmem_limit_bytes=VMEM_BYTES),
        cost_estimate=pl.CostEstimate(
            flops=16 * LEN * width * total, bytes_accessed=24 * LEN * total, transcendentals=0
        ),
        name="back",
    )(*begun, rounded, normed, *kept, *readers, *weighers)


class Wires:
    def __init__(self, mesh):
        self.inner = mesh.shape["fsdp"]
        self.count = mesh.shape["dp"] * self.inner
        rest = [1 << b for b in range(1, self.inner.bit_length() - 1)]
        self.digits = [rest[i : i + 2] for i in range(0, len(rest), 2)]
        core, other = self.inner, 2 * self.inner
        self.bits = {"A": [1, other, core], "B": [other, 1, core]}

    def swap(self, value, mask):
        return lax.ppermute(value, AXES, [(i, i ^ mask) for i in range(self.count)])

    def spread(self, digit):
        return [sum(bit for j, bit in enumerate(digit) if k >> j & 1) for k in range(1 << len(digit))]

    def masks(self, order):
        found = [0]
        for digit in self.digits:
            found = [m ^ s for s in self.spread(digit) for m in found]
        lists = [np.array(found)]
        for bit in self.bits[order]:
            lists = lists + [m ^ bit for m in lists]
        return lists

    def line(self, held):
        for digit in self.digits:
            held = jnp.concatenate([held] + [self.swap(held, m) for m in self.spread(digit)[1:]])
        return held

    def gather(self, part, order):
        held = [self.line(part)]
        for bit in self.bits[order]:
            held = held + [self.swap(one, bit) for one in held]
        return held

    def gather_whole(self, part, order):
        held = self.line(part)
        for bit in self.bits[order]:
            held = jnp.concatenate([held, self.swap(held, bit)])
        return held

    def line_back(self, held, sent):
        for digit in reversed(self.digits):
            masks = self.spread(digit)
            blocks = jnp.split(held, len(masks))
            came = [self.swap(one.astype(sent), m) for one, m in zip(blocks[1:], masks[1:])]
            held = blocks[0]
            for other in came:
                held = held + other.astype(f32)
        return held

    def scatter(self, far, near, order):
        first, second, core = self.bits[order]
        far = far[1] + self.swap(far[0], core).astype(f32)
        far_clear, far_set = jnp.split(far.astype(bf16), 2)
        came_set = self.swap(far_set, second)
        came_clear = self.swap(far_clear, second)
        near = near[1] + self.swap(near[0], core).astype(f32)
        near_clear, near_set = jnp.split(near, 2)
        near_set = near_set + came_set.astype(f32)
        held = near_clear + came_clear.astype(f32) + self.swap(near_set.astype(bf16), first).astype(f32)
        return self.line_back(held, bf16)[0]

    def scatter_small(self, held, order):
        for bit in reversed(self.bits[order]):
            keep, send = jnp.split(held, 2)
            held = keep + self.swap(send, bit)
        return self.line_back(held, f32)[0]


def pick(which, options):
    found = options[-1]
    for k in range(len(options) - 2, -1, -1):
        found = jnp.where(which == k, options[k], found)
    return found


def half(items, k):
    return [items[2 * k], items[2 * k + 1], items[4 + 2 * k], items[5 + 2 * k]]


def solution(mesh):
    wires = Wires(mesh)
    count = wires.count
    masks = {order: wires.masks(order) for order in "AB"}
    exact = partial(jnp.matmul, precision=lax.Precision.HIGHEST)

    def shards(tokens, gating, offsets, prescale, readout, midscale, expand, shifts, contract, cotangent):
        me = lax.axis_index("dp") * wires.inner + lax.axis_index("fsdp")
        unit = readout.shape[0]
        wide = expand.shape[1]
        thin = prescale.shape[0]
        width = tokens.shape[1]
        assert tokens.shape[0] == LEN

        packed = jnp.concatenate([offsets, shifts, prescale, midscale])[None]
        table = wires.gather_whole(packed, "A")
        blocks = gating.T.reshape(3, unit, width)
        there = [[(d, (3 * d + k) % count) for d in range(count)] for k in range(3)]
        came = [lax.ppermute(blocks[k], AXES, there[k]) for k in range(3)]
        gate_part = jnp.stack([pick((me + t * count) % 3, came) for t in range(3)])
        gate_list = wires.gather(gate_part[None], "A")
        rest_list = wires.gather(jnp.concatenate([expand.T, contract, readout])[None], "B")
        merged = unit % 16 != 0
        if merged:
            nb = gate_list[0].shape[0]
            gate_list = [one.transpose(1, 0, 2, 3).reshape(1, 3, -1, width) for one in gate_list]
            cuts = [wide, 2 * wide]
            rest_list = [
                jnp.concatenate([p.reshape(-1, width) for p in jnp.split(one, cuts, axis=1)])[None] for one in rest_list
            ]
            big, small = nb * wide, nb * unit
        else:
            big, small = wide, unit

        gate_place = me ^ jnp.asarray(np.concatenate(half(masks["A"], 0) + half(masks["A"], 1)))
        ffn_place = me ^ jnp.asarray(np.concatenate(half(masks["B"], 0) + half(masks["B"], 1)))
        owner = me ^ jnp.asarray(np.concatenate(masks["A"]))
        natural = jnp.arange(count)
        to_natural = (natural[:, None] == owner[None]).astype(f32)
        to_gate = (gate_place[:, None] == natural[None]).astype(f32)
        to_ffn = (ffn_place[:, None] == natural[None]).astype(f32)
        ordered = exact(to_natural, table.astype(f32))
        cuts = np.cumsum([3 * unit, wide, thin])
        off_c, shift_c, pre_c, mid_c = jnp.split(ordered, cuts, axis=1)
        gain_one = pre_c.reshape(1, -1)
        gain_two = mid_c.reshape(1, -1)
        off_gate = jnp.einsum("pb,tbu->tpu", to_gate, off_c.reshape(3, count, unit), precision=lax.Precision.HIGHEST)
        off_halves = jnp.split(off_gate.reshape(3, -1), 2, axis=1)
        shift_halves = jnp.split(exact(to_ffn, shift_c).reshape(1, -1), 2, axis=1)

        inputs = interleaved(tokens)
        upstream = interleaved(cotangent)
        wide_inputs = inputs.astype(f32)
        scale_one = lax.rsqrt(jnp.mean(wide_inputs * wide_inputs, axis=-1, keepdims=True) + epsilon)
        normed = (wide_inputs * scale_one * gain_one).astype(bf16)
        kept = [gates(normed, off_halves[k], half(gate_list, k)) for k in range(2)]
        readers = [[rest_list[core * 4 + y * 2 + k] for core in range(2) for y in range(2)] for k in range(2)]
        cut = (big, small)
        residual, scale_two, normed_two, branch, grad, far_sent, far_kept, shift_far = ffn_first(
            inputs, upstream, [kept[0][3], kept[1][3]], gain_two, shift_halves[1], half(rest_list, 1),
            readers[0] + readers[1], cut,
        )
        output, residual_grad, rounded, midscale_grad, near_sent, near_kept, shift_near = ffn_second(
            residual, scale_two, normed_two, branch, grad, upstream, gain_two, shift_halves[0], half(rest_list, 0), cut
        )

        def unmerged(grads, size):
            if not merged:
                return grads
            first = 2 * grads.shape[2] // size
            pieces = grads.reshape(2, grads.shape[1], -1, size, width)
            return pieces.transpose(0, 2, 1, 3, 4).reshape(first, grads.shape[1], size, width)

        ffn_part = wires.scatter(
            [unmerged(g, wide) for g in (far_sent, far_kept)], [unmerged(g, wide) for g in (near_sent, near_kept)], "B"
        )
        normed_grad, go_far, keep_far, off_far = back(
            None, rounded, normed, kept[1], readers[1], half(gate_list, 1), 2 * big
        )
        normed_grad, go_near, keep_near, off_near = back(
            normed_grad, rounded, normed, kept[0], readers[0], half(gate_list, 0), 2 * big
        )
        gate_back = wires.scatter(
            [unmerged(g, unit) for g in (go_far, keep_far)], [unmerged(g, unit) for g in (go_near, keep_near)], "A"
        )
        back_way = [[(t, d) for d, t in there[k]] for k in range(3)]
        gating_part = jnp.concatenate(
            [
                lax.ppermute(pick((count * (k - me)) % 3, [gate_back[t] for t in range(3)]), AXES, back_way[k])
                for k in range(3)
            ]
        ).T
        unscaled = wide_inputs * scale_one
        prescale_grad = jnp.sum(normed_grad * unscaled, axis=0)
        pulled = normed_grad * gain_one
        mean = jnp.mean(pulled * unscaled, axis=-1, keepdims=True)
        tokens_grad = sequential(residual_grad + scale_one * (pulled - unscaled * mean))
        block_output = sequential(output)

        off_rows = jnp.concatenate([off_near, off_far], axis=1).reshape(3, count, unit)
        off_rows = jnp.einsum("pb,tpu->tbu", to_gate, off_rows, precision=lax.Precision.HIGHEST)
        shift_rows = exact(to_ffn.T, jnp.concatenate([shift_near, shift_far], axis=1).reshape(count, wide))
        vectors = jnp.concatenate(
            [
                off_rows.reshape(count, 3 * unit),
                shift_rows,
                prescale_grad.reshape(count, thin),
                midscale_grad.reshape(count, thin),
            ],
            axis=1,
        )
        vectors = wires.scatter_small(exact(to_natural.T, vectors), "A")
        offsets_part, shifts_part, prescale_part, midscale_part = jnp.split(vectors, cuts)
        return (
            block_output,
            tokens_grad,
            gating_part,
            offsets_part,
            prescale_part,
            gate_back[3],
            midscale_part,
            ffn_part[0].T,
            shifts_part,
            ffn_part[1],
        )

    rows = P(AXES, None)
    columns = P(None, AXES)
    flat = P(AXES)
    in_specs = (rows, columns, flat, flat, rows, flat, columns, flat, rows, rows)
    out_specs = (rows, rows, columns, flat, flat, rows, flat, columns, flat, rows)
    return jax.shard_map(shards, mesh=mesh, in_specs=in_specs, out_specs=out_specs, check_vma=False)
```

```python
from functools import partial

import jax
import jax.numpy as jnp
import numpy as np
from jax import lax
from jax.experimental import pallas as pl
from jax.experimental.pallas import tpu as pltpu
from jax.sharding import PartitionSpec as P

LEN = 1024
LANES = 8
STEPS = LEN // LANES
ROWS = 256
AXES = ("dp", "fsdp")
epsilon = 1e-06
bf16 = jnp.bfloat16
f32 = jnp.float32
ANY = pl.BlockSpec(memory_space=pl.ANY)
SCALAR = pl.BlockSpec(memory_space=pltpu.SMEM)
FILLER = pl.CostEstimate(flops=10**11, bytes_accessed=10**8, transcendentals=0)
QUICK = pl.CostEstimate(flops=1000, bytes_accessed=1000, transcendentals=0)
PARAMS = pltpu.CompilerParams(vmem_limit_bytes=56 * 1024 * 1024)


def matmul(left, right):
    return jnp.dot(left, right, preferred_element_type=f32)


def across(left, right):
    return lax.dot_general(left, right, (((0,), (0,)), ((), ())), preferred_element_type=f32)


def against(left, right):
    return lax.dot_general(left, right, (((1,), (1,)), ((), ())), preferred_element_type=f32)


def interleave_kernel(values, target, scratch):
    for j in range(scratch.shape[0]):
        columns = slice(j * 128, (j + 1) * 128)
        for run in range(LANES):
            rows = slice(run * STEPS, (run + 1) * STEPS)
            scratch[j, pl.ds(run, STEPS, stride=LANES)] = values[rows, columns].astype(f32)
        target[:, columns] = scratch[j].astype(target.dtype)


def interleaved(values):
    return pl.pallas_call(
        interleave_kernel,
        out_shape=jax.ShapeDtypeStruct(values.shape, values.dtype),
        scratch_shapes=[pltpu.VMEM((values.shape[1] // 128, LEN, 128), f32)],
        compiler_params=PARAMS,
        cost_estimate=QUICK,
        name="interleave",
    )(values)


def sequence_kernel(values, target, scratch):
    for j in range(scratch.shape[0]):
        columns = slice(j * 128, (j + 1) * 128)
        scratch[j] = values[:, columns].astype(f32)
        for run in range(LANES):
            rows = slice(run * STEPS, (run + 1) * STEPS)
            target[rows, columns] = scratch[j, pl.ds(run, STEPS, stride=LANES)].astype(target.dtype)


def sequential(values):
    return pl.pallas_call(
        sequence_kernel,
        out_shape=jax.ShapeDtypeStruct(values.shape, values.dtype),
        scratch_shapes=[pltpu.VMEM((values.shape[1] // 128, LEN, 128), f32)],
        compiler_params=PARAMS,
        cost_estimate=FILLER,
        name="sequence",
    )(values)


def down(values):
    return jnp.concatenate([jnp.zeros_like(values[:1]), values[:-1]], axis=0)


def tiles(k, count):
    if isinstance(k, int):
        return pl.ds(k * LANES, count * LANES)
    return pl.ds(pl.multiple_of(k * LANES, LANES), count * LANES)


def parts():
    return [slice(k, k + ROWS) for k in range(0, LEN, ROWS)]


def start(pairs, sem):
    copies = [pltpu.make_async_copy(source, target, sem) for source, target in pairs]
    for copy in copies:
        copy.start()
    return copies


def finish(copies):
    for copy in copies:
        copy.wait()


def placed(me, lists, arrays, first, size, target):
    found = []
    for masks, array in zip(lists, arrays):
        for b, mask in enumerate(masks):
            at = pl.multiple_of((me ^ mask) * size, size)
            found.append((array.at[b, pl.ds(first, size)], target.at[pl.ds(at, size)]))
    return found


def emitted(plans, rows, size, width):
    if plans is None:
        return [jax.ShapeDtypeStruct((rows, width), f32)]
    return [jax.ShapeDtypeStruct((len(masks), size, width), dtype) for masks, dtype in plans]


def emit(me, plans, source, targets):
    if plans is None:
        targets[0][...] = source[...]
        return
    for (masks, _), target in zip(plans, targets):
        size = target.shape[1]
        for p, mask in enumerate(masks):
            at = pl.multiple_of((me ^ mask) * size, size)
            target[p] = source[pl.ds(at, size)].astype(target.dtype)


def sorted_blocks(me, plans, grads, size):
    whole = grads[0].reshape(-1, size, grads[0].shape[1])
    return [jnp.take(whole, me ^ jnp.asarray(masks), axis=0).astype(dtype) for masks, dtype in plans]


def lanes_of(count, size):
    lane = lax.broadcasted_iota(jnp.int32, (1, count), 1)
    piece = ((lane.astype(f32) + 0.5) * (1.0 / size)).astype(jnp.int32)
    return piece, lane - piece * size


def selector(place):
    rows = lax.broadcasted_iota(jnp.int32, (128, place.shape[1]), 0)
    return jnp.where(rows == place, 1.0, 0.0).astype(bf16)


def laid_out(rows, owners, lane_owner, place):
    spread = matmul(rows, selector(place))
    return jnp.sum(jnp.where(owners == lane_owner, spread, 0.0), axis=0, keepdims=True)


def cut_up(vector, lane_owner, place, count):
    rows = lax.broadcasted_iota(jnp.int32, (count, vector.shape[1]), 0)
    found = jnp.where(rows == lane_owner, vector, 0.0)
    high = found.astype(bf16)
    low = (found - high.astype(f32)).astype(bf16)
    choose = selector(place)
    return against(high, choose) + against(low, choose)


def vectors_kernel(sizes, me, masks, offsets, shift_0, shift_1, prescale, midscale, target):
    count = target.shape[0]
    flat = jnp.concatenate([offsets[t : t + 1] for t in range(3)], axis=1)
    target[:, :128] = cut_up(flat, *lanes_of(flat.shape[1], sizes[0]), count)
    shifts = jnp.concatenate([shift_0[...], shift_1[...]], axis=1)
    target[:, 128:256] = cut_up(shifts, masks[...] ^ me[0], lanes_of(shifts.shape[1], sizes[1])[1], count)
    target[:, 256:384] = cut_up(prescale[...], *lanes_of(prescale.shape[1], sizes[2]), count)
    target[:, 384:512] = cut_up(midscale[...], *lanes_of(midscale.shape[1], sizes[2]), count)


def vector_rows(me, masks, sizes, count, *grads):
    return pl.pallas_call(
        partial(vectors_kernel, sizes),
        in_specs=[SCALAR] + [pl.BlockSpec(memory_space=pltpu.VMEM)] * 6,
        out_specs=pl.BlockSpec(memory_space=pltpu.VMEM),
        out_shape=jax.ShapeDtypeStruct((count, 512), f32),
        compiler_params=PARAMS,
        cost_estimate=QUICK,
        name="vectors",
    )(me, masks, *grads)


def gates_kernel(lists, size, sizes, me, inputs, rows, owner_masks, lane_masks, *refs):
    arrays = refs[: len(lists)]
    normed, share, low, pull_f, pull_i, gain_one, gain_two, shifts = refs[len(lists) : len(lists) + 8]
    weights, pre, mid, decay, drive, offsets, sem = refs[len(lists) + 8 :]
    group = pl.program_id(0)
    wide = share.shape[1]
    hidden = weights.shape[0] // 3

    @pl.when(group == 0)
    def _():
        copies = start(placed(me[0], lists, arrays, 0, size, weights), sem)
        owners = owner_masks[...] ^ me[1]
        width = inputs.shape[1]
        gain = laid_out(rows[:, 256:384], owners, *lanes_of(width, sizes[2]))
        gain_one[...] = gain
        gain_two[...] = laid_out(rows[:, 384:512], owners, *lanes_of(width, sizes[2]))
        place = lanes_of(shifts.shape[1], sizes[1])[1]
        shifts[...] = laid_out(rows[:, 128:256], owners, lane_masks[...] ^ me[1], place)
        flat = laid_out(rows[:, :128], owners, *lanes_of(3 * hidden, sizes[0]))
        for t in range(3):
            for k in range(hidden // wide):
                offsets[k, t : t + 1] = flat[:, t * hidden + k * wide : t * hidden + (k + 1) * wide]
        for part in parts():
            value = inputs[part].astype(f32)
            scale = lax.rsqrt(jnp.mean(value * value, axis=-1, keepdims=True) + epsilon)
            normed[part] = (value * scale * gain).astype(bf16)
        finish(copies)

    def step(k, carry):
        prod, held = carry
        rows = tiles(2 * k, 2)
        forget = 1.0 / (1.0 + jnp.exp(-pre[0, rows]))
        entry = 1.0 / (1.0 + jnp.exp(-pre[1, rows]))
        whole = 1.0 / (forget + entry)
        keep = forget * whole
        rest = entry * whole
        flow = rest * pre[2, rows]
        both = keep * rest
        share[rows] = rest
        mid[0, rows] = both * (1.0 - forget)
        mid[1, rows] = both * (entry - 1.0)
        held_0 = keep[:LANES] * held + flow[:LANES]
        prod_0 = keep[:LANES] * prod
        held = keep[LANES:] * held_0 + flow[LANES:]
        prod = keep[LANES:] * prod_0
        drive[rows] = jnp.concatenate([held_0, held], axis=0)
        decay[rows] = jnp.concatenate([prod_0, prod], axis=0)
        return prod, held

    begin = (jnp.ones((LANES, wide), f32), jnp.zeros((LANES, wide), f32))
    prod, held = begin
    ws = [weights[pl.ds(pl.multiple_of(t * hidden + group * wide, wide), wide)] for t in range(3)]
    for part in parts():
        for t in range(3):
            pre[t, part] = against(normed[part], ws[t]) + offsets[group, t : t + 1]
        for k in range(part.start // (2 * LANES), part.stop // (2 * LANES)):
            prod, held = step(k, (prod, held))
    ends = [jnp.zeros((1, wide), f32)]
    for k in range(LANES - 1):
        ends.append(prod[k : k + 1] * ends[-1] + held[k : k + 1])
    entering = jnp.concatenate(ends, axis=0)
    entering = jnp.concatenate([entering, entering], axis=0)

    def join(k, before):
        rows = tiles(2 * k, 2)
        value = drive[rows] + decay[rows] * entering
        low[rows] = value.astype(bf16)
        change = jnp.concatenate([before, value[:LANES]], axis=0) - pre[2, rows]
        pull_f[rows] = (change * mid[0, rows]).astype(bf16)
        pull_i[rows] = (change * mid[1, rows]).astype(bf16)
        return value[LANES:]

    lax.fori_loop(0, STEPS // 2, join, entering[:LANES], unroll=8)


def gates(me, inputs, rows, owner_masks, lane_masks, arrays, lists, size, sizes, hidden):
    width = inputs.shape[1]
    shape = jax.ShapeDtypeStruct
    whole = lambda one: pl.BlockSpec(one.shape, lambda g: (0, 0))
    wide = 256
    fixed = lambda g: (0, 0)
    tall = lambda g: (0, g)
    out = lambda dtype: jax.ShapeDtypeStruct((LEN, hidden), dtype)
    solid = pl.BlockSpec((LEN, width), fixed)
    return pl.pallas_call(
        partial(gates_kernel, lists, size, sizes),
        grid=(hidden // wide,),
        in_specs=[SCALAR, solid, whole(rows), whole(owner_masks), whole(lane_masks)] + [ANY] * len(arrays),
        out_specs=[solid]
        + [pl.BlockSpec((LEN, wide), tall)] * 4
        + [pl.BlockSpec((1, width), fixed)] * 2
        + [whole(lane_masks)],
        out_shape=[jax.ShapeDtypeStruct((LEN, width), bf16)]
        + [out(f32), out(bf16), out(bf16), out(bf16), shape((1, width), f32)]
        + [shape((1, width), f32), shape(lane_masks.shape, f32)],
        scratch_shapes=[
            pltpu.VMEM((3 * hidden, width), bf16),
            pltpu.VMEM((3, LEN, wide), f32),
            pltpu.VMEM((2, LEN, wide), f32),
            pltpu.VMEM((LEN, wide), f32),
            pltpu.VMEM((LEN, wide), f32),
            pltpu.VMEM((hidden // wide, 3, wide), f32),
            pltpu.SemaphoreType.DMA,
        ],
        compiler_params=PARAMS,
        cost_estimate=FILLER,
        name="gates",
    )(me, inputs, rows, owner_masks, lane_masks, *arrays)


def gelu_both(x):
    inner = np.float32(np.sqrt(2 / np.pi))
    square = x * x
    t = jnp.tanh(inner * (x + np.float32(0.044715) * (square * x)))
    cdf = 0.5 + 0.5 * t
    slope = cdf + (0.5 * x) * (1.0 - t * t) * (inner + np.float32(3 * 0.044715) * inner * square)
    return x * cdf, slope


def ffn_part(part, normed_two, cotangent, shifts, expand, contract, hidden, slope, shift_grad):
    units = expand.shape[0]
    n2 = normed_two[part]
    ct = cotangent[part]
    for j in range(0, units, 256):
        cols = slice(j, j + 256)
        act, grad = gelu_both(against(n2, expand[cols]) + shifts[:, cols])
        hidden[part, cols] = act.astype(bf16)
        rounded = (against(ct, contract[cols]) * grad).astype(bf16)
        slope[part, cols] = rounded
        shift_grad[:, cols] += jnp.sum(rounded.astype(f32), axis=0, keepdims=True)
    return matmul(hidden[part], contract[...]), matmul(slope[part], expand[...])


def ffn_grads(normed_two, cotangent, hidden, slope, sent, kept):
    units = hidden.shape[1]
    blocks, rows, width = kept.shape
    unit = rows // 2
    for j, target in enumerate((kept, sent)):
        cols = slice(j * units // 2, (j + 1) * units // 2)
        target[:, :unit] = across(slope[:, cols], normed_two[...]).astype(target.dtype).reshape(blocks, unit, width)
        target[:, unit:] = across(hidden[:, cols], cotangent[...]).astype(target.dtype).reshape(blocks, unit, width)


def weight_copies(own, unit, expand, contract):
    found, at = [], 0
    for one in own:
        count = one.shape[0]
        found.append((one.at[:, pl.ds(0, unit)], expand.at[pl.ds(at, count)]))
        found.append((one.at[:, pl.ds(unit, unit)], contract.at[pl.ds(at, count)]))
        at += count
    return found


def first_kernel(lists, size, skip, me, gain, shifts, inputs_h, cotangent_h, low_h, *refs):
    readers, own, refs = refs[: len(lists)], refs[len(lists) : -22], refs[-22:]
    (residual_h, normed_h, branch_h, grad_h, sent, kept, shift_grad) = refs[:7]
    (inputs, cotangent, low, readout, expand, contract, residual, normed_two, branch, grad, hidden, slope) = refs[7:19]
    in_sem, weight_sem, out_sem = refs[19:]
    unit = expand.shape[1]
    width = gain.shape[1]
    arriving = start(
        [(inputs_h, inputs), (low_h, low)] + placed(me[0], lists, readers, skip, size, readout), in_sem
    )
    weights = start(weight_copies(own, unit, expand, contract) + [(cotangent_h, cotangent)], weight_sem)
    shift_grad[...] = jnp.zeros_like(shift_grad)
    finish(arriving)
    leaving = []
    for part in parts():
        value = inputs[part].astype(f32) + matmul(low[part], readout[...])
        residual[part] = value
        inverse = lax.rsqrt(jnp.mean(value * value, axis=-1, keepdims=True) + epsilon)
        normed_two[part] = (value * inverse * gain[...]).astype(bf16)
    leaving += start([(residual, residual_h), (normed_two, normed_h)], out_sem)
    finish(weights)
    expand = expand[...].reshape(-1, width)
    contract = contract[...].reshape(-1, width)
    for part in parts():
        branch[part], grad[part] = ffn_part(
            part, normed_two, cotangent, shifts, expand, contract, hidden, slope, shift_grad
        )
        leaving += start([(branch.at[part], branch_h.at[part]), (grad.at[part], grad_h.at[part])], out_sem)
    ffn_grads(normed_two, cotangent, hidden, slope, sent, kept)
    finish(leaving)


def second_kernel(plans, count, me, gain, shifts, residual_h, normed_h, branch_h, grad_h, cotangent_h, low_h, *refs):
    own, refs = refs[:count], refs[count:]
    output_h, back_h, rounded_h, gain_grad, sent, kept, shift_grad = refs[:7]
    targets, refs = refs[7:-18], refs[-18:]
    residual, normed_two, branch, grad, cotangent, low, expand, contract = refs[:8]
    output, back, rounded, hidden, slope, read_grad, in_sem, part_sem, low_sem, out_sem = refs[8:]
    unit = expand.shape[1]
    width = gain.shape[1]
    weights = start(
        [(normed_h, normed_two), (cotangent_h, cotangent)] + weight_copies(own, unit, expand, contract), in_sem
    )
    others = start([(residual_h, residual), (branch_h, branch), (grad_h, grad)], part_sem)
    last = start([(low_h, low)], low_sem)
    gain_grad[...] = jnp.zeros_like(gain_grad)
    shift_grad[...] = jnp.zeros_like(shift_grad)
    finish(weights)
    expand = expand[...].reshape(-1, width)
    contract = contract[...].reshape(-1, width)
    leaving = []
    for k, part in enumerate(parts()):
        one, two = ffn_part(part, normed_two, cotangent, shifts, expand, contract, hidden, slope, shift_grad)
        if k == 0:
            finish(others)
        value = residual[part]
        output[part] = (value + (branch[part] + one)).astype(bf16)
        total = grad[part] + two
        inverse = lax.rsqrt(jnp.mean(value * value, axis=-1, keepdims=True) + epsilon)
        unscaled = value * inverse
        gain_grad[...] += jnp.sum(total * unscaled, axis=0, keepdims=True)
        pulled = total * gain[...]
        mean = jnp.mean(pulled * unscaled, axis=-1, keepdims=True)
        value = cotangent[part].astype(f32) + inverse * (pulled - unscaled * mean)
        back[part] = value
        rounded[part] = value.astype(bf16)
        leaving += start(
            [(o.at[part], h.at[part]) for o, h in ((output, output_h), (back, back_h), (rounded, rounded_h))], out_sem
        )
    ffn_grads(normed_two, cotangent, hidden, slope, sent, kept)
    finish(last)
    read_grad[...] = across(low[...], rounded[...])
    emit(me[0], plans, read_grad, targets)
    finish(leaving)


def vmem(shape, dtype):
    return pltpu.VMEM(shape, dtype)


WHOLE = pl.BlockSpec(memory_space=pltpu.VMEM)


def ffn_first(me, gain, shifts, inputs, cotangent, low, readers, lists, size, skip, own, unit):
    blocks = sum(one.shape[0] for one in own)
    width = inputs.shape[1]
    units = blocks * unit
    kept = (max(1, blocks // 2), 2 * units // max(2, blocks), width)
    shape = jax.ShapeDtypeStruct
    return pl.pallas_call(
        partial(first_kernel, lists, size, skip),
        in_specs=[SCALAR, WHOLE, WHOLE] + [ANY] * (3 + len(readers) + len(own)),
        out_specs=[ANY] * 4 + [WHOLE] * 3,
        out_shape=[
            shape((LEN, width), f32),
            shape((LEN, width), bf16),
            shape((LEN, width), f32),
            shape((LEN, width), f32),
            shape(kept, bf16),
            shape(kept, f32),
            shape((1, units), f32),
        ],
        scratch_shapes=[
            vmem((LEN, width), bf16),
            vmem((LEN, width), bf16),
            vmem(low.shape, bf16),
            vmem((low.shape[1], width), bf16),
            vmem((blocks, unit, width), bf16),
            vmem((blocks, unit, width), bf16),
            vmem((LEN, width), f32),
            vmem((LEN, width), bf16),
            vmem((LEN, width), f32),
            vmem((LEN, width), f32),
            vmem((LEN, units), bf16),
            vmem((LEN, units), bf16),
        ]
        + [pltpu.SemaphoreType.DMA] * 3,
        compiler_params=PARAMS,
        cost_estimate=FILLER,
        name="ffn_first",
    )(me, gain, shifts, inputs, cotangent, low, *readers, *own)


def ffn_second(me, gain, shifts, residual, normed_two, branch, grad, cotangent, low, own, unit, size, plans):
    blocks = sum(one.shape[0] for one in own)
    width = cotangent.shape[1]
    units = blocks * unit
    kept = (max(1, blocks // 2), 2 * units // max(2, blocks), width)
    targets = emitted(plans, low.shape[1], size, width)
    shape = jax.ShapeDtypeStruct
    return pl.pallas_call(
        partial(second_kernel, plans, len(own)),
        in_specs=[SCALAR, WHOLE, WHOLE] + [ANY] * (6 + len(own)),
        out_specs=[ANY] * 3 + [WHOLE] * (4 + len(targets)),
        out_shape=[
            shape((LEN, width), bf16),
            shape((LEN, width), f32),
            shape((LEN, width), bf16),
            shape((1, width), f32),
            shape(kept, bf16),
            shape(kept, f32),
            shape((1, units), f32),
        ]
        + targets,
        scratch_shapes=[
            vmem((LEN, width), f32),
            vmem((LEN, width), bf16),
            vmem((LEN, width), f32),
            vmem((LEN, width), f32),
            vmem((LEN, width), bf16),
            vmem(low.shape, bf16),
            vmem((blocks, unit, width), bf16),
            vmem((blocks, unit, width), bf16),
            vmem((LEN, width), bf16),
            vmem((LEN, width), f32),
            vmem((LEN, width), bf16),
            vmem((LEN, units), bf16),
            vmem((LEN, units), bf16),
            vmem((low.shape[1], width), f32),
        ]
        + [pltpu.SemaphoreType.DMA] * 4,
        compiler_params=PARAMS,
        cost_estimate=FILLER,
        name="ffn_second",
    )(me, gain, shifts, residual, normed_two, branch, grad, cotangent, low, *own)


def back_kernel(lists, size, skip, plans, me, rounded, normed, share, pull_f, pull_i, *refs):
    readers = refs[: len(lists)]
    grads, offset_grad = refs[len(lists) : len(lists) + 2]
    targets = refs[len(lists) + 2 : -6]
    gate_grad, readout, pulled, drive, decay, sem = refs[-6:]
    group = pl.program_id(0)
    wide = share.shape[1]
    hidden = readout.shape[0]

    @pl.when(group == 0)
    def _():
        finish(start(placed(me[0], lists, readers, skip, size, readout), sem))

    reader = readout[pl.ds(pl.multiple_of(group * wide, wide), wide)]
    held = jnp.zeros((LANES, wide), f32)
    prod = jnp.ones((LANES, wide), f32)
    for part in reversed(parts()):
        pulled[part] = against(rounded[part], reader)
        for k in reversed(range(part.start // LANES, part.stop // LANES)):
            if k < STEPS - 1:
                after = 1.0 - share[tiles(k + 1, 1)]
                prod = after * prod
                held = pulled[tiles(k, 1)] + after * held
            else:
                held = pulled[tiles(k, 1)]
            drive[tiles(k, 1)] = held
            decay[tiles(k, 1)] = prod
    first_retain = 1.0 - share[pl.ds(0, LANES)]
    ends = [jnp.zeros((1, wide), f32)]
    for k in range(LANES - 1, 0, -1):
        whole = held[k : k + 1] + prod[k : k + 1] * ends[-1]
        ends.append(first_retain[k : k + 1] * whole)
    entering = jnp.concatenate(ends[::-1], axis=0)
    entering = jnp.concatenate([entering, entering], axis=0)

    def more(k, sums):
        rows = tiles(2 * k, 2)
        carried = drive[rows] + decay[rows] * entering
        found = []
        for t, factor in enumerate((pull_f, pull_i, share)):
            value = (carried * factor[rows].astype(f32)).astype(bf16)
            grads[t, rows] = value
            found.append(sums[t] + value.astype(f32))
        return tuple(found)

    sums = (jnp.zeros((2 * LANES, wide), f32),) * 3
    for k in range(STEPS // 2):
        sums = more(k, sums)
    for t in range(3):
        offset_grad[t : t + 1] = jnp.sum(sums[t], axis=0, keepdims=True)
        rows = pl.ds(pl.multiple_of(t * hidden + group * wide, wide), wide)
        gate_grad[rows] = across(grads[t], normed[...])

    @pl.when(group == hidden // wide - 1)
    def _():
        emit(me[0], plans, gate_grad, targets)


def back(me, rounded, normed, share, pull_f, pull_i, readers, lists, size, skip, plans):
    width = normed.shape[1]
    hidden = share.shape[1]
    wide = 256
    fixed = lambda g: (0, 0)
    tall = lambda g: (0, g)
    shape = jax.ShapeDtypeStruct
    firm = pl.BlockSpec((LEN, width), fixed)
    targets = emitted(plans, 3 * hidden, 3 * size, width)
    return pl.pallas_call(
        partial(back_kernel, lists, size, skip, plans),
        grid=(hidden // wide,),
        in_specs=[SCALAR, firm, firm] + [pl.BlockSpec((LEN, wide), tall)] * 3 + [ANY] * len(readers),
        out_specs=[pl.BlockSpec((3, LEN, wide), lambda g: (0, 0, g)), pl.BlockSpec((3, wide), tall)]
        + [pl.BlockSpec(one.shape, lambda g, rank=len(one.shape): (0,) * rank) for one in targets],
        out_shape=[shape((3, LEN, hidden), bf16), shape((3, hidden), f32)] + targets,
        scratch_shapes=[
            vmem((3 * hidden, width), f32),
            vmem((hidden, width), bf16),
            vmem((LEN, wide), f32),
            vmem((LEN, wide), f32),
            vmem((LEN, wide), f32),
            pltpu.SemaphoreType.DMA,
        ],
        compiler_params=PARAMS,
        cost_estimate=FILLER,
        name="back",
    )(me, rounded, normed, share, pull_f, pull_i, *readers)


def inputs_kernel(lists, size, me, inputs, gain, back, grads_h, *refs):
    arrays = refs[: len(lists)]
    output, gain_grad, grads, weights, weight_sem, sem = refs[len(lists) :]
    arriving = start(placed(me[0], lists, arrays, 0, size, weights), weight_sem)
    hidden = weights.shape[0] // 3
    for part in parts():
        arriving += start([(grads_h.at[t, part], grads.at[t, part]) for t in range(3)], sem)
    gain_grad[...] = jnp.zeros_like(gain_grad)
    finish(arriving)
    for part in parts():
        total = matmul(grads[0, part], weights[:hidden])
        for t in range(1, 3):
            total = total + matmul(grads[t, part], weights[t * hidden : (t + 1) * hidden])
        value = inputs[part].astype(f32)
        inverse = lax.rsqrt(jnp.mean(value * value, axis=-1, keepdims=True) + epsilon)
        unscaled = value * inverse
        gain_grad[...] += jnp.sum(total * unscaled, axis=0, keepdims=True)
        pulled = total * gain[...]
        mean = jnp.mean(pulled * unscaled, axis=-1, keepdims=True)
        output[part] = back[part] + inverse * (pulled - unscaled * mean)


def inputs_back(me, inputs, gain, back_grad, grads, arrays, lists, size):
    width = inputs.shape[1]
    hidden = grads.shape[2]
    return pl.pallas_call(
        partial(inputs_kernel, lists, size),
        in_specs=[SCALAR, WHOLE, WHOLE, WHOLE, ANY] + [ANY] * len(arrays),
        out_specs=[WHOLE, WHOLE],
        out_shape=[jax.ShapeDtypeStruct((LEN, width), f32), jax.ShapeDtypeStruct((1, width), f32)],
        scratch_shapes=[
            vmem((3, LEN, hidden), bf16),
            vmem((3 * hidden, width), bf16),
            pltpu.SemaphoreType.DMA,
            pltpu.SemaphoreType.DMA,
        ],
        compiler_params=PARAMS,
        cost_estimate=FILLER,
        name="inputs_back",
    )(me, inputs, gain, back_grad, grads, *arrays)


class Wires:
    def __init__(self, mesh):
        self.inner = mesh.shape["fsdp"]
        self.count = mesh.shape["dp"] * self.inner
        rest = [1 << b for b in range(1, self.inner.bit_length() - 1)]
        self.digits = [rest[i : i + 2] for i in range(0, len(rest), 2)]
        self.core, self.x, self.y = self.inner, 2 * self.inner, 1
        self.bits = {"A": [self.y, self.x, self.core], "B": [self.x, self.y, self.core]}

    def swap(self, value, mask):
        return lax.ppermute(value, AXES, [(i, i ^ mask) for i in range(self.count)])

    def spread(self, digit):
        return [sum(bit for j, bit in enumerate(digit) if k >> j & 1) for k in range(1 << len(digit))]

    def masks(self, order):
        found = [0]
        for digit in self.digits:
            found = [m ^ s for s in self.spread(digit) for m in found]
        lists = [found]
        for bit in self.bits[order]:
            lists = lists + [[m ^ bit for m in one] for one in lists]
        return lists

    def line(self, held, digits, tie=None):
        for digit in digits:
            came = [self.swap(held, m) for m in self.spread(digit)[1:]]
            if tie:
                _, *came = tie(*came)
            held = jnp.concatenate([held] + came)
        return held

    def line_start(self, held):
        for digit in reversed(self.digits[1:]):
            held = self.line_end(*self.line_step(held, digit))
        return self.line_step(held, self.digits[0])

    def line_step(self, held, digit):
        masks = self.spread(digit)
        blocks = jnp.split(held, len(masks))
        return blocks[0], [self.swap(one.astype(bf16), m) for one, m in zip(blocks[1:], masks[1:])]

    def line_end(self, held, came):
        for other in came:
            held = held + other.astype(f32)
        return held


def tied(*values):
    return lax.optimization_barrier(values)


def solution(mesh):
    wires = Wires(mesh)
    count = wires.count
    masks = {order: wires.masks(order) for order in "AB"}
    flat = {order: sum(masks[order], []) for order in "AB"}

    def shards(tokens, gating, offsets, prescale, readout, midscale, expand, shifts, contract, cotangent):
        swap = wires.swap
        index = lax.axis_index("dp") * wires.inner + lax.axis_index("fsdp")
        unit = readout.shape[0]
        wide = expand.shape[1]
        thin = prescale.shape[0]
        width = tokens.shape[1]
        hidden = count * unit
        assert tokens.shape[0] == LEN
        me = index.astype(jnp.int32).reshape(1)

        rest = jnp.concatenate([expand.T, contract])[None]
        row = jnp.concatenate([jnp.pad(one, (0, 128 - one.shape[0])) for one in (offsets, shifts, prescale, midscale)])
        taken = 4 * unit
        part = jnp.pad(jnp.concatenate([gating.T, readout, row[None]]), ((0, -(taken + 1) % 8), (0, 0)))
        inputs = interleaved(tokens)
        gate_line = wires.line(part[None], wires.digits, lambda *came: tied(inputs, *came))
        gate_line, rest, cotangent = tied(gate_line, rest, cotangent)
        nz = gate_line.shape[0]
        cut = nz // 2
        gate_x = swap(gate_line, wires.x)
        gate_y = swap(gate_line, wires.y)
        rest_early = [swap(rest, m) for m in wires.spread(wires.digits[0])[1:]]
        upstream = interleaved(cotangent)
        gate_x, upstream, rest_early[0], rest_early[1] = tied(gate_x, upstream, rest_early[0], rest_early[1])
        gate_y, rest_early[2] = tied(gate_y, rest_early[2])
        gate_list = [gate_line, gate_x, gate_y, swap(gate_x[:cut], wires.y), swap(gate_y[cut:], wires.x)]
        gate_list += [swap(one, wires.core) for one in gate_list]
        rest_line = wires.line(jnp.concatenate([rest, *rest_early]), wires.digits[1:])
        rest_x = swap(rest_line, wires.x)
        rest_y = swap(rest_line, wires.y)
        rest_core = swap(rest_line, wires.core)

        quads = masks["A"]
        gate_lists = [quads[0], quads[2], quads[1], quads[3][:cut], quads[3][cut:]]
        gate_lists += [[m ^ wires.core for m in one] for one in gate_lists]
        rows = jnp.concatenate([one[:, taken] for one in gate_list])
        sizes = (3 * unit, wide, thin)
        owner_masks = jnp.asarray(np.array(sum(gate_lists, []), np.int32)[:, None])
        ffn_masks = np.concatenate([masks["A"][k] for k in (0, 1, 4, 5, 2, 3, 6, 7)])
        lane_masks = jnp.asarray(np.repeat(ffn_masks, wide).astype(np.int32)[None])

        if unit % 16:
            places = np.argsort(np.asarray(sum(gate_lists, [])))
            whole = jnp.take(jnp.concatenate(gate_list), jnp.asarray(places)[index ^ jnp.arange(count)], axis=0)
            gate_list = [
                jnp.concatenate([whole[:, : 3 * unit].reshape(-1, width), whole[:, 3 * unit : taken].reshape(-1, width)])[None]
            ]
            gate_lists, gate_size, read_size, zero = [[0]], 3 * hidden, hidden, jnp.zeros_like(me)
            ffn_unit = 4 * nz * wide
        else:
            gate_size, read_size, zero = 3 * unit, unit, me
            ffn_unit = wide

        both = jnp.concatenate([zero, me])
        normed, share, low, pull_f, pull_i, gain_one, gain_two, all_shifts = gates(
            both, inputs, rows, owner_masks, lane_masks, gate_list, gate_lists, gate_size, sizes, hidden
        )
        shift_halves = jnp.split(all_shifts, 2, axis=1)
        low, rest_y, rest_x, rest_core = tied(low, rest_y, rest_x, rest_core)
        rest_corner = [swap(rest_x[:cut], wires.y), swap(rest_y[cut:], wires.x)]

        def merged(group):
            if not unit % 16:
                return group
            halves = [jnp.concatenate([one[:, at : at + wide].reshape(-1, width) for one in group]) for at in (0, wide)]
            return [jnp.concatenate(halves)[None]]

        own = merged([rest_line, rest_y, rest_core, swap(rest_y, wires.core)])

        def apart(grads):
            if not unit % 16:
                return grads
            return grads.reshape(2, -1, wide, width).transpose(1, 0, 2, 3).reshape(-1, 2 * wide, width)

        residual, normed_two, branch, grad, sent_0, kept_0, shift_0 = ffn_first(
            zero, gain_two, shift_halves[0], inputs, upstream, low, gate_list, gate_lists, read_size, gate_size, own,
            ffn_unit,
        )
        residual, normed_two, branch, grad, sent_0, kept_0, shift_0, rest_x, *rest_corner = tied(
            residual, normed_two, branch, grad, sent_0, kept_0, shift_0, rest_x, *rest_corner
        )
        far = [rest_x, *rest_corner]
        own = merged(far + [swap(one, wires.core) for one in far])
        near_core = swap(apart(sent_0), wires.core)
        half = count // 2
        read_plans = [(flat["A"][:half], f32), (flat["A"][half:], bf16)]
        output, residual_grad, rounded, midscale_grad, sent_1, kept_1, shift_1, *read_blocks = ffn_second(
            zero, gain_two, shift_halves[1], residual, normed_two, branch, grad, upstream, low, own, ffn_unit, unit,
            None if unit % 16 else read_plans,
        )
        read_kept, read_sent = sorted_blocks(index, read_plans, read_blocks, unit) if unit % 16 else read_blocks

        output, residual_grad, rounded, midscale_grad, sent_1, kept_1, shift_1, read_kept, read_sent, near_core = tied(
            output, residual_grad, rounded, midscale_grad, sent_1, kept_1, shift_1, read_kept, read_sent, near_core
        )
        far_core = swap(apart(sent_1), wires.core)
        read_core = swap(read_sent, wires.core)
        ffn_terms = [(apart(kept_0), near_core), (apart(kept_1), far_core)]

        def quad(k, low, high):
            kept, came = ffn_terms[k // 2]
            base = k % 2 * nz
            ffn = kept[base + low : base + high] + came[base + low : base + high].astype(f32)
            base = k * nz
            read = read_kept[base + low : base + high] + read_core[base + low : base + high].astype(f32)
            return jnp.concatenate([ffn, read], axis=1)

        send_a, send_b = quad(3, 0, cut).astype(bf16), quad(3, cut, nz).astype(bf16)
        rounded, send_a, send_b = tied(rounded, send_a, send_b)
        corner_a, corner_b = swap(send_a, wires.y), swap(send_b, wires.x)
        gate_plans = [
            (flat["A"][:half], f32), (masks["A"][7], bf16), (masks["A"][4] + masks["A"][5] + masks["A"][6], bf16)
        ]
        gate_grads, off_grad, *gate_blocks = back(
            zero, rounded, normed, share, pull_f, pull_i, gate_list, gate_lists, read_size, gate_size,
            None if unit % 16 else gate_plans,
        )
        if unit % 16:
            gate_blocks = sorted_blocks(index, gate_plans, gate_blocks, 3 * unit)
        gate_kept, corner_sent, others_sent, gate_grads, off_grad, corner_a, corner_b = tied(
            *gate_blocks, gate_grads, off_grad, corner_a, corner_b
        )
        corner_core = swap(corner_sent, wires.core)
        others_core = swap(others_sent, wires.core)
        send_x = jnp.concatenate([quad(2, 0, cut) + corner_a.astype(f32), quad(2, cut, nz)]).astype(bf16)
        send_y = jnp.concatenate([quad(1, 0, cut), quad(1, cut, nz) + corner_b.astype(f32)]).astype(bf16)
        gate_corner = (gate_kept[3 * nz :] + corner_core.astype(f32)).astype(bf16)
        send_a, send_b = gate_corner[:cut], gate_corner[cut:]
        gate_grads, send_a, send_b, send_x, send_y, output, midscale_grad, off_grad, shift_0, shift_1 = tied(
            gate_grads, send_a, send_b, send_x, send_y, output, midscale_grad, off_grad, shift_0, shift_1
        )
        corner_a, corner_b = swap(send_a, wires.y), swap(send_b, wires.x)
        rest_x, rest_y = swap(send_x, wires.x), swap(send_y, wires.y)
        tokens_grad, prescale_grad = inputs_back(
            zero, inputs, gain_one, residual_grad, gate_grads, gate_list, gate_lists, gate_size
        )
        block_output = sequential(output)
        corner_a, corner_b, rest_x, rest_y, tokens_grad, prescale_grad, block_output = tied(
            corner_a, corner_b, rest_x, rest_y, tokens_grad, prescale_grad, block_output
        )

        def side(k, low, high):
            part = slice(k * nz + low, k * nz + high)
            return gate_kept[part] + others_core[part].astype(f32)

        send_x = jnp.concatenate([side(2, 0, cut) + corner_a.astype(f32), side(2, cut, nz)]).astype(bf16)
        send_y = jnp.concatenate([side(1, 0, cut), side(1, cut, nz) + corner_b.astype(f32)]).astype(bf16)
        send_x, send_y, prescale_grad, rest_x, rest_y = tied(send_x, send_y, prescale_grad, rest_x, rest_y)
        gate_x, gate_y = swap(send_x, wires.x), swap(send_y, wires.y)
        rest_kept, rest_came = wires.line_start(quad(0, 0, nz) + rest_x.astype(f32) + rest_y.astype(f32))
        vectors = vector_rows(
            me, lane_masks, sizes, count, off_grad, shift_0, shift_1, prescale_grad, midscale_grad
        )
        gate_x, gate_y, tokens_grad, vectors, rest_came[0], rest_came[1] = tied(
            gate_x, gate_y, tokens_grad, vectors, rest_came[0], rest_came[1]
        )
        gate_part = side(0, 0, nz) + gate_x.astype(f32) + gate_y.astype(f32)
        gate_kept, gate_came = wires.line_start(gate_part)
        vectors = lax.all_to_all(vectors, AXES, 0, 0, tiled=True)
        tokens_grad = sequential(tokens_grad)
        tokens_grad, vectors, block_output, rest_kept, rest_came, gate_kept, gate_came = tied(
            tokens_grad, vectors, block_output, rest_kept, rest_came, gate_kept, gate_came
        )
        rest_part = wires.line_end(rest_kept, rest_came)[0]
        gate_part = wires.line_end(gate_kept, gate_came)[0]
        vectors = jnp.sum(vectors, axis=0)
        offsets_part, shifts_part, prescale_part, midscale_part = (
            vectors[at : at + size] for at, size in zip(range(0, 512, 128), (*sizes, thin))
        )
        return (
            block_output,
            tokens_grad,
            gate_part.T,
            offsets_part,
            prescale_part,
            rest_part[2 * wide :],
            midscale_part,
            rest_part[:wide].T,
            shifts_part,
            rest_part[wide : 2 * wide],
        )

    rows = P(AXES, None)
    columns = P(None, AXES)
    line = P(AXES)
    in_specs = (rows, columns, line, line, rows, line, columns, line, rows, rows)
    out_specs = (rows, rows, columns, line, line, rows, line, columns, line, rows)
    return jax.shard_map(shards, mesh=mesh, in_specs=in_specs, out_specs=out_specs, check_vma=False)
```

```python
from functools import partial

import jax
import jax.numpy as jnp
import numpy as np
from jax import lax
from jax.experimental import pallas as pl
from jax.experimental.pallas import tpu as pltpu
from jax.sharding import PartitionSpec as P

LEN = 1024
LANES = 8
STEPS = LEN // LANES
ROWS = 256
AXES = ("dp", "fsdp")
epsilon = 1e-06
bf16 = jnp.bfloat16
f32 = jnp.float32
ANY = pl.BlockSpec(memory_space=pl.ANY)
SCALAR = pl.BlockSpec(memory_space=pltpu.SMEM)
FILLER = pl.CostEstimate(flops=10**11, bytes_accessed=10**8, transcendentals=0)
QUICK = pl.CostEstimate(flops=1000, bytes_accessed=1000, transcendentals=0)
PARAMS = pltpu.CompilerParams(vmem_limit_bytes=56 * 1024 * 1024)


def matmul(left, right):
    return jnp.dot(left, right, preferred_element_type=f32)


def across(left, right):
    return lax.dot_general(left, right, (((0,), (0,)), ((), ())), preferred_element_type=f32)


def against(left, right):
    return lax.dot_general(left, right, (((1,), (1,)), ((), ())), preferred_element_type=f32)


def interleave_kernel(values, target, scratch):
    for j in range(scratch.shape[0]):
        columns = slice(j * 128, (j + 1) * 128)
        for run in range(LANES):
            rows = slice(run * STEPS, (run + 1) * STEPS)
            scratch[j, pl.ds(run, STEPS, stride=LANES)] = values[rows, columns].astype(f32)
        target[:, columns] = scratch[j].astype(target.dtype)


def interleaved(values):
    return pl.pallas_call(
        interleave_kernel,
        out_shape=jax.ShapeDtypeStruct(values.shape, values.dtype),
        scratch_shapes=[pltpu.VMEM((values.shape[1] // 128, LEN, 128), f32)],
        compiler_params=PARAMS,
        cost_estimate=QUICK,
        name="interleave",
    )(values)


def sequence_kernel(values, target, scratch):
    for j in range(scratch.shape[0]):
        columns = slice(j * 128, (j + 1) * 128)
        scratch[j] = values[:, columns].astype(f32)
        for run in range(LANES):
            rows = slice(run * STEPS, (run + 1) * STEPS)
            target[rows, columns] = scratch[j, pl.ds(run, STEPS, stride=LANES)].astype(target.dtype)


def sequential(values, cost):
    return pl.pallas_call(
        sequence_kernel,
        out_shape=jax.ShapeDtypeStruct(values.shape, values.dtype),
        scratch_shapes=[pltpu.VMEM((values.shape[1] // 128, LEN, 128), f32)],
        compiler_params=PARAMS,
        cost_estimate=cost,
        name="sequence",
    )(values)


def down(values):
    return jnp.concatenate([jnp.zeros_like(values[:1]), values[:-1]], axis=0)


def tiles(k, count):
    if isinstance(k, int):
        return pl.ds(k * LANES, count * LANES)
    return pl.ds(pl.multiple_of(k * LANES, LANES), count * LANES)


def parts():
    return [slice(k, k + ROWS) for k in range(0, LEN, ROWS)]


def start(pairs, sem):
    copies = [pltpu.make_async_copy(source, target, sem) for source, target in pairs]
    for copy in copies:
        copy.start()
    return copies


def finish(copies):
    for copy in copies:
        copy.wait()


def placed(me, lists, arrays, first, size, target):
    found = []
    for masks, array in zip(lists, arrays):
        for b, mask in enumerate(masks):
            at = pl.multiple_of((me ^ mask) * size, size)
            found.append((array.at[b, pl.ds(first, size)], target.at[pl.ds(at, size)]))
    return found


def emitted(plans, rows, size, width):
    if plans is None:
        return [jax.ShapeDtypeStruct((rows, width), f32)]
    return [jax.ShapeDtypeStruct((len(masks), size, width), dtype) for masks, dtype in plans]


def emit(me, plans, source, targets):
    if plans is None:
        targets[0][...] = source[...]
        return
    for (masks, _), target in zip(plans, targets):
        size = target.shape[1]
        for p, mask in enumerate(masks):
            at = pl.multiple_of((me ^ mask) * size, size)
            target[p] = source[pl.ds(at, size)].astype(target.dtype)


def sorted_blocks(me, plans, grads, size):
    whole = grads[0].reshape(-1, size, grads[0].shape[1])
    return [jnp.take(whole, me ^ jnp.asarray(masks), axis=0).astype(dtype) for masks, dtype in plans]


def lanes_of(count, size):
    lane = lax.broadcasted_iota(jnp.int32, (1, count), 1)
    piece = ((lane.astype(f32) + 0.5) * (1.0 / size)).astype(jnp.int32)
    return piece, lane - piece * size


def selector(place):
    rows = lax.broadcasted_iota(jnp.int32, (128, place.shape[1]), 0)
    return jnp.where(rows == place, 1.0, 0.0).astype(bf16)


def laid_out(rows, owners, lane_owner, place):
    spread = matmul(rows, selector(place))
    return jnp.sum(jnp.where(owners == lane_owner, spread, 0.0), axis=0, keepdims=True)


def cut_up(vector, lane_owner, place, count):
    rows = lax.broadcasted_iota(jnp.int32, (count, vector.shape[1]), 0)
    found = jnp.where(rows == lane_owner, vector, 0.0)
    high = found.astype(bf16)
    low = (found - high.astype(f32)).astype(bf16)
    choose = selector(place)
    return against(high, choose) + against(low, choose)


def vectors_kernel(sizes, me, masks, offsets, shift_0, shift_1, prescale, midscale, target):
    count = target.shape[0]
    flat = jnp.concatenate([offsets[t : t + 1] for t in range(3)], axis=1)
    target[:, :128] = cut_up(flat, *lanes_of(flat.shape[1], sizes[0]), count)
    shifts = jnp.concatenate([shift_0[...], shift_1[...]], axis=1)
    target[:, 128:256] = cut_up(shifts, masks[...] ^ me[0], lanes_of(shifts.shape[1], sizes[1])[1], count)
    target[:, 256:384] = cut_up(prescale[...], *lanes_of(prescale.shape[1], sizes[2]), count)
    target[:, 384:512] = cut_up(midscale[...], *lanes_of(midscale.shape[1], sizes[2]), count)


def vector_rows(me, masks, sizes, count, *grads):
    return pl.pallas_call(
        partial(vectors_kernel, sizes),
        in_specs=[SCALAR] + [pl.BlockSpec(memory_space=pltpu.VMEM)] * 6,
        out_specs=pl.BlockSpec(memory_space=pltpu.VMEM),
        out_shape=jax.ShapeDtypeStruct((count, 512), f32),
        compiler_params=PARAMS,
        cost_estimate=FILLER,
        name="vectors",
    )(me, masks, *grads)


def gates_kernel(lists, size, taken, row_count, sizes, me, inputs, owner_masks, lane_masks, *refs):
    row_arrays, refs = refs[:row_count], refs[row_count:]
    arrays = refs[: len(lists)]
    normed, share, low, pull_f, pull_i, gain_one, gain_two, shifts = refs[len(lists) : len(lists) + 8]
    weights, pre, mid, decay, drive, offsets, small, sem, small_sem = refs[len(lists) + 8 :]
    group = pl.program_id(0)
    wide = share.shape[1]
    hidden = weights.shape[0] // 3

    @pl.when(group == 0)
    def _():
        copies = start(placed(me[0], lists, arrays, 0, size, weights), sem)
        found, at = [], 0
        for array in row_arrays:
            found.append((array.at[:, pl.ds(taken, LANES)], small.at[pl.ds(at, array.shape[0])]))
            at += array.shape[0]
        finish(start(found, small_sem))
        rows = jnp.sum(small[...].astype(f32), axis=1).astype(bf16)
        owners = owner_masks[...] ^ me[1]
        width = inputs.shape[1]
        gain = laid_out(rows[:, 256:384], owners, *lanes_of(width, sizes[2]))
        gain_one[...] = gain
        gain_two[...] = laid_out(rows[:, 384:512], owners, *lanes_of(width, sizes[2]))
        place = lanes_of(shifts.shape[1], sizes[1])[1]
        shifts[...] = laid_out(rows[:, 128:256], owners, lane_masks[...] ^ me[1], place)
        flat = laid_out(rows[:, :128], owners, *lanes_of(3 * hidden, sizes[0]))
        for t in range(3):
            for k in range(hidden // wide):
                offsets[k, t : t + 1] = flat[:, t * hidden + k * wide : t * hidden + (k + 1) * wide]
        for part in parts():
            value = inputs[part].astype(f32)
            scale = lax.rsqrt(jnp.mean(value * value, axis=-1, keepdims=True) + epsilon)
            normed[part] = (value * scale * gain).astype(bf16)
        finish(copies)

    def step(k, carry):
        prod, held = carry
        rows = tiles(2 * k, 2)
        forget = 1.0 / (1.0 + jnp.exp(-pre[0, rows]))
        entry = 1.0 / (1.0 + jnp.exp(-pre[1, rows]))
        whole = 1.0 / (forget + entry)
        keep = forget * whole
        rest = entry * whole
        flow = rest * pre[2, rows]
        both = keep * rest
        share[rows] = rest
        mid[0, rows] = both * (1.0 - forget)
        mid[1, rows] = both * (entry - 1.0)
        held_0 = keep[:LANES] * held + flow[:LANES]
        prod_0 = keep[:LANES] * prod
        held = keep[LANES:] * held_0 + flow[LANES:]
        prod = keep[LANES:] * prod_0
        drive[rows] = jnp.concatenate([held_0, held], axis=0)
        decay[rows] = jnp.concatenate([prod_0, prod], axis=0)
        return prod, held

    begin = (jnp.ones((LANES, wide), f32), jnp.zeros((LANES, wide), f32))
    prod, held = begin
    ws = [weights[pl.ds(pl.multiple_of(t * hidden + group * wide, wide), wide)] for t in range(3)]
    for part in parts():
        for t in range(3):
            pre[t, part] = against(normed[part], ws[t]) + offsets[group, t : t + 1]
        for k in range(part.start // (2 * LANES), part.stop // (2 * LANES)):
            prod, held = step(k, (prod, held))
    ends = [jnp.zeros((1, wide), f32)]
    for k in range(LANES - 1):
        ends.append(prod[k : k + 1] * ends[-1] + held[k : k + 1])
    entering = jnp.concatenate(ends, axis=0)
    entering = jnp.concatenate([entering, entering], axis=0)

    def join(k, before):
        rows = tiles(2 * k, 2)
        value = drive[rows] + decay[rows] * entering
        low[rows] = value.astype(bf16)
        change = jnp.concatenate([before, value[:LANES]], axis=0) - pre[2, rows]
        pull_f[rows] = (change * mid[0, rows]).astype(bf16)
        pull_i[rows] = (change * mid[1, rows]).astype(bf16)
        return value[LANES:]

    lax.fori_loop(0, STEPS // 2, join, entering[:LANES], unroll=8)


def gates(me, inputs, row_arrays, taken, owner_masks, lane_masks, arrays, lists, size, sizes, hidden):
    width = inputs.shape[1]
    shape = jax.ShapeDtypeStruct
    whole = lambda one: pl.BlockSpec(one.shape, lambda g: (0, 0))
    wide = 256
    fixed = lambda g: (0, 0)
    tall = lambda g: (0, g)
    out = lambda dtype: jax.ShapeDtypeStruct((LEN, hidden), dtype)
    solid = pl.BlockSpec((LEN, width), fixed)
    return pl.pallas_call(
        partial(gates_kernel, lists, size, taken, len(row_arrays), sizes),
        grid=(hidden // wide,),
        in_specs=[SCALAR, solid, whole(owner_masks), whole(lane_masks)] + [ANY] * (len(row_arrays) + len(arrays)),
        out_specs=[solid]
        + [pl.BlockSpec((LEN, wide), tall)] * 4
        + [pl.BlockSpec((1, width), fixed)] * 2
        + [whole(lane_masks)],
        out_shape=[jax.ShapeDtypeStruct((LEN, width), bf16)]
        + [out(f32), out(bf16), out(bf16), out(bf16), shape((1, width), f32)]
        + [shape((1, width), f32), shape(lane_masks.shape, f32)],
        scratch_shapes=[
            pltpu.VMEM((3 * hidden, width), bf16),
            pltpu.VMEM((3, LEN, wide), f32),
            pltpu.VMEM((2, LEN, wide), f32),
            pltpu.VMEM((LEN, wide), f32),
            pltpu.VMEM((LEN, wide), f32),
            pltpu.VMEM((hidden // wide, 3, wide), f32),
            pltpu.VMEM((owner_masks.shape[0], LANES, width), bf16),
            pltpu.SemaphoreType.DMA,
            pltpu.SemaphoreType.DMA,
        ],
        compiler_params=PARAMS,
        cost_estimate=FILLER,
        name="gates",
    )(me, inputs, owner_masks, lane_masks, *row_arrays, *arrays)


def gelu_both(x):
    inner = np.float32(np.sqrt(2 / np.pi))
    square = x * x
    t = jnp.tanh(inner * (x + np.float32(0.044715) * (square * x)))
    cdf = 0.5 + 0.5 * t
    slope = cdf + (0.5 * x) * (1.0 - t * t) * (inner + np.float32(3 * 0.044715) * inner * square)
    return x * cdf, slope


def ffn_part(part, normed_two, cotangent, shifts, expand, contract, hidden, slope, shift_grad):
    units = expand.shape[0]
    n2 = normed_two[part]
    ct = cotangent[part]
    for j in range(0, units, 256):
        cols = slice(j, j + 256)
        act, grad = gelu_both(against(n2, expand[cols]) + shifts[:, cols])
        hidden[part, cols] = act.astype(bf16)
        rounded = (against(ct, contract[cols]) * grad).astype(bf16)
        slope[part, cols] = rounded
        shift_grad[:, cols] += jnp.sum(rounded.astype(f32), axis=0, keepdims=True)
    return matmul(hidden[part], contract[...]), matmul(slope[part], expand[...])


def ffn_grads(normed_two, cotangent, hidden, slope, sent, kept):
    units = hidden.shape[1]
    blocks, rows, width = kept.shape
    unit = rows // 2
    for j, target in enumerate((kept, sent)):
        cols = slice(j * units // 2, (j + 1) * units // 2)
        target[:, :unit] = across(slope[:, cols], normed_two[...]).astype(target.dtype).reshape(blocks, unit, width)
        target[:, unit:] = across(hidden[:, cols], cotangent[...]).astype(target.dtype).reshape(blocks, unit, width)


def weight_copies(own, unit, expand, contract):
    found, at = [], 0
    for one in own:
        count = one.shape[0]
        found.append((one.at[:, pl.ds(0, unit)], expand.at[pl.ds(at, count)]))
        found.append((one.at[:, pl.ds(unit, unit)], contract.at[pl.ds(at, count)]))
        at += count
    return found


def first_kernel(lists, size, skip, me, gain, shifts, inputs_h, cotangent_h, low_h, *refs):
    readers, own, refs = refs[: len(lists)], refs[len(lists) : -22], refs[-22:]
    (residual_h, normed_h, branch_h, grad_h, sent, kept, shift_grad) = refs[:7]
    (inputs, cotangent, low, readout, expand, contract, residual, normed_two, branch, grad, hidden, slope) = refs[7:19]
    in_sem, weight_sem, out_sem = refs[19:]
    unit = expand.shape[1]
    width = gain.shape[1]
    arriving = start(
        [(inputs_h, inputs), (low_h, low)] + placed(me[0], lists, readers, skip, size, readout), in_sem
    )
    weights = start(weight_copies(own, unit, expand, contract) + [(cotangent_h, cotangent)], weight_sem)
    shift_grad[...] = jnp.zeros_like(shift_grad)
    finish(arriving)
    leaving = []
    for part in parts():
        value = inputs[part].astype(f32) + matmul(low[part], readout[...])
        residual[part] = value
        inverse = lax.rsqrt(jnp.mean(value * value, axis=-1, keepdims=True) + epsilon)
        normed_two[part] = (value * inverse * gain[...]).astype(bf16)
    leaving += start([(residual, residual_h), (normed_two, normed_h)], out_sem)
    finish(weights)
    expand = expand[...].reshape(-1, width)
    contract = contract[...].reshape(-1, width)
    for part in parts():
        branch[part], grad[part] = ffn_part(
            part, normed_two, cotangent, shifts, expand, contract, hidden, slope, shift_grad
        )
        leaving += start([(branch.at[part], branch_h.at[part]), (grad.at[part], grad_h.at[part])], out_sem)
    ffn_grads(normed_two, cotangent, hidden, slope, sent, kept)
    finish(leaving)


def second_kernel(plans, count, me, gain, shifts, residual_h, normed_h, branch_h, grad_h, cotangent_h, low_h, *refs):
    own, refs = refs[:count], refs[count:]
    output_h, back_h, rounded_h, gain_grad, sent, kept, shift_grad = refs[:7]
    targets, refs = refs[7:-18], refs[-18:]
    residual, normed_two, branch, grad, cotangent, low, expand, contract = refs[:8]
    output, back, rounded, hidden, slope, read_grad, in_sem, part_sem, low_sem, out_sem = refs[8:]
    unit = expand.shape[1]
    width = gain.shape[1]
    weights = start(
        [(normed_h, normed_two), (cotangent_h, cotangent)] + weight_copies(own, unit, expand, contract), in_sem
    )
    others = start([(residual_h, residual), (branch_h, branch), (grad_h, grad)], part_sem)
    last = start([(low_h, low)], low_sem)
    gain_grad[...] = jnp.zeros_like(gain_grad)
    shift_grad[...] = jnp.zeros_like(shift_grad)
    finish(weights)
    expand = expand[...].reshape(-1, width)
    contract = contract[...].reshape(-1, width)
    leaving = []
    for k, part in enumerate(parts()):
        one, two = ffn_part(part, normed_two, cotangent, shifts, expand, contract, hidden, slope, shift_grad)
        if k == 0:
            finish(others)
        value = residual[part]
        output[part] = (value + (branch[part] + one)).astype(bf16)
        total = grad[part] + two
        inverse = lax.rsqrt(jnp.mean(value * value, axis=-1, keepdims=True) + epsilon)
        unscaled = value * inverse
        gain_grad[...] += jnp.sum(total * unscaled, axis=0, keepdims=True)
        pulled = total * gain[...]
        mean = jnp.mean(pulled * unscaled, axis=-1, keepdims=True)
        value = cotangent[part].astype(f32) + inverse * (pulled - unscaled * mean)
        back[part] = value
        rounded[part] = value.astype(bf16)
        leaving += start(
            [(o.at[part], h.at[part]) for o, h in ((output, output_h), (back, back_h), (rounded, rounded_h))], out_sem
        )
    ffn_grads(normed_two, cotangent, hidden, slope, sent, kept)
    finish(last)
    read_grad[...] = across(low[...], rounded[...])
    emit(me[0], plans, read_grad, targets)
    finish(leaving)


def vmem(shape, dtype):
    return pltpu.VMEM(shape, dtype)


WHOLE = pl.BlockSpec(memory_space=pltpu.VMEM)


def ffn_first(me, gain, shifts, inputs, cotangent, low, readers, lists, size, skip, own, unit):
    blocks = sum(one.shape[0] for one in own)
    width = inputs.shape[1]
    units = blocks * unit
    kept = (max(1, blocks // 2), 2 * units // max(2, blocks), width)
    shape = jax.ShapeDtypeStruct
    return pl.pallas_call(
        partial(first_kernel, lists, size, skip),
        in_specs=[SCALAR, WHOLE, WHOLE] + [ANY] * (3 + len(readers) + len(own)),
        out_specs=[ANY] * 4 + [WHOLE] * 3,
        out_shape=[
            shape((LEN, width), f32),
            shape((LEN, width), bf16),
            shape((LEN, width), f32),
            shape((LEN, width), f32),
            shape(kept, bf16),
            shape(kept, f32),
            shape((1, units), f32),
        ],
        scratch_shapes=[
            vmem((LEN, width), bf16),
            vmem((LEN, width), bf16),
            vmem(low.shape, bf16),
            vmem((low.shape[1], width), bf16),
            vmem((blocks, unit, width), bf16),
            vmem((blocks, unit, width), bf16),
            vmem((LEN, width), f32),
            vmem((LEN, width), bf16),
            vmem((LEN, width), f32),
            vmem((LEN, width), f32),
            vmem((LEN, units), bf16),
            vmem((LEN, units), bf16),
        ]
        + [pltpu.SemaphoreType.DMA] * 3,
        compiler_params=PARAMS,
        cost_estimate=FILLER,
        name="ffn_first",
    )(me, gain, shifts, inputs, cotangent, low, *readers, *own)


def ffn_second(me, gain, shifts, residual, normed_two, branch, grad, cotangent, low, own, unit, size, plans):
    blocks = sum(one.shape[0] for one in own)
    width = cotangent.shape[1]
    units = blocks * unit
    kept = (max(1, blocks // 2), 2 * units // max(2, blocks), width)
    targets = emitted(plans, low.shape[1], size, width)
    shape = jax.ShapeDtypeStruct
    return pl.pallas_call(
        partial(second_kernel, plans, len(own)),
        in_specs=[SCALAR, WHOLE, WHOLE] + [ANY] * (6 + len(own)),
        out_specs=[ANY] * 3 + [WHOLE] * (4 + len(targets)),
        out_shape=[
            shape((LEN, width), bf16),
            shape((LEN, width), f32),
            shape((LEN, width), bf16),
            shape((1, width), f32),
            shape(kept, bf16),
            shape(kept, f32),
            shape((1, units), f32),
        ]
        + targets,
        scratch_shapes=[
            vmem((LEN, width), f32),
            vmem((LEN, width), bf16),
            vmem((LEN, width), f32),
            vmem((LEN, width), f32),
            vmem((LEN, width), bf16),
            vmem(low.shape, bf16),
            vmem((blocks, unit, width), bf16),
            vmem((blocks, unit, width), bf16),
            vmem((LEN, width), bf16),
            vmem((LEN, width), f32),
            vmem((LEN, width), bf16),
            vmem((LEN, units), bf16),
            vmem((LEN, units), bf16),
            vmem((low.shape[1], width), f32),
        ]
        + [pltpu.SemaphoreType.DMA] * 4,
        compiler_params=PARAMS,
        cost_estimate=FILLER,
        name="ffn_second",
    )(me, gain, shifts, residual, normed_two, branch, grad, cotangent, low, *own)


def back_kernel(lists, size, skip, plans, me, rounded, normed, share, pull_f, pull_i, *refs):
    readers = refs[: len(lists)]
    grads, offset_grad = refs[len(lists) : len(lists) + 2]
    targets = refs[len(lists) + 2 : -6]
    gate_grad, readout, pulled, drive, decay, sem = refs[-6:]
    group = pl.program_id(0)
    wide = share.shape[1]
    hidden = readout.shape[0]

    @pl.when(group == 0)
    def _():
        finish(start(placed(me[0], lists, readers, skip, size, readout), sem))

    reader = readout[pl.ds(pl.multiple_of(group * wide, wide), wide)]
    held = jnp.zeros((LANES, wide), f32)
    prod = jnp.ones((LANES, wide), f32)
    for part in reversed(parts()):
        pulled[part] = against(rounded[part], reader)
        for k in reversed(range(part.start // LANES, part.stop // LANES)):
            if k < STEPS - 1:
                after = 1.0 - share[tiles(k + 1, 1)]
                prod = after * prod
                held = pulled[tiles(k, 1)] + after * held
            else:
                held = pulled[tiles(k, 1)]
            drive[tiles(k, 1)] = held
            decay[tiles(k, 1)] = prod
    first_retain = 1.0 - share[pl.ds(0, LANES)]
    ends = [jnp.zeros((1, wide), f32)]
    for k in range(LANES - 1, 0, -1):
        whole = held[k : k + 1] + prod[k : k + 1] * ends[-1]
        ends.append(first_retain[k : k + 1] * whole)
    entering = jnp.concatenate(ends[::-1], axis=0)
    entering = jnp.concatenate([entering, entering], axis=0)

    def more(k, sums):
        rows = tiles(2 * k, 2)
        carried = drive[rows] + decay[rows] * entering
        found = []
        for t, factor in enumerate((pull_f, pull_i, share)):
            value = (carried * factor[rows].astype(f32)).astype(bf16)
            grads[t, rows] = value
            found.append(sums[t] + value.astype(f32))
        return tuple(found)

    sums = (jnp.zeros((2 * LANES, wide), f32),) * 3
    for k in range(STEPS // 2):
        sums = more(k, sums)
    for t in range(3):
        offset_grad[t : t + 1] = jnp.sum(sums[t], axis=0, keepdims=True)
        rows = pl.ds(pl.multiple_of(t * hidden + group * wide, wide), wide)
        gate_grad[rows] = across(grads[t], normed[...])

    @pl.when(group == hidden // wide - 1)
    def _():
        emit(me[0], plans, gate_grad, targets)


def back(me, rounded, normed, share, pull_f, pull_i, readers, lists, size, skip, plans):
    width = normed.shape[1]
    hidden = share.shape[1]
    wide = 256
    fixed = lambda g: (0, 0)
    tall = lambda g: (0, g)
    shape = jax.ShapeDtypeStruct
    firm = pl.BlockSpec((LEN, width), fixed)
    targets = emitted(plans, 3 * hidden, 3 * size, width)
    return pl.pallas_call(
        partial(back_kernel, lists, size, skip, plans),
        grid=(hidden // wide,),
        in_specs=[SCALAR, firm, firm] + [pl.BlockSpec((LEN, wide), tall)] * 3 + [ANY] * len(readers),
        out_specs=[pl.BlockSpec((3, LEN, wide), lambda g: (0, 0, g)), pl.BlockSpec((3, wide), tall)]
        + [pl.BlockSpec(one.shape, lambda g, rank=len(one.shape): (0,) * rank) for one in targets],
        out_shape=[shape((3, LEN, hidden), bf16), shape((3, hidden), f32)] + targets,
        scratch_shapes=[
            vmem((3 * hidden, width), f32),
            vmem((hidden, width), bf16),
            vmem((LEN, wide), f32),
            vmem((LEN, wide), f32),
            vmem((LEN, wide), f32),
            pltpu.SemaphoreType.DMA,
        ],
        compiler_params=PARAMS,
        cost_estimate=FILLER,
        name="back",
    )(me, rounded, normed, share, pull_f, pull_i, *readers)


def inputs_kernel(lists, size, me, inputs, gain, back, grads_h, *refs):
    arrays = refs[: len(lists)]
    output, gain_grad, grads, weights, weight_sem, sem = refs[len(lists) :]
    arriving = start(placed(me[0], lists, arrays, 0, size, weights), weight_sem)
    hidden = weights.shape[0] // 3
    for part in parts():
        arriving += start([(grads_h.at[t, part], grads.at[t, part]) for t in range(3)], sem)
    gain_grad[...] = jnp.zeros_like(gain_grad)
    finish(arriving)
    for part in parts():
        total = matmul(grads[0, part], weights[:hidden])
        for t in range(1, 3):
            total = total + matmul(grads[t, part], weights[t * hidden : (t + 1) * hidden])
        value = inputs[part].astype(f32)
        inverse = lax.rsqrt(jnp.mean(value * value, axis=-1, keepdims=True) + epsilon)
        unscaled = value * inverse
        gain_grad[...] += jnp.sum(total * unscaled, axis=0, keepdims=True)
        pulled = total * gain[...]
        mean = jnp.mean(pulled * unscaled, axis=-1, keepdims=True)
        output[part] = back[part] + inverse * (pulled - unscaled * mean)


def inputs_back(me, inputs, gain, back_grad, grads, arrays, lists, size):
    width = inputs.shape[1]
    hidden = grads.shape[2]
    return pl.pallas_call(
        partial(inputs_kernel, lists, size),
        in_specs=[SCALAR, WHOLE, WHOLE, WHOLE, ANY] + [ANY] * len(arrays),
        out_specs=[WHOLE, WHOLE],
        out_shape=[jax.ShapeDtypeStruct((LEN, width), f32), jax.ShapeDtypeStruct((1, width), f32)],
        scratch_shapes=[
            vmem((3, LEN, hidden), bf16),
            vmem((3 * hidden, width), bf16),
            pltpu.SemaphoreType.DMA,
            pltpu.SemaphoreType.DMA,
        ],
        compiler_params=PARAMS,
        cost_estimate=FILLER,
        name="inputs_back",
    )(me, inputs, gain, back_grad, grads, *arrays)


class Wires:
    def __init__(self, mesh):
        self.inner = mesh.shape["fsdp"]
        self.count = mesh.shape["dp"] * self.inner
        rest = [1 << b for b in range(1, self.inner.bit_length() - 1)]
        self.digits = [rest[i : i + 2] for i in range(0, len(rest), 2)]
        self.core, self.x, self.y = self.inner, 2 * self.inner, 1
        self.bits = {"A": [self.y, self.x, self.core], "B": [self.x, self.y, self.core]}

    def swap(self, value, mask):
        return lax.ppermute(value, AXES, [(i, i ^ mask) for i in range(self.count)])

    def spread(self, digit):
        return [sum(bit for j, bit in enumerate(digit) if k >> j & 1) for k in range(1 << len(digit))]

    def masks(self, order):
        found = [0]
        for digit in self.digits:
            found = [m ^ s for s in self.spread(digit) for m in found]
        lists = [found]
        for bit in self.bits[order]:
            lists = lists + [[m ^ bit for m in one] for one in lists]
        return lists

    def line(self, held, digits, tie=None):
        for digit in digits:
            came = [self.swap(held, m) for m in self.spread(digit)[1:]]
            if tie:
                _, *came = tie(*came)
            held = jnp.concatenate([held] + came)
        return held

    def line_start(self, held):
        for digit in reversed(self.digits[1:]):
            held = self.line_end(*self.line_step(held, digit))
        return self.line_step(held, self.digits[0])

    def line_step(self, held, digit):
        masks = self.spread(digit)
        blocks = jnp.split(held, len(masks))
        return blocks[0], [self.swap(one.astype(bf16), m) for one, m in zip(blocks[1:], masks[1:])]

    def line_end(self, held, came):
        for other in came:
            held = held + other.astype(f32)
        return held


def tied(*values):
    return lax.optimization_barrier(values)


def solution(mesh):
    wires = Wires(mesh)
    count = wires.count
    masks = {order: wires.masks(order) for order in "AB"}
    flat = {order: sum(masks[order], []) for order in "AB"}

    def shards(tokens, gating, offsets, prescale, readout, midscale, expand, shifts, contract, cotangent):
        swap = wires.swap
        index = lax.axis_index("dp") * wires.inner + lax.axis_index("fsdp")
        unit = readout.shape[0]
        wide = expand.shape[1]
        thin = prescale.shape[0]
        width = tokens.shape[1]
        hidden = count * unit
        assert tokens.shape[0] == LEN
        me = index.astype(jnp.int32).reshape(1)

        rest = jnp.concatenate([expand.T, contract])[None]
        row = jnp.concatenate([jnp.pad(one, (0, 128 - one.shape[0])) for one in (offsets, shifts, prescale, midscale)])
        taken = 4 * unit
        part = jnp.pad(jnp.concatenate([gating.T, readout, row[None]]), ((0, LANES - 1), (0, 0)))
        inputs = interleaved(tokens)
        gate_line = wires.line(part[None], wires.digits, lambda *came: tied(inputs, *came))
        gate_line, rest, cotangent = tied(gate_line, rest, cotangent)
        nz = gate_line.shape[0]
        cut = nz // 2
        gate_x = swap(gate_line, wires.x)
        gate_y = swap(gate_line, wires.y)
        rest_early = [swap(rest, m) for m in wires.spread(wires.digits[0])[1:]]
        upstream = interleaved(cotangent)
        gate_x, upstream, rest_early[1], rest_early[2] = tied(gate_x, upstream, rest_early[1], rest_early[2])
        gate_y, rest_early[0] = tied(gate_y, rest_early[0])
        gate_list = [gate_line, gate_x, gate_y, swap(gate_x[:cut], wires.y), swap(gate_y[cut:], wires.x)]
        gate_list += [swap(one, wires.core) for one in gate_list]
        rest_line = wires.line(jnp.concatenate([rest, *rest_early]), wires.digits[1:])
        rest_x = swap(rest_line, wires.x)
        rest_y = swap(rest_line, wires.y)
        rest_core = swap(rest_line, wires.core)

        quads = masks["A"]
        gate_lists = [quads[0], quads[2], quads[1], quads[3][:cut], quads[3][cut:]]
        gate_lists += [[m ^ wires.core for m in one] for one in gate_lists]
        row_arrays = gate_list
        sizes = (3 * unit, wide, thin)
        owner_masks = jnp.asarray(np.array(sum(gate_lists, []), np.int32)[:, None])
        ffn_masks = np.concatenate([masks["A"][k] for k in (0, 1, 4, 5, 2, 3, 6, 7)])
        lane_masks = jnp.asarray(np.repeat(ffn_masks, wide).astype(np.int32)[None])

        if unit % 16:
            places = np.argsort(np.asarray(sum(gate_lists, [])))
            whole = jnp.take(jnp.concatenate(gate_list), jnp.asarray(places)[index ^ jnp.arange(count)], axis=0)
            gate_list = [
                jnp.concatenate([whole[:, : 3 * unit].reshape(-1, width), whole[:, 3 * unit : taken].reshape(-1, width)])[None]
            ]
            row_arrays = [jnp.concatenate([one[:, taken : taken + LANES] for one in row_arrays])]
            gate_lists, gate_size, read_size, zero = [[0]], 3 * hidden, hidden, jnp.zeros_like(me)
            ffn_unit = 4 * nz * wide
        else:
            gate_size, read_size, zero = 3 * unit, unit, me
            ffn_unit = wide

        both = jnp.concatenate([zero, me])
        normed, share, low, pull_f, pull_i, gain_one, gain_two, all_shifts = gates(
            both, inputs, row_arrays, 0 if unit % 16 else taken, owner_masks, lane_masks, gate_list, gate_lists, gate_size, sizes, hidden
        )
        shift_halves = jnp.split(all_shifts, 2, axis=1)
        low, rest_y, rest_x, rest_core = tied(low, rest_y, rest_x, rest_core)
        rest_corner = [swap(rest_x[:cut], wires.y), swap(rest_y[cut:], wires.x)]

        def merged(group):
            if not unit % 16:
                return group
            halves = [jnp.concatenate([one[:, at : at + wide].reshape(-1, width) for one in group]) for at in (0, wide)]
            return [jnp.concatenate(halves)[None]]

        own = merged([rest_line, rest_y, rest_core, swap(rest_y, wires.core)])

        def apart(grads):
            if not unit % 16:
                return grads
            return grads.reshape(2, -1, wide, width).transpose(1, 0, 2, 3).reshape(-1, 2 * wide, width)

        residual, normed_two, branch, grad, sent_0, kept_0, shift_0 = ffn_first(
            zero, gain_two, shift_halves[0], inputs, upstream, low, gate_list, gate_lists, read_size, gate_size, own,
            ffn_unit,
        )
        residual, normed_two, branch, grad, sent_0, kept_0, shift_0, rest_x, *rest_corner = tied(
            residual, normed_two, branch, grad, sent_0, kept_0, shift_0, rest_x, *rest_corner
        )
        far = [rest_x, *rest_corner]
        own = merged(far + [swap(one, wires.core) for one in far])
        near_core = swap(apart(sent_0), wires.core)
        half = count // 2
        read_plans = [(flat["A"][:half], f32), (flat["A"][half:], bf16)]
        output, residual_grad, rounded, midscale_grad, sent_1, kept_1, shift_1, *read_blocks = ffn_second(
            zero, gain_two, shift_halves[1], residual, normed_two, branch, grad, upstream, low, own, ffn_unit, unit,
            None if unit % 16 else read_plans,
        )
        read_kept, read_sent = sorted_blocks(index, read_plans, read_blocks, unit) if unit % 16 else read_blocks

        output, residual_grad, rounded, midscale_grad, sent_1, kept_1, shift_1, read_kept, read_sent, near_core = tied(
            output, residual_grad, rounded, midscale_grad, sent_1, kept_1, shift_1, read_kept, read_sent, near_core
        )
        far_core = swap(apart(sent_1), wires.core)
        read_core = swap(read_sent, wires.core)
        ffn_terms = [(apart(kept_0), near_core), (apart(kept_1), far_core)]

        def quad(k, low, high):
            kept, came = ffn_terms[k // 2]
            base = k % 2 * nz
            ffn = kept[base + low : base + high] + came[base + low : base + high].astype(f32)
            base = k * nz
            read = read_kept[base + low : base + high] + read_core[base + low : base + high].astype(f32)
            return jnp.concatenate([ffn, read], axis=1)

        send_x = jnp.concatenate([quad(3, cut, nz), quad(2, cut, nz)]).astype(bf16)
        send_y = jnp.concatenate([quad(3, 0, cut), quad(1, 0, cut)]).astype(bf16)
        rounded, send_x, send_y = tied(rounded, send_x, send_y)
        rest_x, rest_y = swap(send_x, wires.x), swap(send_y, wires.y)
        places = [quads[3][cut:] + quads[2][cut:] + quads[3][:cut] + quads[1][:cut]]
        places.append(quads[2][:cut] + quads[1][cut:] + quads[0])
        away = [[m ^ wires.core for m in one] for one in places]
        gate_plans = [(places[0], f32), (places[1], f32), (away[0], bf16), (away[1], bf16)]
        gate_grads, off_grad, *gate_blocks = back(
            zero, rounded, normed, share, pull_f, pull_i, gate_list, gate_lists, read_size, gate_size,
            None if unit % 16 else gate_plans,
        )
        if unit % 16:
            gate_blocks = sorted_blocks(index, gate_plans, gate_blocks, 3 * unit)
        first_kept, second_kept, first_sent, second_sent, gate_grads, off_grad, rest_x, rest_y = tied(
            *gate_blocks, gate_grads, off_grad, rest_x, rest_y
        )
        first_core = swap(first_sent, wires.core)
        second_core = swap(second_sent, wires.core)
        first = (first_kept + first_core.astype(f32)).astype(bf16)
        send_x = (quad(2, 0, cut) + rest_y[:cut].astype(f32)).astype(bf16)
        send_y = (quad(1, cut, nz) + rest_x[:cut].astype(f32)).astype(bf16)
        gate_grads, first, send_x, send_y, output, midscale_grad, off_grad, shift_0, shift_1 = tied(
            gate_grads, first, send_x, send_y, output, midscale_grad, off_grad, shift_0, shift_1
        )
        gate_x, gate_y = swap(first[:nz], wires.x), swap(first[nz:], wires.y)
        rest_xx, rest_yy = swap(send_x, wires.x), swap(send_y, wires.y)
        tokens_grad, prescale_grad = inputs_back(
            zero, inputs, gain_one, residual_grad, gate_grads, gate_list, gate_lists, gate_size
        )
        tokens_grad, prescale_grad, gate_x, gate_y, rest_xx, rest_yy = tied(
            tokens_grad, prescale_grad, gate_x, gate_y, rest_xx, rest_yy
        )

        def second(low, high):
            return second_kept[low:high] + second_core[low:high].astype(f32)

        send_x = (second(0, cut) + gate_y[:cut].astype(f32)).astype(bf16)
        send_y = (second(cut, nz) + gate_x[:cut].astype(f32)).astype(bf16)
        send_x, send_y, rest_xx, rest_yy = tied(send_x, send_y, rest_xx, rest_yy)
        gate_xx, gate_yy = swap(send_x, wires.x), swap(send_y, wires.y)

        def met(x_way, y_way, xx_way, yy_way):
            low_half = y_way[cut:].astype(f32) + xx_way.astype(f32)
            return jnp.concatenate([low_half, x_way[cut:].astype(f32) + yy_way.astype(f32)])

        rest_part = quad(0, 0, nz) + met(rest_x, rest_y, rest_xx, rest_yy)
        rest_part, output, prescale_grad = tied(rest_part, output, prescale_grad)
        rest_kept, rest_came = wires.line_start(rest_part)
        vectors = vector_rows(
            me, lane_masks, sizes, count, off_grad, shift_0, shift_1, prescale_grad, midscale_grad
        )
        gate_xx, gate_yy, vectors = tied(gate_xx, gate_yy, vectors)
        gate_part = second(nz, 2 * nz) + met(gate_x, gate_y, gate_xx, gate_yy)
        gate_part, tokens_grad, vectors, output = tied(gate_part, tokens_grad, vectors, output)
        gate_kept, gate_came = wires.line_start(gate_part)
        vectors = lax.all_to_all(vectors, AXES, 0, 0, tiled=True)
        tokens_grad = sequential(tokens_grad, FILLER)
        tokens_grad, output = tied(tokens_grad, output)
        block_output = sequential(output, QUICK)
        tokens_grad, block_output, vectors, gate_came, rest_came = tied(
            tokens_grad, block_output, vectors, gate_came, rest_came
        )
        vectors = jnp.sum(vectors, axis=0)
        vector_parts = [vectors[at : at + size] for at, size in zip(range(0, 512, 128), (*sizes, thin))]
        tokens_grad, vector_parts, block_output, rest_kept, rest_came, gate_kept, gate_came = tied(
            tokens_grad, vector_parts, block_output, rest_kept, rest_came, gate_kept, gate_came
        )
        rest_part = wires.line_end(rest_kept, rest_came)[0]
        gate_part = wires.line_end(gate_kept, gate_came)[0]
        offsets_part, shifts_part, prescale_part, midscale_part = vector_parts
        return (
            block_output,
            tokens_grad,
            gate_part.T,
            offsets_part,
            prescale_part,
            rest_part[2 * wide :],
            midscale_part,
            rest_part[:wide].T,
            shifts_part,
            rest_part[wide : 2 * wide],
        )

    rows = P(AXES, None)
    columns = P(None, AXES)
    line = P(AXES)
    in_specs = (rows, columns, line, line, rows, line, columns, line, rows, rows)
    out_specs = (rows, rows, columns, line, line, rows, line, columns, line, rows)
    return jax.shard_map(shards, mesh=mesh, in_specs=in_specs, out_specs=out_specs, check_vma=False)
```

```python
from functools import partial

import jax
import jax.numpy as jnp
import numpy as np
from jax import lax
from jax.experimental import pallas as pl
from jax.experimental.pallas import tpu as pltpu
from jax.sharding import PartitionSpec as P

LEN = 1024
LANES = 8
STEPS = LEN // LANES
ROWS = 256
AXES = ("dp", "fsdp")
epsilon = 1e-06
bf16 = jnp.bfloat16
f32 = jnp.float32
ANY = pl.BlockSpec(memory_space=pl.ANY)
SCALAR = pl.BlockSpec(memory_space=pltpu.SMEM)
FILLER = pl.CostEstimate(flops=10**11, bytes_accessed=10**8, transcendentals=0)
QUICK = pl.CostEstimate(flops=1000, bytes_accessed=1000, transcendentals=0)
PARAMS = pltpu.CompilerParams(vmem_limit_bytes=56 * 1024 * 1024)


def matmul(left, right):
    return jnp.dot(left, right, preferred_element_type=f32)


def across(left, right):
    return lax.dot_general(left, right, (((0,), (0,)), ((), ())), preferred_element_type=f32)


def against(left, right):
    return lax.dot_general(left, right, (((1,), (1,)), ((), ())), preferred_element_type=f32)


def interleave_kernel(values, target, scratch):
    for j in range(scratch.shape[0]):
        columns = slice(j * 128, (j + 1) * 128)
        for run in range(LANES):
            rows = slice(run * STEPS, (run + 1) * STEPS)
            scratch[j, pl.ds(run, STEPS, stride=LANES)] = values[rows, columns].astype(f32)
        target[:, columns] = scratch[j].astype(target.dtype)


def interleaved(values):
    return pl.pallas_call(
        interleave_kernel,
        out_shape=jax.ShapeDtypeStruct(values.shape, values.dtype),
        scratch_shapes=[pltpu.VMEM((values.shape[1] // 128, LEN, 128), f32)],
        compiler_params=PARAMS,
        cost_estimate=QUICK,
        name="interleave",
    )(values)


def sequence_kernel(values, target, scratch):
    for j in range(scratch.shape[0]):
        columns = slice(j * 128, (j + 1) * 128)
        scratch[j] = values[:, columns].astype(f32)
        for run in range(LANES):
            rows = slice(run * STEPS, (run + 1) * STEPS)
            target[rows, columns] = scratch[j, pl.ds(run, STEPS, stride=LANES)].astype(target.dtype)


def sequential(values, cost):
    return pl.pallas_call(
        sequence_kernel,
        out_shape=jax.ShapeDtypeStruct(values.shape, values.dtype),
        scratch_shapes=[pltpu.VMEM((values.shape[1] // 128, LEN, 128), f32)],
        compiler_params=PARAMS,
        cost_estimate=cost,
        name="sequence",
    )(values)


def down(values):
    return jnp.concatenate([jnp.zeros_like(values[:1]), values[:-1]], axis=0)


def tiles(k, count):
    if isinstance(k, int):
        return pl.ds(k * LANES, count * LANES)
    return pl.ds(pl.multiple_of(k * LANES, LANES), count * LANES)


def parts():
    return [slice(k, k + ROWS) for k in range(0, LEN, ROWS)]


def start(pairs, sem):
    copies = [pltpu.make_async_copy(source, target, sem) for source, target in pairs]
    for copy in copies:
        copy.start()
    return copies


def finish(copies):
    for copy in copies:
        copy.wait()


def placed(me, lists, arrays, first, size, target):
    found = []
    for masks, array in zip(lists, arrays):
        for b, mask in enumerate(masks):
            at = pl.multiple_of((me ^ mask) * size, size)
            found.append((array.at[b, pl.ds(first, size)], target.at[pl.ds(at, size)]))
    return found


def emitted(plans, rows, size, width):
    if plans is None:
        return [jax.ShapeDtypeStruct((rows, width), f32)]
    return [jax.ShapeDtypeStruct((len(masks), size, width), dtype) for masks, dtype in plans]


def emit(me, plans, source, targets):
    if plans is None:
        targets[0][...] = source[...]
        return
    for (masks, _), target in zip(plans, targets):
        size = target.shape[1]
        for p, mask in enumerate(masks):
            at = pl.multiple_of((me ^ mask) * size, size)
            target[p] = source[pl.ds(at, size)].astype(target.dtype)


def sorted_blocks(me, plans, grads, size):
    whole = grads[0].reshape(-1, size, grads[0].shape[1])
    return [jnp.take(whole, me ^ jnp.asarray(masks), axis=0).astype(dtype) for masks, dtype in plans]


def lanes_of(count, size):
    lane = lax.broadcasted_iota(jnp.int32, (1, count), 1)
    piece = ((lane.astype(f32) + 0.5) * (1.0 / size)).astype(jnp.int32)
    return piece, lane - piece * size


def selector(place):
    rows = lax.broadcasted_iota(jnp.int32, (128, place.shape[1]), 0)
    return jnp.where(rows == place, 1.0, 0.0).astype(bf16)


def laid_out(rows, owners, lane_owner, place):
    spread = matmul(rows, selector(place))
    return jnp.sum(jnp.where(owners == lane_owner, spread, 0.0), axis=0, keepdims=True)


def cut_up(vector, lane_owner, place, count):
    rows = lax.broadcasted_iota(jnp.int32, (count, vector.shape[1]), 0)
    found = jnp.where(rows == lane_owner, vector, 0.0)
    high = found.astype(bf16)
    low = (found - high.astype(f32)).astype(bf16)
    choose = selector(place)
    return against(high, choose) + against(low, choose)


def vectors_kernel(sizes, me, masks, offsets, shift_0, shift_1, prescale, midscale, target):
    count = target.shape[0]
    flat = jnp.concatenate([offsets[t : t + 1] for t in range(3)], axis=1)
    target[:, :128] = cut_up(flat, *lanes_of(flat.shape[1], sizes[0]), count)
    shifts = jnp.concatenate([shift_0[...], shift_1[...]], axis=1)
    target[:, 128:256] = cut_up(shifts, masks[...] ^ me[0], lanes_of(shifts.shape[1], sizes[1])[1], count)
    target[:, 256:384] = cut_up(prescale[...], *lanes_of(prescale.shape[1], sizes[2]), count)
    target[:, 384:512] = cut_up(midscale[...], *lanes_of(midscale.shape[1], sizes[2]), count)


def vector_rows(me, masks, sizes, count, *grads):
    return pl.pallas_call(
        partial(vectors_kernel, sizes),
        in_specs=[SCALAR] + [pl.BlockSpec(memory_space=pltpu.VMEM)] * 6,
        out_specs=pl.BlockSpec(memory_space=pltpu.VMEM),
        out_shape=jax.ShapeDtypeStruct((count, 512), f32),
        compiler_params=PARAMS,
        cost_estimate=FILLER,
        name="vectors",
    )(me, masks, *grads)


def gates_kernel(lists, size, taken, row_count, sizes, me, inputs, owner_masks, lane_masks, *refs):
    row_arrays, refs = refs[:row_count], refs[row_count:]
    arrays = refs[: len(lists)]
    normed, share, low, pull_f, pull_i, gain_one, gain_two, shifts = refs[len(lists) : len(lists) + 8]
    weights, pre, mid, decay, drive, offsets, small, sem, small_sem = refs[len(lists) + 8 :]
    group = pl.program_id(0)
    wide = share.shape[1]
    hidden = weights.shape[0] // 3

    @pl.when(group == 0)
    def _():
        copies = start(placed(me[0], lists, arrays, 0, size, weights), sem)
        found, at = [], 0
        for array in row_arrays:
            found.append((array.at[:, pl.ds(taken, LANES)], small.at[pl.ds(at, array.shape[0])]))
            at += array.shape[0]
        finish(start(found, small_sem))
        rows = jnp.sum(small[...].astype(f32), axis=1).astype(bf16)
        owners = owner_masks[...] ^ me[1]
        width = inputs.shape[1]
        gain = laid_out(rows[:, 256:384], owners, *lanes_of(width, sizes[2]))
        gain_one[...] = gain
        gain_two[...] = laid_out(rows[:, 384:512], owners, *lanes_of(width, sizes[2]))
        place = lanes_of(shifts.shape[1], sizes[1])[1]
        shifts[...] = laid_out(rows[:, 128:256], owners, lane_masks[...] ^ me[1], place)
        flat = laid_out(rows[:, :128], owners, *lanes_of(3 * hidden, sizes[0]))
        for t in range(3):
            for k in range(hidden // wide):
                offsets[k, t : t + 1] = flat[:, t * hidden + k * wide : t * hidden + (k + 1) * wide]
        for part in parts():
            value = inputs[part].astype(f32)
            scale = lax.rsqrt(jnp.mean(value * value, axis=-1, keepdims=True) + epsilon)
            normed[part] = (value * scale * gain).astype(bf16)
        finish(copies)

    def step(k, carry):
        prod, held = carry
        rows = tiles(2 * k, 2)
        forget = 1.0 / (1.0 + jnp.exp(-pre[0, rows]))
        entry = 1.0 / (1.0 + jnp.exp(-pre[1, rows]))
        whole = 1.0 / (forget + entry)
        keep = forget * whole
        rest = entry * whole
        flow = rest * pre[2, rows]
        both = keep * rest
        share[rows] = rest
        mid[0, rows] = both * (1.0 - forget)
        mid[1, rows] = both * (entry - 1.0)
        held_0 = keep[:LANES] * held + flow[:LANES]
        prod_0 = keep[:LANES] * prod
        held = keep[LANES:] * held_0 + flow[LANES:]
        prod = keep[LANES:] * prod_0
        drive[rows] = jnp.concatenate([held_0, held], axis=0)
        decay[rows] = jnp.concatenate([prod_0, prod], axis=0)
        return prod, held

    begin = (jnp.ones((LANES, wide), f32), jnp.zeros((LANES, wide), f32))
    prod, held = begin
    ws = [weights[pl.ds(pl.multiple_of(t * hidden + group * wide, wide), wide)] for t in range(3)]
    for part in parts():
        for t in range(3):
            pre[t, part] = against(normed[part], ws[t]) + offsets[group, t : t + 1]
        for k in range(part.start // (2 * LANES), part.stop // (2 * LANES)):
            prod, held = step(k, (prod, held))
    ends = [jnp.zeros((1, wide), f32)]
    for k in range(LANES - 1):
        ends.append(prod[k : k + 1] * ends[-1] + held[k : k + 1])
    entering = jnp.concatenate(ends, axis=0)
    entering = jnp.concatenate([entering, entering], axis=0)

    def join(k, before):
        rows = tiles(2 * k, 2)
        value = drive[rows] + decay[rows] * entering
        low[rows] = value.astype(bf16)
        change = jnp.concatenate([before, value[:LANES]], axis=0) - pre[2, rows]
        pull_f[rows] = (change * mid[0, rows]).astype(bf16)
        pull_i[rows] = (change * mid[1, rows]).astype(bf16)
        return value[LANES:]

    lax.fori_loop(0, STEPS // 2, join, entering[:LANES], unroll=8)


def gates(me, inputs, row_arrays, taken, owner_masks, lane_masks, arrays, lists, size, sizes, hidden):
    width = inputs.shape[1]
    shape = jax.ShapeDtypeStruct
    whole = lambda one: pl.BlockSpec(one.shape, lambda g: (0, 0))
    wide = 256
    fixed = lambda g: (0, 0)
    tall = lambda g: (0, g)
    out = lambda dtype: jax.ShapeDtypeStruct((LEN, hidden), dtype)
    solid = pl.BlockSpec((LEN, width), fixed)
    return pl.pallas_call(
        partial(gates_kernel, lists, size, taken, len(row_arrays), sizes),
        grid=(hidden // wide,),
        in_specs=[SCALAR, solid, whole(owner_masks), whole(lane_masks)] + [ANY] * (len(row_arrays) + len(arrays)),
        out_specs=[solid]
        + [pl.BlockSpec((LEN, wide), tall)] * 4
        + [pl.BlockSpec((1, width), fixed)] * 2
        + [whole(lane_masks)],
        out_shape=[jax.ShapeDtypeStruct((LEN, width), bf16)]
        + [out(f32), out(bf16), out(bf16), out(bf16), shape((1, width), f32)]
        + [shape((1, width), f32), shape(lane_masks.shape, f32)],
        scratch_shapes=[
            pltpu.VMEM((3 * hidden, width), bf16),
            pltpu.VMEM((3, LEN, wide), f32),
            pltpu.VMEM((2, LEN, wide), f32),
            pltpu.VMEM((LEN, wide), f32),
            pltpu.VMEM((LEN, wide), f32),
            pltpu.VMEM((hidden // wide, 3, wide), f32),
            pltpu.VMEM((owner_masks.shape[0], LANES, width), bf16),
            pltpu.SemaphoreType.DMA,
            pltpu.SemaphoreType.DMA,
        ],
        compiler_params=PARAMS,
        cost_estimate=FILLER,
        name="gates",
    )(me, inputs, owner_masks, lane_masks, *row_arrays, *arrays)


def gelu_both(x):
    inner = np.float32(np.sqrt(2 / np.pi))
    square = x * x
    t = jnp.tanh(inner * (x + np.float32(0.044715) * (square * x)))
    cdf = 0.5 + 0.5 * t
    slope = cdf + (0.5 * x) * (1.0 - t * t) * (inner + np.float32(3 * 0.044715) * inner * square)
    return x * cdf, slope


def ffn_part(part, normed_two, cotangent, shifts, base, expand, contract, hidden, slope, shift_grad):
    units = expand.shape[0]
    n2 = normed_two[part]
    ct = cotangent[part]
    for j in range(0, units, 256):
        cols = slice(j, j + 256)
        act, grad = gelu_both(against(n2, expand[cols]) + shifts[:, base + j : base + j + 256])
        hidden[part, cols] = act.astype(bf16)
        rounded = (against(ct, contract[cols]) * grad).astype(bf16)
        slope[part, cols] = rounded
        shift_grad[:, cols] += jnp.sum(rounded.astype(f32), axis=0, keepdims=True)
    return matmul(hidden[part], contract[...]), matmul(slope[part], expand[...])


def ffn_grads(normed_two, cotangent, hidden, slope, sent, kept):
    units = hidden.shape[1]
    blocks, rows, width = kept.shape
    unit = rows // 2
    for j, target in enumerate((kept, sent)):
        cols = slice(j * units // 2, (j + 1) * units // 2)
        target[:, :unit] = across(slope[:, cols], normed_two[...]).astype(target.dtype).reshape(blocks, unit, width)
        target[:, unit:] = across(hidden[:, cols], cotangent[...]).astype(target.dtype).reshape(blocks, unit, width)


def weight_copies(own, unit, expand, contract):
    found, at = [], 0
    for one in own:
        count = one.shape[0]
        found.append((one.at[:, pl.ds(0, unit)], expand.at[pl.ds(at, count)]))
        found.append((one.at[:, pl.ds(unit, unit)], contract.at[pl.ds(at, count)]))
        at += count
    return found


def first_kernel(lists, size, skip, me, gain, shifts, inputs_h, cotangent_h, low_h, *refs):
    readers, own, refs = refs[: len(lists)], refs[len(lists) : -22], refs[-22:]
    (residual_h, normed_h, branch_h, grad_h, sent, kept, shift_grad) = refs[:7]
    (inputs, cotangent, low, readout, expand, contract, residual, normed_two, branch, grad, hidden, slope) = refs[7:19]
    in_sem, weight_sem, out_sem = refs[19:]
    unit = expand.shape[1]
    width = gain.shape[1]
    arriving = start(
        [(inputs_h, inputs), (low_h, low)] + placed(me[0], lists, readers, skip, size, readout), in_sem
    )
    weights = start(weight_copies(own, unit, expand, contract) + [(cotangent_h, cotangent)], weight_sem)
    shift_grad[...] = jnp.zeros_like(shift_grad)
    finish(arriving)
    leaving = []
    for part in parts():
        value = inputs[part].astype(f32) + matmul(low[part], readout[...])
        residual[part] = value
        inverse = lax.rsqrt(jnp.mean(value * value, axis=-1, keepdims=True) + epsilon)
        normed_two[part] = (value * inverse * gain[...]).astype(bf16)
    leaving += start([(residual, residual_h), (normed_two, normed_h)], out_sem)
    finish(weights)
    expand = expand[...].reshape(-1, width)
    contract = contract[...].reshape(-1, width)
    for part in parts():
        branch[part], grad[part] = ffn_part(
            part, normed_two, cotangent, shifts, 0, expand, contract, hidden, slope, shift_grad
        )
        leaving += start([(branch.at[part], branch_h.at[part]), (grad.at[part], grad_h.at[part])], out_sem)
    ffn_grads(normed_two, cotangent, hidden, slope, sent, kept)
    finish(leaving)


def second_kernel(plans, count, me, gain, shifts, residual_h, normed_h, branch_h, grad_h, cotangent_h, low_h, *refs):
    own, refs = refs[:count], refs[count:]
    output_h, back_h, rounded_h, gain_grad, sent, kept, shift_grad = refs[:7]
    targets, refs = refs[7:-18], refs[-18:]
    residual, normed_two, branch, grad, cotangent, low, expand, contract = refs[:8]
    output, back, rounded, hidden, slope, read_grad, in_sem, part_sem, low_sem, out_sem = refs[8:]
    unit = expand.shape[1]
    width = gain.shape[1]
    weights = start(
        [(normed_h, normed_two), (cotangent_h, cotangent)] + weight_copies(own, unit, expand, contract), in_sem
    )
    others = start([(residual_h, residual), (branch_h, branch), (grad_h, grad)], part_sem)
    last = start([(low_h, low)], low_sem)
    gain_grad[...] = jnp.zeros_like(gain_grad)
    shift_grad[...] = jnp.zeros_like(shift_grad)
    finish(weights)
    expand = expand[...].reshape(-1, width)
    contract = contract[...].reshape(-1, width)
    leaving = []
    for k, part in enumerate(parts()):
        one, two = ffn_part(
            part, normed_two, cotangent, shifts, hidden.shape[1], expand, contract, hidden, slope, shift_grad
        )
        if k == 0:
            finish(others)
        value = residual[part]
        output[part] = (value + (branch[part] + one)).astype(bf16)
        total = grad[part] + two
        inverse = lax.rsqrt(jnp.mean(value * value, axis=-1, keepdims=True) + epsilon)
        unscaled = value * inverse
        gain_grad[...] += jnp.sum(total * unscaled, axis=0, keepdims=True)
        pulled = total * gain[...]
        mean = jnp.mean(pulled * unscaled, axis=-1, keepdims=True)
        value = cotangent[part].astype(f32) + inverse * (pulled - unscaled * mean)
        back[part] = value
        rounded[part] = value.astype(bf16)
        leaving += start(
            [(o.at[part], h.at[part]) for o, h in ((output, output_h), (back, back_h), (rounded, rounded_h))], out_sem
        )
    ffn_grads(normed_two, cotangent, hidden, slope, sent, kept)
    finish(last)
    read_grad[...] = across(low[...], rounded[...])
    emit(me[0], plans, read_grad, targets)
    finish(leaving)


def vmem(shape, dtype):
    return pltpu.VMEM(shape, dtype)


WHOLE = pl.BlockSpec(memory_space=pltpu.VMEM)


def ffn_first(me, gain, shifts, inputs, cotangent, low, readers, lists, size, skip, own, unit):
    blocks = sum(one.shape[0] for one in own)
    width = inputs.shape[1]
    units = blocks * unit
    kept = (max(1, blocks // 2), 2 * units // max(2, blocks), width)
    shape = jax.ShapeDtypeStruct
    return pl.pallas_call(
        partial(first_kernel, lists, size, skip),
        in_specs=[SCALAR, WHOLE, WHOLE] + [ANY] * (3 + len(readers) + len(own)),
        out_specs=[ANY] * 4 + [WHOLE] * 3,
        out_shape=[
            shape((LEN, width), f32),
            shape((LEN, width), bf16),
            shape((LEN, width), f32),
            shape((LEN, width), f32),
            shape(kept, bf16),
            shape(kept, f32),
            shape((1, units), f32),
        ],
        scratch_shapes=[
            vmem((LEN, width), bf16),
            vmem((LEN, width), bf16),
            vmem(low.shape, bf16),
            vmem((low.shape[1], width), bf16),
            vmem((blocks, unit, width), bf16),
            vmem((blocks, unit, width), bf16),
            vmem((LEN, width), f32),
            vmem((LEN, width), bf16),
            vmem((LEN, width), f32),
            vmem((LEN, width), f32),
            vmem((LEN, units), bf16),
            vmem((LEN, units), bf16),
        ]
        + [pltpu.SemaphoreType.DMA] * 3,
        compiler_params=PARAMS,
        cost_estimate=FILLER,
        name="ffn_first",
    )(me, gain, shifts, inputs, cotangent, low, *readers, *own)


def ffn_second(me, gain, shifts, residual, normed_two, branch, grad, cotangent, low, own, unit, size, plans):
    blocks = sum(one.shape[0] for one in own)
    width = cotangent.shape[1]
    units = blocks * unit
    kept = (max(1, blocks // 2), 2 * units // max(2, blocks), width)
    targets = emitted(plans, low.shape[1], size, width)
    shape = jax.ShapeDtypeStruct
    return pl.pallas_call(
        partial(second_kernel, plans, len(own)),
        in_specs=[SCALAR, WHOLE, WHOLE] + [ANY] * (6 + len(own)),
        out_specs=[ANY] * 3 + [WHOLE] * (4 + len(targets)),
        out_shape=[
            shape((LEN, width), bf16),
            shape((LEN, width), f32),
            shape((LEN, width), bf16),
            shape((1, width), f32),
            shape(kept, bf16),
            shape(kept, f32),
            shape((1, units), f32),
        ]
        + targets,
        scratch_shapes=[
            vmem((LEN, width), f32),
            vmem((LEN, width), bf16),
            vmem((LEN, width), f32),
            vmem((LEN, width), f32),
            vmem((LEN, width), bf16),
            vmem(low.shape, bf16),
            vmem((blocks, unit, width), bf16),
            vmem((blocks, unit, width), bf16),
            vmem((LEN, width), bf16),
            vmem((LEN, width), f32),
            vmem((LEN, width), bf16),
            vmem((LEN, units), bf16),
            vmem((LEN, units), bf16),
            vmem((low.shape[1], width), f32),
        ]
        + [pltpu.SemaphoreType.DMA] * 4,
        compiler_params=PARAMS,
        cost_estimate=FILLER,
        name="ffn_second",
    )(me, gain, shifts, residual, normed_two, branch, grad, cotangent, low, *own)


def back_kernel(lists, size, skip, plans, me, rounded, normed, share, pull_f, pull_i, *refs):
    readers = refs[: len(lists)]
    grads, offset_grad = refs[len(lists) : len(lists) + 2]
    targets = refs[len(lists) + 2 : -6]
    gate_grad, readout, pulled, drive, decay, sem = refs[-6:]
    group = pl.program_id(0)
    wide = share.shape[1]
    hidden = readout.shape[0]

    @pl.when(group == 0)
    def _():
        finish(start(placed(me[0], lists, readers, skip, size, readout), sem))

    reader = readout[pl.ds(pl.multiple_of(group * wide, wide), wide)]
    held = jnp.zeros((LANES, wide), f32)
    prod = jnp.ones((LANES, wide), f32)
    for part in reversed(parts()):
        pulled[part] = against(rounded[part], reader)
        for k in reversed(range(part.start // LANES, part.stop // LANES)):
            if k < STEPS - 1:
                after = 1.0 - share[tiles(k + 1, 1)]
                prod = after * prod
                held = pulled[tiles(k, 1)] + after * held
            else:
                held = pulled[tiles(k, 1)]
            drive[tiles(k, 1)] = held
            decay[tiles(k, 1)] = prod
    first_retain = 1.0 - share[pl.ds(0, LANES)]
    ends = [jnp.zeros((1, wide), f32)]
    for k in range(LANES - 1, 0, -1):
        whole = held[k : k + 1] + prod[k : k + 1] * ends[-1]
        ends.append(first_retain[k : k + 1] * whole)
    entering = jnp.concatenate(ends[::-1], axis=0)
    entering = jnp.concatenate([entering, entering], axis=0)

    def more(k, sums):
        rows = tiles(2 * k, 2)
        carried = drive[rows] + decay[rows] * entering
        found = []
        for t, factor in enumerate((pull_f, pull_i, share)):
            value = (carried * factor[rows].astype(f32)).astype(bf16)
            grads[t, rows] = value
            found.append(sums[t] + value.astype(f32))
        return tuple(found)

    sums = (jnp.zeros((2 * LANES, wide), f32),) * 3
    for k in range(STEPS // 2):
        sums = more(k, sums)
    for t in range(3):
        offset_grad[t : t + 1] = jnp.sum(sums[t], axis=0, keepdims=True)
        rows = pl.ds(pl.multiple_of(t * hidden + group * wide, wide), wide)
        gate_grad[rows] = across(grads[t], normed[...])

    @pl.when(group == hidden // wide - 1)
    def _():
        emit(me[0], plans, gate_grad, targets)


def back(me, rounded, normed, share, pull_f, pull_i, readers, lists, size, skip, plans):
    width = normed.shape[1]
    hidden = share.shape[1]
    wide = 256
    fixed = lambda g: (0, 0)
    tall = lambda g: (0, g)
    shape = jax.ShapeDtypeStruct
    firm = pl.BlockSpec((LEN, width), fixed)
    targets = emitted(plans, 3 * hidden, 3 * size, width)
    return pl.pallas_call(
        partial(back_kernel, lists, size, skip, plans),
        grid=(hidden // wide,),
        in_specs=[SCALAR, firm, firm] + [pl.BlockSpec((LEN, wide), tall)] * 3 + [ANY] * len(readers),
        out_specs=[pl.BlockSpec((3, LEN, wide), lambda g: (0, 0, g)), pl.BlockSpec((3, wide), tall)]
        + [pl.BlockSpec(one.shape, lambda g, rank=len(one.shape): (0,) * rank) for one in targets],
        out_shape=[shape((3, LEN, hidden), bf16), shape((3, hidden), f32)] + targets,
        scratch_shapes=[
            vmem((3 * hidden, width), f32),
            vmem((hidden, width), bf16),
            vmem((LEN, wide), f32),
            vmem((LEN, wide), f32),
            vmem((LEN, wide), f32),
            pltpu.SemaphoreType.DMA,
        ],
        compiler_params=PARAMS,
        cost_estimate=FILLER,
        name="back",
    )(me, rounded, normed, share, pull_f, pull_i, *readers)


def inputs_kernel(lists, size, me, inputs, gain, back, grads_h, *refs):
    arrays = refs[: len(lists)]
    output, gain_grad, grads, weights, weight_sem, sem = refs[len(lists) :]
    arriving = start(placed(me[0], lists, arrays, 0, size, weights), weight_sem)
    hidden = weights.shape[0] // 3
    for part in parts():
        arriving += start([(grads_h.at[t, part], grads.at[t, part]) for t in range(3)], sem)
    gain_grad[...] = jnp.zeros_like(gain_grad)
    finish(arriving)
    for part in parts():
        total = matmul(grads[0, part], weights[:hidden])
        for t in range(1, 3):
            total = total + matmul(grads[t, part], weights[t * hidden : (t + 1) * hidden])
        value = inputs[part].astype(f32)
        inverse = lax.rsqrt(jnp.mean(value * value, axis=-1, keepdims=True) + epsilon)
        unscaled = value * inverse
        gain_grad[...] += jnp.sum(total * unscaled, axis=0, keepdims=True)
        pulled = total * gain[...]
        mean = jnp.mean(pulled * unscaled, axis=-1, keepdims=True)
        output[part] = back[part] + inverse * (pulled - unscaled * mean)


def inputs_back(me, inputs, gain, back_grad, grads, arrays, lists, size):
    width = inputs.shape[1]
    hidden = grads.shape[2]
    return pl.pallas_call(
        partial(inputs_kernel, lists, size),
        in_specs=[SCALAR, WHOLE, WHOLE, WHOLE, ANY] + [ANY] * len(arrays),
        out_specs=[WHOLE, WHOLE],
        out_shape=[jax.ShapeDtypeStruct((LEN, width), f32), jax.ShapeDtypeStruct((1, width), f32)],
        scratch_shapes=[
            vmem((3, LEN, hidden), bf16),
            vmem((3 * hidden, width), bf16),
            pltpu.SemaphoreType.DMA,
            pltpu.SemaphoreType.DMA,
        ],
        compiler_params=PARAMS,
        cost_estimate=FILLER,
        name="inputs_back",
    )(me, inputs, gain, back_grad, grads, *arrays)


class Wires:
    def __init__(self, mesh):
        self.inner = mesh.shape["fsdp"]
        self.count = mesh.shape["dp"] * self.inner
        rest = [1 << b for b in range(1, self.inner.bit_length() - 1)]
        self.digits = [rest[i : i + 2] for i in range(0, len(rest), 2)]
        self.core, self.x, self.y = self.inner, 2 * self.inner, 1
        self.bits = {"A": [self.y, self.x, self.core], "B": [self.x, self.y, self.core]}

    def swap(self, value, mask):
        return lax.ppermute(value, AXES, [(i, i ^ mask) for i in range(self.count)])

    def spread(self, digit):
        return [sum(bit for j, bit in enumerate(digit) if k >> j & 1) for k in range(1 << len(digit))]

    def masks(self, order):
        found = [0]
        for digit in self.digits:
            found = [m ^ s for s in self.spread(digit) for m in found]
        lists = [found]
        for bit in self.bits[order]:
            lists = lists + [[m ^ bit for m in one] for one in lists]
        return lists

    def line(self, held, digits, tie=None):
        for digit in digits:
            came = [self.swap(held, m) for m in self.spread(digit)[1:]]
            if tie:
                _, *came = tie(*came)
            held = jnp.concatenate([held] + came)
        return held

    def line_start(self, held):
        for digit in reversed(self.digits[1:]):
            held = self.line_end(*self.line_step(held, digit))
        return self.line_step(held, self.digits[0])

    def line_step(self, held, digit):
        masks = self.spread(digit)
        blocks = jnp.split(held, len(masks))
        return blocks[0], [self.swap(one.astype(bf16), m) for one, m in zip(blocks[1:], masks[1:])]

    def line_end(self, held, came):
        for other in came:
            held = held + other.astype(f32)
        return held


def tied(*values):
    return lax.optimization_barrier(values)


def solution(mesh):
    wires = Wires(mesh)
    count = wires.count
    masks = {order: wires.masks(order) for order in "AB"}
    flat = {order: sum(masks[order], []) for order in "AB"}

    def shards(tokens, gating, offsets, prescale, readout, midscale, expand, shifts, contract, cotangent):
        swap = wires.swap
        index = lax.axis_index("dp") * wires.inner + lax.axis_index("fsdp")
        unit = readout.shape[0]
        wide = expand.shape[1]
        thin = prescale.shape[0]
        width = tokens.shape[1]
        hidden = count * unit
        assert tokens.shape[0] == LEN
        me = index.astype(jnp.int32).reshape(1)

        rest = jnp.concatenate([expand.T, contract])[None]
        row = jnp.concatenate([jnp.pad(one, (0, 128 - one.shape[0])) for one in (offsets, shifts, prescale, midscale)])
        taken = 4 * unit
        part = jnp.pad(jnp.concatenate([gating.T, readout, row[None]]), ((0, LANES - 1), (0, 0)))
        inputs = interleaved(tokens)
        gate_line = wires.line(part[None], wires.digits, lambda *came: tied(inputs, *came))
        gate_line, rest, cotangent = tied(gate_line, rest, cotangent)
        nz = gate_line.shape[0]
        cut = nz // 2
        gate_x = swap(gate_line, wires.x)
        gate_y = swap(gate_line, wires.y)
        rest_early = [swap(rest, m) for m in wires.spread(wires.digits[0])[1:]]
        upstream = interleaved(cotangent)
        gate_x, upstream, rest_early[1], rest_early[2] = tied(gate_x, upstream, rest_early[1], rest_early[2])
        gate_y, rest_early[0] = tied(gate_y, rest_early[0])
        gate_list = [gate_line, gate_x, gate_y, swap(gate_x[:cut], wires.y), swap(gate_y[cut:], wires.x)]
        gate_list += [swap(one, wires.core) for one in gate_list]
        rest_line = wires.line(jnp.concatenate([rest, *rest_early]), wires.digits[1:])
        rest_x = swap(rest_line, wires.x)
        rest_y = swap(rest_line, wires.y)
        rest_core = swap(rest_line, wires.core)

        quads = masks["A"]
        gate_lists = [quads[0], quads[2], quads[1], quads[3][:cut], quads[3][cut:]]
        gate_lists += [[m ^ wires.core for m in one] for one in gate_lists]
        row_arrays = gate_list
        sizes = (3 * unit, wide, thin)
        owner_masks = jnp.asarray(np.array(sum(gate_lists, []), np.int32)[:, None])
        ffn_masks = np.concatenate([masks["A"][k] for k in (0, 1, 4, 5, 2, 3, 6, 7)])
        lane_masks = jnp.asarray(np.repeat(ffn_masks, wide).astype(np.int32)[None])

        if unit % 16:
            places = np.argsort(np.asarray(sum(gate_lists, [])))
            whole = jnp.take(jnp.concatenate(gate_list), jnp.asarray(places)[index ^ jnp.arange(count)], axis=0)
            gate_list = [
                jnp.concatenate([whole[:, : 3 * unit].reshape(-1, width), whole[:, 3 * unit : taken].reshape(-1, width)])[None]
            ]
            row_arrays = [jnp.concatenate([one[:, taken : taken + LANES] for one in row_arrays])]
            gate_lists, gate_size, read_size, zero = [[0]], 3 * hidden, hidden, jnp.zeros_like(me)
            ffn_unit = 4 * nz * wide
        else:
            gate_size, read_size, zero = 3 * unit, unit, me
            ffn_unit = wide

        both = jnp.concatenate([zero, me])
        normed, share, low, pull_f, pull_i, gain_one, gain_two, all_shifts = gates(
            both, inputs, row_arrays, 0 if unit % 16 else taken, owner_masks, lane_masks, gate_list, gate_lists, gate_size, sizes, hidden
        )
        low, rest_y, rest_x, rest_core = tied(low, rest_y, rest_x, rest_core)
        rest_corner = [swap(rest_x, wires.y)]

        def merged(group):
            if not unit % 16:
                return group
            halves = [jnp.concatenate([one[:, at : at + wide].reshape(-1, width) for one in group]) for at in (0, wide)]
            return [jnp.concatenate(halves)[None]]

        own = merged([rest_line, rest_y, rest_core, swap(rest_y, wires.core)])

        def apart(grads):
            if not unit % 16:
                return grads
            return grads.reshape(2, -1, wide, width).transpose(1, 0, 2, 3).reshape(-1, 2 * wide, width)

        residual, normed_two, branch, grad, sent_0, kept_0, shift_0 = ffn_first(
            zero, gain_two, all_shifts, inputs, upstream, low, gate_list, gate_lists, read_size, gate_size, own,
            ffn_unit,
        )
        residual, normed_two, branch, grad, sent_0, kept_0, shift_0, rest_x, *rest_corner = tied(
            residual, normed_two, branch, grad, sent_0, kept_0, shift_0, rest_x, *rest_corner
        )
        far = [rest_x, *rest_corner]
        own = merged(far + [swap(one, wires.core) for one in far])
        near_core = swap(apart(sent_0), wires.core)
        half = count // 2
        read_plans = [(flat["A"][:half], f32), (flat["A"][half:], bf16)]
        output, residual_grad, rounded, midscale_grad, sent_1, kept_1, shift_1, *read_blocks = ffn_second(
            zero, gain_two, all_shifts, residual, normed_two, branch, grad, upstream, low, own, ffn_unit, unit,
            None if unit % 16 else read_plans,
        )
        read_kept, read_sent = sorted_blocks(index, read_plans, read_blocks, unit) if unit % 16 else read_blocks

        output, residual_grad, rounded, midscale_grad, sent_1, kept_1, shift_1, read_kept, read_sent, near_core = tied(
            output, residual_grad, rounded, midscale_grad, sent_1, kept_1, shift_1, read_kept, read_sent, near_core
        )
        far_core = swap(apart(sent_1), wires.core)
        read_core = swap(read_sent, wires.core)
        ffn_terms = [(apart(kept_0), near_core), (apart(kept_1), far_core)]

        def quad(k, low, high):
            kept, came = ffn_terms[k // 2]
            base = k % 2 * nz
            ffn = kept[base + low : base + high] + came[base + low : base + high].astype(f32)
            base = k * nz
            read = read_kept[base + low : base + high] + read_core[base + low : base + high].astype(f32)
            return jnp.concatenate([ffn, read], axis=1)

        send_x = jnp.concatenate([quad(3, cut, nz), quad(2, cut, nz)]).astype(bf16)
        send_y = jnp.concatenate([quad(3, 0, cut), quad(1, 0, cut)]).astype(bf16)
        rounded, send_x, send_y = tied(rounded, send_x, send_y)
        rest_x, rest_y = swap(send_x, wires.x), swap(send_y, wires.y)
        places = [quads[3][cut:] + quads[2][cut:] + quads[3][:cut] + quads[1][:cut]]
        places.append(quads[2][:cut] + quads[1][cut:] + quads[0])
        away = [[m ^ wires.core for m in one] for one in places]
        gate_plans = [(places[0], f32), (places[1], f32), (away[0], bf16), (away[1], bf16)]
        gate_grads, off_grad, *gate_blocks = back(
            zero, rounded, normed, share, pull_f, pull_i, gate_list, gate_lists, read_size, gate_size,
            None if unit % 16 else gate_plans,
        )
        if unit % 16:
            gate_blocks = sorted_blocks(index, gate_plans, gate_blocks, 3 * unit)
        first_kept, second_kept, first_sent, second_sent, gate_grads, off_grad, rest_x, rest_y = tied(
            *gate_blocks, gate_grads, off_grad, rest_x, rest_y
        )
        first_core = swap(first_sent, wires.core)
        second_core = swap(second_sent, wires.core)
        first = (first_kept + first_core.astype(f32)).astype(bf16)
        send_x = (quad(2, 0, cut) + rest_y[:cut].astype(f32)).astype(bf16)
        send_y = (quad(1, cut, nz) + rest_x[:cut].astype(f32)).astype(bf16)
        gate_grads, first, send_x, send_y, output, midscale_grad, off_grad, shift_0, shift_1 = tied(
            gate_grads, first, send_x, send_y, output, midscale_grad, off_grad, shift_0, shift_1
        )
        gate_x, gate_y = swap(first[:nz], wires.x), swap(first[nz:], wires.y)
        rest_xx, rest_yy = swap(send_x, wires.x), swap(send_y, wires.y)
        tokens_grad, prescale_grad = inputs_back(
            zero, inputs, gain_one, residual_grad, gate_grads, gate_list, gate_lists, gate_size
        )
        tokens_grad, prescale_grad, gate_x, gate_y, rest_xx, rest_yy = tied(
            tokens_grad, prescale_grad, gate_x, gate_y, rest_xx, rest_yy
        )

        def second(low, high):
            return second_kept[low:high] + second_core[low:high].astype(f32)

        send_x = (second(0, cut) + gate_y[:cut].astype(f32)).astype(bf16)
        send_y = (second(cut, nz) + gate_x[:cut].astype(f32)).astype(bf16)
        send_x, send_y, rest_xx, rest_yy = tied(send_x, send_y, rest_xx, rest_yy)
        gate_xx, gate_yy = swap(send_x, wires.x), swap(send_y, wires.y)

        def met(x_way, y_way, xx_way, yy_way):
            low_half = y_way[cut:].astype(f32) + xx_way.astype(f32)
            return jnp.concatenate([low_half, x_way[cut:].astype(f32) + yy_way.astype(f32)])

        rest_part = quad(0, 0, nz) + met(rest_x, rest_y, rest_xx, rest_yy)
        rest_part, output, prescale_grad = tied(rest_part, output, prescale_grad)
        rest_kept, rest_came = wires.line_start(rest_part)
        vectors = vector_rows(
            me, lane_masks, sizes, count, off_grad, shift_0, shift_1, prescale_grad, midscale_grad
        )
        gate_xx, gate_yy, vectors = tied(gate_xx, gate_yy, vectors)
        gate_part = second(nz, 2 * nz) + met(gate_x, gate_y, gate_xx, gate_yy)
        gate_part, tokens_grad, vectors, output = tied(gate_part, tokens_grad, vectors, output)
        gate_kept, gate_came = wires.line_start(gate_part)
        vectors = lax.all_to_all(vectors, AXES, 0, 0, tiled=True)
        tokens_grad = sequential(tokens_grad, FILLER)
        tokens_grad, output = tied(tokens_grad, output)
        block_output = sequential(output, QUICK)
        tokens_grad, block_output, vectors, gate_came, rest_came = tied(
            tokens_grad, block_output, vectors, gate_came, rest_came
        )
        vectors = jnp.sum(vectors, axis=0)
        vector_parts = [vectors[at : at + size] for at, size in zip(range(0, 512, 128), (*sizes, thin))]
        tokens_grad, vector_parts, block_output, rest_kept, rest_came, gate_kept, gate_came = tied(
            tokens_grad, vector_parts, block_output, rest_kept, rest_came, gate_kept, gate_came
        )
        rest_part = wires.line_end(rest_kept, rest_came)[0]
        gate_part = wires.line_end(gate_kept, gate_came)[0]
        offsets_part, shifts_part, prescale_part, midscale_part = vector_parts
        return (
            block_output,
            tokens_grad,
            gate_part.T,
            offsets_part,
            prescale_part,
            rest_part[2 * wide :],
            midscale_part,
            rest_part[:wide].T,
            shifts_part,
            rest_part[wide : 2 * wide],
        )

    rows = P(AXES, None)
    columns = P(None, AXES)
    line = P(AXES)
    in_specs = (rows, columns, line, line, rows, line, columns, line, rows, rows)
    out_specs = (rows, rows, columns, line, line, rows, line, columns, line, rows)
    return jax.shard_map(shards, mesh=mesh, in_specs=in_specs, out_specs=out_specs, check_vma=False)
```

```python
from functools import partial

import jax
import jax.numpy as jnp
import numpy as np
from jax import lax
from jax.experimental import pallas as pl
from jax.experimental.pallas import tpu as pltpu
from jax.sharding import PartitionSpec as P

LEN = 1024
LANES = 8
STEPS = LEN // LANES
ROWS = 256
AXES = ("dp", "fsdp")
epsilon = 1e-06
bf16 = jnp.bfloat16
f32 = jnp.float32
ANY = pl.BlockSpec(memory_space=pl.ANY)
SCALAR = pl.BlockSpec(memory_space=pltpu.SMEM)
FILLER = pl.CostEstimate(flops=10**11, bytes_accessed=10**8, transcendentals=0)
QUICK = pl.CostEstimate(flops=1000, bytes_accessed=1000, transcendentals=0)
PARAMS = pltpu.CompilerParams(vmem_limit_bytes=56 * 1024 * 1024)


def matmul(left, right):
    return jnp.dot(left, right, preferred_element_type=f32)


def across(left, right):
    return lax.dot_general(left, right, (((0,), (0,)), ((), ())), preferred_element_type=f32)


def against(left, right):
    return lax.dot_general(left, right, (((1,), (1,)), ((), ())), preferred_element_type=f32)


def interleave_kernel(values, target, scratch):
    for j in range(scratch.shape[0]):
        columns = slice(j * 128, (j + 1) * 128)
        for run in range(LANES):
            rows = slice(run * STEPS, (run + 1) * STEPS)
            scratch[j, pl.ds(run, STEPS, stride=LANES)] = values[rows, columns].astype(f32)
        target[:, columns] = scratch[j].astype(target.dtype)


def interleaved(values):
    return pl.pallas_call(
        interleave_kernel,
        out_shape=jax.ShapeDtypeStruct(values.shape, values.dtype),
        scratch_shapes=[pltpu.VMEM((values.shape[1] // 128, LEN, 128), f32)],
        compiler_params=PARAMS,
        cost_estimate=QUICK,
        name="interleave",
    )(values)


def sequence_kernel(values, target, scratch):
    for j in range(scratch.shape[0]):
        columns = slice(j * 128, (j + 1) * 128)
        scratch[j] = values[:, columns].astype(f32)
        for run in range(LANES):
            rows = slice(run * STEPS, (run + 1) * STEPS)
            target[rows, columns] = scratch[j, pl.ds(run, STEPS, stride=LANES)].astype(target.dtype)


def sequential(values, cost):
    return pl.pallas_call(
        sequence_kernel,
        out_shape=jax.ShapeDtypeStruct(values.shape, values.dtype),
        scratch_shapes=[pltpu.VMEM((values.shape[1] // 128, LEN, 128), f32)],
        compiler_params=PARAMS,
        cost_estimate=cost,
        name="sequence",
    )(values)


def down(values):
    return jnp.concatenate([jnp.zeros_like(values[:1]), values[:-1]], axis=0)


def tiles(k, count):
    if isinstance(k, int):
        return pl.ds(k * LANES, count * LANES)
    return pl.ds(pl.multiple_of(k * LANES, LANES), count * LANES)


def parts():
    return [slice(k, k + ROWS) for k in range(0, LEN, ROWS)]


def start(pairs, sem):
    copies = [pltpu.make_async_copy(source, target, sem) for source, target in pairs]
    for copy in copies:
        copy.start()
    return copies


def finish(copies):
    for copy in copies:
        copy.wait()


def placed(me, lists, arrays, first, size, target):
    found = []
    for masks, array in zip(lists, arrays):
        for b, mask in enumerate(masks):
            at = pl.multiple_of((me ^ mask) * size, size)
            found.append((array.at[b, pl.ds(first, size)], target.at[pl.ds(at, size)]))
    return found


def emitted(plans, rows, size, width):
    if plans is None:
        return [jax.ShapeDtypeStruct((rows, width), f32)]
    return [jax.ShapeDtypeStruct((len(masks), size, width), dtype) for masks, dtype in plans]


def emit(me, plans, source, targets):
    if plans is None:
        targets[0][...] = source[...]
        return
    for (masks, _), target in zip(plans, targets):
        size = target.shape[1]
        for p, mask in enumerate(masks):
            at = pl.multiple_of((me ^ mask) * size, size)
            target[p] = source[pl.ds(at, size)].astype(target.dtype)


def sorted_blocks(me, plans, grads, size):
    whole = grads[0].reshape(-1, size, grads[0].shape[1])
    return [jnp.take(whole, me ^ jnp.asarray(masks), axis=0).astype(dtype) for masks, dtype in plans]


def lanes_of(count, size):
    lane = lax.broadcasted_iota(jnp.int32, (1, count), 1)
    piece = ((lane.astype(f32) + 0.5) * (1.0 / size)).astype(jnp.int32)
    return piece, lane - piece * size


def selector(place):
    rows = lax.broadcasted_iota(jnp.int32, (128, place.shape[1]), 0)
    return jnp.where(rows == place, 1.0, 0.0).astype(bf16)


def laid_out(rows, owners, lane_owner, place):
    spread = matmul(rows, selector(place))
    return jnp.sum(jnp.where(owners == lane_owner, spread, 0.0), axis=0, keepdims=True)


def cut_up(vector, lane_owner, place, count):
    rows = lax.broadcasted_iota(jnp.int32, (count, vector.shape[1]), 0)
    found = jnp.where(rows == lane_owner, vector, 0.0)
    high = found.astype(bf16)
    low = (found - high.astype(f32)).astype(bf16)
    choose = selector(place)
    return against(high, choose) + against(low, choose)


def vectors_kernel(sizes, me, masks, offsets, shift_0, shift_1, prescale, midscale, target):
    count = target.shape[0]
    flat = jnp.concatenate([offsets[t : t + 1] for t in range(3)], axis=1)
    target[:, :128] = cut_up(flat, *lanes_of(flat.shape[1], sizes[0]), count)
    shifts = jnp.concatenate([shift_0[...], shift_1[...]], axis=1)
    target[:, 128:256] = cut_up(shifts, masks[...] ^ me[0], lanes_of(shifts.shape[1], sizes[1])[1], count)
    target[:, 256:384] = cut_up(prescale[...], *lanes_of(prescale.shape[1], sizes[2]), count)
    target[:, 384:512] = cut_up(midscale[...], *lanes_of(midscale.shape[1], sizes[2]), count)


def vector_rows(me, masks, sizes, count, *grads):
    return pl.pallas_call(
        partial(vectors_kernel, sizes),
        in_specs=[SCALAR] + [pl.BlockSpec(memory_space=pltpu.VMEM)] * 6,
        out_specs=pl.BlockSpec(memory_space=pltpu.VMEM),
        out_shape=jax.ShapeDtypeStruct((count, 512), f32),
        compiler_params=PARAMS,
        cost_estimate=FILLER,
        name="vectors",
    )(me, masks, *grads)


def gates_kernel(lists, size, taken, row_count, sizes, me, inputs, owner_masks, lane_masks, *refs):
    row_arrays, refs = refs[:row_count], refs[row_count:]
    arrays = refs[: len(lists)]
    normed, share, low, pull_f, pull_i, gain_one, gain_two, shifts = refs[len(lists) : len(lists) + 8]
    weights, pre, mid, decay, drive, offsets, small, sem, small_sem = refs[len(lists) + 8 :]
    group = pl.program_id(0)
    wide = share.shape[1]
    hidden = weights.shape[0] // 3

    @pl.when(group == 0)
    def _():
        copies = start(placed(me[0], lists, arrays, 0, size, weights), sem)
        found, at = [], 0
        for array in row_arrays:
            found.append((array.at[:, pl.ds(taken, LANES)], small.at[pl.ds(at, array.shape[0])]))
            at += array.shape[0]
        finish(start(found, small_sem))
        rows = jnp.sum(small[...].astype(f32), axis=1).astype(bf16)
        owners = owner_masks[...] ^ me[1]
        width = inputs.shape[1]
        gain = laid_out(rows[:, 256:384], owners, *lanes_of(width, sizes[2]))
        gain_one[...] = gain
        gain_two[...] = laid_out(rows[:, 384:512], owners, *lanes_of(width, sizes[2]))
        place = lanes_of(shifts.shape[1], sizes[1])[1]
        shifts[...] = laid_out(rows[:, 128:256], owners, lane_masks[...] ^ me[1], place)
        flat = laid_out(rows[:, :128], owners, *lanes_of(3 * hidden, sizes[0]))
        for t in range(3):
            for k in range(hidden // wide):
                offsets[k, t : t + 1] = flat[:, t * hidden + k * wide : t * hidden + (k + 1) * wide]
        for part in parts():
            value = inputs[part].astype(f32)
            scale = lax.rsqrt(jnp.mean(value * value, axis=-1, keepdims=True) + epsilon)
            normed[part] = (value * scale * gain).astype(bf16)
        finish(copies)

    def step(k, carry):
        prod, held = carry
        rows = tiles(2 * k, 2)
        forget = 1.0 / (1.0 + jnp.exp(-pre[0, rows]))
        entry = 1.0 / (1.0 + jnp.exp(-pre[1, rows]))
        whole = 1.0 / (forget + entry)
        keep = forget * whole
        rest = entry * whole
        flow = rest * pre[2, rows]
        both = keep * rest
        share[rows] = rest
        mid[0, rows] = both * (1.0 - forget)
        mid[1, rows] = both * (entry - 1.0)
        held_0 = keep[:LANES] * held + flow[:LANES]
        prod_0 = keep[:LANES] * prod
        held = keep[LANES:] * held_0 + flow[LANES:]
        prod = keep[LANES:] * prod_0
        drive[rows] = jnp.concatenate([held_0, held], axis=0)
        decay[rows] = jnp.concatenate([prod_0, prod], axis=0)
        return prod, held

    begin = (jnp.ones((LANES, wide), f32), jnp.zeros((LANES, wide), f32))
    prod, held = begin
    ws = [weights[pl.ds(pl.multiple_of(t * hidden + group * wide, wide), wide)] for t in range(3)]
    for part in parts():
        for t in range(3):
            pre[t, part] = against(normed[part], ws[t]) + offsets[group, t : t + 1]
        for k in range(part.start // (2 * LANES), part.stop // (2 * LANES)):
            prod, held = step(k, (prod, held))
    ends = [jnp.zeros((1, wide), f32)]
    for k in range(LANES - 1):
        ends.append(prod[k : k + 1] * ends[-1] + held[k : k + 1])
    entering = jnp.concatenate(ends, axis=0)
    entering = jnp.concatenate([entering, entering], axis=0)

    def join(k, before):
        rows = tiles(2 * k, 2)
        value = drive[rows] + decay[rows] * entering
        low[rows] = value.astype(bf16)
        change = jnp.concatenate([before, value[:LANES]], axis=0) - pre[2, rows]
        pull_f[rows] = (change * mid[0, rows]).astype(bf16)
        pull_i[rows] = (change * mid[1, rows]).astype(bf16)
        return value[LANES:]

    lax.fori_loop(0, STEPS // 2, join, entering[:LANES], unroll=8)


def gates(me, inputs, row_arrays, taken, owner_masks, lane_masks, arrays, lists, size, sizes, hidden):
    width = inputs.shape[1]
    shape = jax.ShapeDtypeStruct
    whole = lambda one: pl.BlockSpec(one.shape, lambda g: (0, 0))
    wide = 256
    fixed = lambda g: (0, 0)
    tall = lambda g: (0, g)
    out = lambda dtype: jax.ShapeDtypeStruct((LEN, hidden), dtype)
    solid = pl.BlockSpec((LEN, width), fixed)
    return pl.pallas_call(
        partial(gates_kernel, lists, size, taken, len(row_arrays), sizes),
        grid=(hidden // wide,),
        in_specs=[SCALAR, solid, whole(owner_masks), whole(lane_masks)] + [ANY] * (len(row_arrays) + len(arrays)),
        out_specs=[solid]
        + [pl.BlockSpec((LEN, wide), tall)] * 4
        + [pl.BlockSpec((1, width), fixed)] * 2
        + [whole(lane_masks)],
        out_shape=[jax.ShapeDtypeStruct((LEN, width), bf16)]
        + [out(f32), out(bf16), out(bf16), out(bf16), shape((1, width), f32)]
        + [shape((1, width), f32), shape(lane_masks.shape, f32)],
        scratch_shapes=[
            pltpu.VMEM((3 * hidden, width), bf16),
            pltpu.VMEM((3, LEN, wide), f32),
            pltpu.VMEM((2, LEN, wide), f32),
            pltpu.VMEM((LEN, wide), f32),
            pltpu.VMEM((LEN, wide), f32),
            pltpu.VMEM((hidden // wide, 3, wide), f32),
            pltpu.VMEM((owner_masks.shape[0], LANES, width), bf16),
            pltpu.SemaphoreType.DMA,
            pltpu.SemaphoreType.DMA,
        ],
        compiler_params=PARAMS,
        cost_estimate=FILLER,
        name="gates",
    )(me, inputs, owner_masks, lane_masks, *row_arrays, *arrays)


def gelu_both(x):
    inner = np.float32(np.sqrt(2 / np.pi))
    square = x * x
    t = jnp.tanh(inner * (x + np.float32(0.044715) * (square * x)))
    cdf = 0.5 + 0.5 * t
    slope = cdf + (0.5 * x) * (1.0 - t * t) * (inner + np.float32(3 * 0.044715) * inner * square)
    return x * cdf, slope


def ffn_part(part, normed_two, cotangent, shifts, base, expand, contract, hidden, slope, shift_grad):
    units = expand.shape[0]
    n2 = normed_two[part]
    ct = cotangent[part]
    for j in range(0, units, 256):
        cols = slice(j, j + 256)
        act, grad = gelu_both(against(n2, expand[cols]) + shifts[:, base + j : base + j + 256])
        hidden[part, cols] = act.astype(bf16)
        rounded = (against(ct, contract[cols]) * grad).astype(bf16)
        slope[part, cols] = rounded
        shift_grad[:, cols] += jnp.sum(rounded.astype(f32), axis=0, keepdims=True)
    return matmul(hidden[part], contract[...]), matmul(slope[part], expand[...])


def ffn_grads(normed_two, cotangent, hidden, slope, stages, targets, sem):
    units = hidden.shape[1]
    copies = []
    for j in (1, 0):
        stage = stages[j]
        blocks, rows, width = stage.shape
        unit = rows // 2
        cols = slice(j * units // 2, (j + 1) * units // 2)
        stage[:, :unit] = across(slope[:, cols], normed_two[...]).astype(stage.dtype).reshape(blocks, unit, width)
        stage[:, unit:] = across(hidden[:, cols], cotangent[...]).astype(stage.dtype).reshape(blocks, unit, width)
        copies += start([(stage, targets[j])], sem)
    return copies


def weight_copies(own, unit, expand, contract):
    found, at = [], 0
    for one in own:
        count = one.shape[0]
        found.append((one.at[:, pl.ds(0, unit)], expand.at[pl.ds(at, count)]))
        found.append((one.at[:, pl.ds(unit, unit)], contract.at[pl.ds(at, count)]))
        at += count
    return found


def first_kernel(lists, size, skip, me, gain, shifts, inputs_h, cotangent_h, low_h, *refs):
    readers, own, refs = refs[: len(lists)], refs[len(lists) : -24], refs[-24:]
    (residual_h, normed_h, branch_h, grad_h, sent, kept, shift_grad) = refs[:7]
    (inputs, cotangent, low, readout, expand, contract, residual, normed_two, branch, grad, hidden, slope) = refs[7:19]
    in_sem, weight_sem, out_sem, *stages = refs[19:]
    unit = expand.shape[1]
    width = gain.shape[1]
    arriving = start(
        [(inputs_h, inputs), (low_h, low)] + placed(me[0], lists, readers, skip, size, readout), in_sem
    )
    weights = start(weight_copies(own, unit, expand, contract) + [(cotangent_h, cotangent)], weight_sem)
    shift_grad[...] = jnp.zeros_like(shift_grad)
    finish(arriving)
    leaving = []
    for part in parts():
        value = inputs[part].astype(f32) + matmul(low[part], readout[...])
        residual[part] = value
        inverse = lax.rsqrt(jnp.mean(value * value, axis=-1, keepdims=True) + epsilon)
        normed_two[part] = (value * inverse * gain[...]).astype(bf16)
    leaving += start([(residual, residual_h), (normed_two, normed_h)], out_sem)
    finish(weights)
    expand = expand[...].reshape(-1, width)
    contract = contract[...].reshape(-1, width)
    for part in parts():
        branch[part], grad[part] = ffn_part(
            part, normed_two, cotangent, shifts, 0, expand, contract, hidden, slope, shift_grad
        )
        leaving += start([(branch.at[part], branch_h.at[part]), (grad.at[part], grad_h.at[part])], out_sem)
    leaving += ffn_grads(normed_two, cotangent, hidden, slope, stages, (kept, sent), out_sem)
    finish(leaving)


def second_kernel(plans, count, me, gain, shifts, residual_h, normed_h, branch_h, grad_h, cotangent_h, low_h, *refs):
    own, refs = refs[:count], refs[count:]
    output_h, back_h, rounded_h, gain_grad, sent, kept, shift_grad = refs[:7]
    targets, refs = refs[7:-20], refs[-20:]
    residual, normed_two, branch, grad, cotangent, low, expand, contract = refs[:8]
    output, back, rounded, hidden, slope, read_grad, in_sem, part_sem, low_sem, out_sem, *stages = refs[8:]
    unit = expand.shape[1]
    width = gain.shape[1]
    weights = start(
        [(normed_h, normed_two), (cotangent_h, cotangent)] + weight_copies(own, unit, expand, contract), in_sem
    )
    others = start([(residual_h, residual), (branch_h, branch), (grad_h, grad)], part_sem)
    last = start([(low_h, low)], low_sem)
    gain_grad[...] = jnp.zeros_like(gain_grad)
    shift_grad[...] = jnp.zeros_like(shift_grad)
    finish(weights)
    expand = expand[...].reshape(-1, width)
    contract = contract[...].reshape(-1, width)
    leaving = []
    for k, part in enumerate(parts()):
        one, two = ffn_part(
            part, normed_two, cotangent, shifts, hidden.shape[1], expand, contract, hidden, slope, shift_grad
        )
        if k == 0:
            finish(others)
        value = residual[part]
        output[part] = (value + (branch[part] + one)).astype(bf16)
        total = grad[part] + two
        inverse = lax.rsqrt(jnp.mean(value * value, axis=-1, keepdims=True) + epsilon)
        unscaled = value * inverse
        gain_grad[...] += jnp.sum(total * unscaled, axis=0, keepdims=True)
        pulled = total * gain[...]
        mean = jnp.mean(pulled * unscaled, axis=-1, keepdims=True)
        value = cotangent[part].astype(f32) + inverse * (pulled - unscaled * mean)
        back[part] = value
        rounded[part] = value.astype(bf16)
        leaving += start(
            [(o.at[part], h.at[part]) for o, h in ((output, output_h), (back, back_h), (rounded, rounded_h))], out_sem
        )
    leaving += ffn_grads(normed_two, cotangent, hidden, slope, stages, (kept, sent), out_sem)
    finish(last)
    read_grad[...] = across(low[...], rounded[...])
    emit(me[0], plans, read_grad, targets)
    finish(leaving)


def vmem(shape, dtype):
    return pltpu.VMEM(shape, dtype)


WHOLE = pl.BlockSpec(memory_space=pltpu.VMEM)


def ffn_first(me, gain, shifts, inputs, cotangent, low, readers, lists, size, skip, own, unit):
    blocks = sum(one.shape[0] for one in own)
    width = inputs.shape[1]
    units = blocks * unit
    kept = (max(1, blocks // 2), 2 * units // max(2, blocks), width)
    shape = jax.ShapeDtypeStruct
    return pl.pallas_call(
        partial(first_kernel, lists, size, skip),
        in_specs=[SCALAR, WHOLE, WHOLE] + [ANY] * (3 + len(readers) + len(own)),
        out_specs=[ANY] * 6 + [WHOLE],
        out_shape=[
            shape((LEN, width), f32),
            shape((LEN, width), bf16),
            shape((LEN, width), f32),
            shape((LEN, width), f32),
            shape(kept, bf16),
            shape(kept, f32),
            shape((1, units), f32),
        ],
        scratch_shapes=[
            vmem((LEN, width), bf16),
            vmem((LEN, width), bf16),
            vmem(low.shape, bf16),
            vmem((low.shape[1], width), bf16),
            vmem((blocks, unit, width), bf16),
            vmem((blocks, unit, width), bf16),
            vmem((LEN, width), f32),
            vmem((LEN, width), bf16),
            vmem((LEN, width), f32),
            vmem((LEN, width), f32),
            vmem((LEN, units), bf16),
            vmem((LEN, units), bf16),
        ]
        + [pltpu.SemaphoreType.DMA] * 3
        + [vmem(kept, f32), vmem(kept, bf16)],
        compiler_params=PARAMS,
        cost_estimate=FILLER,
        name="ffn_first",
    )(me, gain, shifts, inputs, cotangent, low, *readers, *own)


def ffn_second(me, gain, shifts, residual, normed_two, branch, grad, cotangent, low, own, unit, size, plans):
    blocks = sum(one.shape[0] for one in own)
    width = cotangent.shape[1]
    units = blocks * unit
    kept = (max(1, blocks // 2), 2 * units // max(2, blocks), width)
    targets = emitted(plans, low.shape[1], size, width)
    shape = jax.ShapeDtypeStruct
    return pl.pallas_call(
        partial(second_kernel, plans, len(own)),
        in_specs=[SCALAR, WHOLE, WHOLE] + [ANY] * (6 + len(own)),
        out_specs=[ANY] * 3 + [WHOLE, ANY, ANY] + [WHOLE] * (1 + len(targets)),
        out_shape=[
            shape((LEN, width), bf16),
            shape((LEN, width), f32),
            shape((LEN, width), bf16),
            shape((1, width), f32),
            shape(kept, bf16),
            shape(kept, f32),
            shape((1, units), f32),
        ]
        + targets,
        scratch_shapes=[
            vmem((LEN, width), f32),
            vmem((LEN, width), bf16),
            vmem((LEN, width), f32),
            vmem((LEN, width), f32),
            vmem((LEN, width), bf16),
            vmem(low.shape, bf16),
            vmem((blocks, unit, width), bf16),
            vmem((blocks, unit, width), bf16),
            vmem((LEN, width), bf16),
            vmem((LEN, width), f32),
            vmem((LEN, width), bf16),
            vmem((LEN, units), bf16),
            vmem((LEN, units), bf16),
            vmem((low.shape[1], width), f32),
        ]
        + [pltpu.SemaphoreType.DMA] * 4
        + [vmem(kept, f32), vmem(kept, bf16)],
        compiler_params=PARAMS,
        cost_estimate=FILLER,
        name="ffn_second",
    )(me, gain, shifts, residual, normed_two, branch, grad, cotangent, low, *own)


def back_kernel(lists, size, skip, plans, me, rounded, normed, share, pull_f, pull_i, *refs):
    readers = refs[: len(lists)]
    grads, offset_grad = refs[len(lists) : len(lists) + 2]
    targets = refs[len(lists) + 2 : -6]
    gate_grad, readout, pulled, drive, decay, sem = refs[-6:]
    group = pl.program_id(0)
    wide = share.shape[1]
    hidden = readout.shape[0]

    @pl.when(group == 0)
    def _():
        finish(start(placed(me[0], lists, readers, skip, size, readout), sem))

    reader = readout[pl.ds(pl.multiple_of(group * wide, wide), wide)]
    held = jnp.zeros((LANES, wide), f32)
    prod = jnp.ones((LANES, wide), f32)
    for part in reversed(parts()):
        pulled[part] = against(rounded[part], reader)
        for k in reversed(range(part.start // LANES, part.stop // LANES)):
            if k < STEPS - 1:
                after = 1.0 - share[tiles(k + 1, 1)]
                prod = after * prod
                held = pulled[tiles(k, 1)] + after * held
            else:
                held = pulled[tiles(k, 1)]
            drive[tiles(k, 1)] = held
            decay[tiles(k, 1)] = prod
    first_retain = 1.0 - share[pl.ds(0, LANES)]
    ends = [jnp.zeros((1, wide), f32)]
    for k in range(LANES - 1, 0, -1):
        whole = held[k : k + 1] + prod[k : k + 1] * ends[-1]
        ends.append(first_retain[k : k + 1] * whole)
    entering = jnp.concatenate(ends[::-1], axis=0)
    entering = jnp.concatenate([entering, entering], axis=0)

    def more(k, sums):
        rows = tiles(2 * k, 2)
        carried = drive[rows] + decay[rows] * entering
        found = []
        for t, factor in enumerate((pull_f, pull_i, share)):
            value = (carried * factor[rows].astype(f32)).astype(bf16)
            grads[t, rows] = value
            found.append(sums[t] + value.astype(f32))
        return tuple(found)

    sums = (jnp.zeros((2 * LANES, wide), f32),) * 3
    for k in range(STEPS // 2):
        sums = more(k, sums)
    for t in range(3):
        offset_grad[t : t + 1] = jnp.sum(sums[t], axis=0, keepdims=True)
        rows = pl.ds(pl.multiple_of(t * hidden + group * wide, wide), wide)
        gate_grad[rows] = across(grads[t], normed[...])

    @pl.when(group == hidden // wide - 1)
    def _():
        emit(me[0], plans, gate_grad, targets)


def back(me, rounded, normed, share, pull_f, pull_i, readers, lists, size, skip, plans):
    width = normed.shape[1]
    hidden = share.shape[1]
    wide = 256
    fixed = lambda g: (0, 0)
    tall = lambda g: (0, g)
    shape = jax.ShapeDtypeStruct
    firm = pl.BlockSpec((LEN, width), fixed)
    targets = emitted(plans, 3 * hidden, 3 * size, width)
    return pl.pallas_call(
        partial(back_kernel, lists, size, skip, plans),
        grid=(hidden // wide,),
        in_specs=[SCALAR, firm, firm] + [pl.BlockSpec((LEN, wide), tall)] * 3 + [ANY] * len(readers),
        out_specs=[pl.BlockSpec((3, LEN, wide), lambda g: (0, 0, g)), pl.BlockSpec((3, wide), tall)]
        + [pl.BlockSpec(one.shape, lambda g, rank=len(one.shape): (0,) * rank) for one in targets],
        out_shape=[shape((3, LEN, hidden), bf16), shape((3, hidden), f32)] + targets,
        scratch_shapes=[
            vmem((3 * hidden, width), f32),
            vmem((hidden, width), bf16),
            vmem((LEN, wide), f32),
            vmem((LEN, wide), f32),
            vmem((LEN, wide), f32),
            pltpu.SemaphoreType.DMA,
        ],
        compiler_params=PARAMS,
        cost_estimate=FILLER,
        name="back",
    )(me, rounded, normed, share, pull_f, pull_i, *readers)


def inputs_kernel(lists, size, me, inputs, gain, back, grads_h, *refs):
    arrays = refs[: len(lists)]
    output, gain_grad, grads, weights, weight_sem, sem = refs[len(lists) :]
    arriving = start(placed(me[0], lists, arrays, 0, size, weights), weight_sem)
    hidden = weights.shape[0] // 3
    for part in parts():
        arriving += start([(grads_h.at[t, part], grads.at[t, part]) for t in range(3)], sem)
    gain_grad[...] = jnp.zeros_like(gain_grad)
    finish(arriving)
    for part in parts():
        total = matmul(grads[0, part], weights[:hidden])
        for t in range(1, 3):
            total = total + matmul(grads[t, part], weights[t * hidden : (t + 1) * hidden])
        value = inputs[part].astype(f32)
        inverse = lax.rsqrt(jnp.mean(value * value, axis=-1, keepdims=True) + epsilon)
        unscaled = value * inverse
        gain_grad[...] += jnp.sum(total * unscaled, axis=0, keepdims=True)
        pulled = total * gain[...]
        mean = jnp.mean(pulled * unscaled, axis=-1, keepdims=True)
        output[part] = back[part] + inverse * (pulled - unscaled * mean)


def inputs_back(me, inputs, gain, back_grad, grads, arrays, lists, size):
    width = inputs.shape[1]
    hidden = grads.shape[2]
    return pl.pallas_call(
        partial(inputs_kernel, lists, size),
        in_specs=[SCALAR, WHOLE, WHOLE, WHOLE, ANY] + [ANY] * len(arrays),
        out_specs=[WHOLE, WHOLE],
        out_shape=[jax.ShapeDtypeStruct((LEN, width), f32), jax.ShapeDtypeStruct((1, width), f32)],
        scratch_shapes=[
            vmem((3, LEN, hidden), bf16),
            vmem((3 * hidden, width), bf16),
            pltpu.SemaphoreType.DMA,
            pltpu.SemaphoreType.DMA,
        ],
        compiler_params=PARAMS,
        cost_estimate=FILLER,
        name="inputs_back",
    )(me, inputs, gain, back_grad, grads, *arrays)


class Wires:
    def __init__(self, mesh):
        self.inner = mesh.shape["fsdp"]
        self.count = mesh.shape["dp"] * self.inner
        rest = [1 << b for b in range(1, self.inner.bit_length() - 1)]
        self.digits = [rest[i : i + 2] for i in range(0, len(rest), 2)]
        self.core, self.x, self.y = self.inner, 2 * self.inner, 1
        self.bits = {"A": [self.y, self.x, self.core], "B": [self.x, self.y, self.core]}

    def swap(self, value, mask):
        return lax.ppermute(value, AXES, [(i, i ^ mask) for i in range(self.count)])

    def spread(self, digit):
        return [sum(bit for j, bit in enumerate(digit) if k >> j & 1) for k in range(1 << len(digit))]

    def masks(self, order):
        found = [0]
        for digit in self.digits:
            found = [m ^ s for s in self.spread(digit) for m in found]
        lists = [found]
        for bit in self.bits[order]:
            lists = lists + [[m ^ bit for m in one] for one in lists]
        return lists

    def line(self, held, digits, tie=None):
        for digit in digits:
            came = [self.swap(held, m) for m in self.spread(digit)[1:]]
            if tie:
                _, *came = tie(*came)
            held = jnp.concatenate([held] + came)
        return held

    def line_start(self, held):
        for digit in reversed(self.digits[1:]):
            held = self.line_end(*self.line_step(held, digit))
        return self.line_step(held, self.digits[0])

    def line_step(self, held, digit):
        masks = self.spread(digit)
        blocks = jnp.split(held, len(masks))
        return blocks[0], [self.swap(one.astype(bf16), m) for one, m in zip(blocks[1:], masks[1:])]

    def line_end(self, held, came):
        for other in came:
            held = held + other.astype(f32)
        return held


def tied(*values):
    return lax.optimization_barrier(values)


def solution(mesh):
    wires = Wires(mesh)
    count = wires.count
    masks = {order: wires.masks(order) for order in "AB"}
    flat = {order: sum(masks[order], []) for order in "AB"}

    def shards(tokens, gating, offsets, prescale, readout, midscale, expand, shifts, contract, cotangent):
        swap = wires.swap
        index = lax.axis_index("dp") * wires.inner + lax.axis_index("fsdp")
        unit = readout.shape[0]
        wide = expand.shape[1]
        thin = prescale.shape[0]
        width = tokens.shape[1]
        hidden = count * unit
        assert tokens.shape[0] == LEN
        me = index.astype(jnp.int32).reshape(1)

        rest = jnp.concatenate([expand.T, contract])[None]
        row = jnp.concatenate([jnp.pad(one, (0, 128 - one.shape[0])) for one in (offsets, shifts, prescale, midscale)])
        taken = 4 * unit
        part = jnp.pad(jnp.concatenate([gating.T, readout, row[None]]), ((0, LANES - 1), (0, 0)))
        inputs = interleaved(tokens)
        gate_line = wires.line(part[None], wires.digits, lambda *came: tied(inputs, *came))
        gate_line, rest, cotangent = tied(gate_line, rest, cotangent)
        nz = gate_line.shape[0]
        cut = nz // 2
        gate_x = swap(gate_line, wires.x)
        gate_y = swap(gate_line, wires.y)
        rest_early = [swap(rest, m) for m in wires.spread(wires.digits[0])[1:]]
        upstream = interleaved(cotangent)
        gate_x, upstream, rest_early[1], rest_early[2] = tied(gate_x, upstream, rest_early[1], rest_early[2])
        gate_y, rest_early[0] = tied(gate_y, rest_early[0])
        gate_list = [gate_line, gate_x, gate_y, swap(gate_x[:cut], wires.y), swap(gate_y[cut:], wires.x)]
        gate_list += [swap(one, wires.core) for one in gate_list]
        rest_line = wires.line(jnp.concatenate([rest, *rest_early]), wires.digits[1:])
        rest_x = swap(rest_line, wires.x)
        rest_y = swap(rest_line, wires.y)
        rest_core = swap(rest_line, wires.core)

        quads = masks["A"]
        gate_lists = [quads[0], quads[2], quads[1], quads[3][:cut], quads[3][cut:]]
        gate_lists += [[m ^ wires.core for m in one] for one in gate_lists]
        row_arrays = gate_list
        sizes = (3 * unit, wide, thin)
        owner_masks = jnp.asarray(np.array(sum(gate_lists, []), np.int32)[:, None])
        ffn_masks = np.concatenate([masks["A"][k] for k in (0, 1, 4, 5, 2, 3, 6, 7)])
        lane_masks = jnp.asarray(np.repeat(ffn_masks, wide).astype(np.int32)[None])

        if unit % 16:
            places = np.argsort(np.asarray(sum(gate_lists, [])))
            whole = jnp.take(jnp.concatenate(gate_list), jnp.asarray(places)[index ^ jnp.arange(count)], axis=0)
            gate_list = [
                jnp.concatenate([whole[:, : 3 * unit].reshape(-1, width), whole[:, 3 * unit : taken].reshape(-1, width)])[None]
            ]
            row_arrays = [jnp.concatenate([one[:, taken : taken + LANES] for one in row_arrays])]
            gate_lists, gate_size, read_size, zero = [[0]], 3 * hidden, hidden, jnp.zeros_like(me)
            ffn_unit = 4 * nz * wide
        else:
            gate_size, read_size, zero = 3 * unit, unit, me
            ffn_unit = wide

        both = jnp.concatenate([zero, me])
        normed, share, low, pull_f, pull_i, gain_one, gain_two, all_shifts = gates(
            both, inputs, row_arrays, 0 if unit % 16 else taken, owner_masks, lane_masks, gate_list, gate_lists, gate_size, sizes, hidden
        )
        low, rest_y, rest_x, rest_core = tied(low, rest_y, rest_x, rest_core)
        rest_corner = [swap(rest_x, wires.y)]

        def merged(group):
            if not unit % 16:
                return group
            halves = [jnp.concatenate([one[:, at : at + wide].reshape(-1, width) for one in group]) for at in (0, wide)]
            return [jnp.concatenate(halves)[None]]

        own = merged([rest_line, rest_y, rest_core, swap(rest_y, wires.core)])

        def apart(grads):
            if not unit % 16:
                return grads
            return grads.reshape(2, -1, wide, width).transpose(1, 0, 2, 3).reshape(-1, 2 * wide, width)

        residual, normed_two, branch, grad, sent_0, kept_0, shift_0 = ffn_first(
            zero, gain_two, all_shifts, inputs, upstream, low, gate_list, gate_lists, read_size, gate_size, own,
            ffn_unit,
        )
        residual, normed_two, branch, grad, sent_0, kept_0, shift_0, rest_x, *rest_corner = tied(
            residual, normed_two, branch, grad, sent_0, kept_0, shift_0, rest_x, *rest_corner
        )
        far = [rest_x, *rest_corner]
        own = merged(far + [swap(one, wires.core) for one in far])
        near_core = swap(apart(sent_0), wires.core)
        half = count // 2
        read_plans = [(flat["A"][:half], f32), (flat["A"][half:], bf16)]
        output, residual_grad, rounded, midscale_grad, sent_1, kept_1, shift_1, *read_blocks = ffn_second(
            zero, gain_two, all_shifts, residual, normed_two, branch, grad, upstream, low, own, ffn_unit, unit,
            None if unit % 16 else read_plans,
        )
        read_kept, read_sent = sorted_blocks(index, read_plans, read_blocks, unit) if unit % 16 else read_blocks

        output, residual_grad, rounded, midscale_grad, sent_1, kept_1, shift_1, read_kept, read_sent, near_core = tied(
            output, residual_grad, rounded, midscale_grad, sent_1, kept_1, shift_1, read_kept, read_sent, near_core
        )
        far_core = swap(apart(sent_1), wires.core)
        read_core = swap(read_sent, wires.core)
        ffn_terms = [(apart(kept_0), near_core), (apart(kept_1), far_core)]

        def quad(k, low, high):
            kept, came = ffn_terms[k // 2]
            base = k % 2 * nz
            ffn = kept[base + low : base + high] + came[base + low : base + high].astype(f32)
            base = k * nz
            read = read_kept[base + low : base + high] + read_core[base + low : base + high].astype(f32)
            return jnp.concatenate([ffn, read], axis=1)

        send_x = jnp.concatenate([quad(3, cut, nz), quad(2, cut, nz)]).astype(bf16)
        send_y = jnp.concatenate([quad(3, 0, cut), quad(1, 0, cut)]).astype(bf16)
        rounded, send_x, send_y = tied(rounded, send_x, send_y)
        rest_x, rest_y = swap(send_x, wires.x), swap(send_y, wires.y)
        places = [quads[3][cut:] + quads[2][cut:] + quads[3][:cut] + quads[1][:cut]]
        places.append(quads[2][:cut] + quads[1][cut:] + quads[0])
        away = [[m ^ wires.core for m in one] for one in places]
        gate_plans = [(places[0], f32), (places[1], f32), (away[0], bf16), (away[1], bf16)]
        gate_grads, off_grad, *gate_blocks = back(
            zero, rounded, normed, share, pull_f, pull_i, gate_list, gate_lists, read_size, gate_size,
            None if unit % 16 else gate_plans,
        )
        if unit % 16:
            gate_blocks = sorted_blocks(index, gate_plans, gate_blocks, 3 * unit)
        first_kept, second_kept, first_sent, second_sent, gate_grads, off_grad, rest_x, rest_y = tied(
            *gate_blocks, gate_grads, off_grad, rest_x, rest_y
        )
        first_core = swap(first_sent, wires.core)
        second_core = swap(second_sent, wires.core)
        first = (first_kept + first_core.astype(f32)).astype(bf16)
        send_x = (quad(2, 0, cut) + rest_y[:cut].astype(f32)).astype(bf16)
        send_y = (quad(1, cut, nz) + rest_x[:cut].astype(f32)).astype(bf16)
        gate_grads, first, send_x, send_y, output, midscale_grad, off_grad, shift_0, shift_1 = tied(
            gate_grads, first, send_x, send_y, output, midscale_grad, off_grad, shift_0, shift_1
        )
        gate_x, gate_y = swap(first[:nz], wires.x), swap(first[nz:], wires.y)
        rest_xx, rest_yy = swap(send_x, wires.x), swap(send_y, wires.y)
        tokens_grad, prescale_grad = inputs_back(
            zero, inputs, gain_one, residual_grad, gate_grads, gate_list, gate_lists, gate_size
        )
        tokens_grad, prescale_grad, gate_x, gate_y, rest_xx, rest_yy = tied(
            tokens_grad, prescale_grad, gate_x, gate_y, rest_xx, rest_yy
        )

        def second(low, high):
            return second_kept[low:high] + second_core[low:high].astype(f32)

        send_x = (second(0, cut) + gate_y[:cut].astype(f32)).astype(bf16)
        send_y = (second(cut, nz) + gate_x[:cut].astype(f32)).astype(bf16)
        send_x, send_y, rest_xx, rest_yy = tied(send_x, send_y, rest_xx, rest_yy)
        gate_xx, gate_yy = swap(send_x, wires.x), swap(send_y, wires.y)

        def met(x_way, y_way, xx_way, yy_way):
            low_half = y_way[cut:].astype(f32) + xx_way.astype(f32)
            return jnp.concatenate([low_half, x_way[cut:].astype(f32) + yy_way.astype(f32)])

        rest_part = quad(0, 0, nz) + met(rest_x, rest_y, rest_xx, rest_yy)
        rest_part, output, prescale_grad = tied(rest_part, output, prescale_grad)
        rest_kept, rest_came = wires.line_start(rest_part)
        vectors = vector_rows(
            me, lane_masks, sizes, count, off_grad, shift_0, shift_1, prescale_grad, midscale_grad
        )
        gate_xx, gate_yy, vectors = tied(gate_xx, gate_yy, vectors)
        gate_part = second(nz, 2 * nz) + met(gate_x, gate_y, gate_xx, gate_yy)
        gate_part, tokens_grad, vectors, output = tied(gate_part, tokens_grad, vectors, output)
        gate_kept, gate_came = wires.line_start(gate_part)
        vectors = lax.all_to_all(vectors, AXES, 0, 0, tiled=True)
        tokens_grad = sequential(tokens_grad, FILLER)
        tokens_grad, output = tied(tokens_grad, output)
        block_output = sequential(output, QUICK)
        tokens_grad, block_output, vectors, gate_came, rest_came = tied(
            tokens_grad, block_output, vectors, gate_came, rest_came
        )
        vectors = jnp.sum(vectors, axis=0)
        vector_parts = [vectors[at : at + size] for at, size in zip(range(0, 512, 128), (*sizes, thin))]
        tokens_grad, vector_parts, block_output, rest_kept, rest_came, gate_kept, gate_came = tied(
            tokens_grad, vector_parts, block_output, rest_kept, rest_came, gate_kept, gate_came
        )
        rest_part = wires.line_end(rest_kept, rest_came)[0]
        gate_part = wires.line_end(gate_kept, gate_came)[0]
        offsets_part, shifts_part, prescale_part, midscale_part = vector_parts
        return (
            block_output,
            tokens_grad,
            gate_part.T,
            offsets_part,
            prescale_part,
            rest_part[2 * wide :],
            midscale_part,
            rest_part[:wide].T,
            shifts_part,
            rest_part[wide : 2 * wide],
        )

    rows = P(AXES, None)
    columns = P(None, AXES)
    line = P(AXES)
    in_specs = (rows, columns, line, line, rows, line, columns, line, rows, rows)
    out_specs = (rows, rows, columns, line, line, rows, line, columns, line, rows)
    return jax.shard_map(shards, mesh=mesh, in_specs=in_specs, out_specs=out_specs, check_vma=False)
```
